32 devices in a mesh: rows: 8 (over z, y), cols: 4 (over x, core).
Axes of the slice: x: 2, y: 2, z: 4, core: 2. Of those that a mesh axis runs over, the one named last changes fastest.
Arguments:
- h_start: float32 [4096, 128], P(('rows', 'cols')), may hold values from -6 to 6
- cotangent: float32 [4096, 128], P(('rows', 'cols')), may hold values from -6 to 6
- node_type: int32 [4096], P(('rows', 'cols')), may hold values from 0 to 7
- teleport: float32 [8], replicated, may hold values from 0.05 to 0.5
- tile_values: bfloat16 [8, 4, 24, 128, 128], P('rows', 'cols'), may hold values from -0.109375 to 0.109375
- tile_row: int32 [8, 4, 24], P('rows', 'cols'), may hold values from 0 to 3, as said below
- tile_col: int32 [8, 4, 24], P('rows', 'cols'), may hold values from 0 to 7
- tile_count: int32 [8, 4], P('rows', 'cols'), may hold values from 3 to 24, as said below
Outputs:
- propagated: float32 [4096, 128], P(('rows', 'cols'))
- input_grad: float32 [4096, 128], P(('rows', 'cols'))
The draws below stay inside these ranges and needn't reach their ends.
Inputs may be any that keep to these rules, and one draw needn't show every extreme that they name: Within one row block and column range, the pairs (tile_row, tile_col) of the 24 slots are all different. `tile_count`: slots at or beyond the count are not part of A. In every draw 1 row blocks use all 24 slots in every column range.
All inputs are finite; a program needn't handle non-finite values.
Results may differ from the reference program's by a relative error of at most 0.0029.
Values may be sent and summed in bfloat16 or wider, within the bound.
No kernel may reach another device: no remote copies, remote signals or barrier semaphores. Data moves between devices by JAX's collectives and lax.ppermute only.
A program may use at most 64 MiB of HBM per device.

```python
import math
import jax
import jax.numpy as jnp
from jax import lax

F = 128
TB = 128
TYPES = 8
TILES_DEV = 1
ROW_BLOCKS = 8
RANGES = 4
ROW_TILES = 4
COL_TILES = 8
SLOTS = 24
HUBS = 1
NODES = 4096


def pick_order(single):
    return jax.random.permutation(single, ROW_TILES * COL_TILES)


def tile_layout(key):
    layout_key = jax.random.fold_in(key, 101)
    device_keys = jax.random.split(layout_key, ROW_BLOCKS * RANGES)
    slot_order = jax.vmap(pick_order)(device_keys)[:, :SLOTS]
    slot_order = slot_order.reshape(ROW_BLOCKS, RANGES, SLOTS).astype(jnp.int32)
    return (slot_order // COL_TILES, slot_order % COL_TILES)


def draw_tile_row(key, part):
    return tile_layout(key)[0]


def draw_tile_col(key, part):
    return tile_layout(key)[1]


def draw_tile_count(key, part):
    hub_order = jax.random.permutation(jax.random.fold_in(key, 202), ROW_BLOCKS)
    is_hub = jnp.zeros((ROW_BLOCKS,), jnp.int32).at[hub_order[:HUBS]].set(1)
    light_count = jax.random.randint(jax.random.fold_in(key, 303), (ROW_BLOCKS, RANGES), SLOTS // 8, SLOTS // 2 + 1, dtype=jnp.int32)
    return jnp.where(is_hub[:, None] == 1, SLOTS, light_count).astype(jnp.int32)


def place_ends(array, stream_key, least, high):
    index_at = [jax.random.randint(jax.random.fold_in(stream_key, axis), (), 0, length) for axis, length in enumerate(array.shape)]
    widest = array.shape.index(max(array.shape))
    next_to = index_at[:widest] + [(index_at[widest] + 1) % array.shape[widest]] + index_at[widest + 1:]
    return array.at[tuple(index_at)].set(least).at[tuple(next_to)].set(high)


def steps_of(own_key, extent, cuts, least, largest):
    def one(position, parts):
        heights = jax.random.uniform(jax.random.fold_in(jax.random.fold_in(own_key, 6), position), (parts,), jnp.float32, least / len(cuts), largest / len(cuts))
        return jnp.repeat(jnp.exp(heights), extent[position] // parts).reshape((-1,) + (1,) * (len(extent) - position - 1))

    factor_of = one(*cuts[0])
    for cut in cuts[1:]:
        factor_of = factor_of * one(*cut)
    return factor_of


def noise(rng, shape, width, most, cuts=(), held_as=jnp.bfloat16):
    loudness = steps_of(rng, shape, cuts, -0.22, 0.18) if cuts else 1.0
    drawn = jax.random.normal(rng, shape, jnp.float32) * width * loudness
    return jnp.minimum(jnp.maximum(drawn, -most), most).astype(held_as)


def setup_inputs(seed: int = 0) -> dict:
    splits = jax.random.split(jax.random.key(seed), 9)
    h_start = noise(splits[0], (NODES, F), 1.0, 6.0, ((0, 32),), jnp.float32)
    cotangent = noise(splits[1], (NODES, F), 1.0, 6.0, ((0, 32),), jnp.float32)
    node_type = place_ends(jax.random.randint(splits[2], (NODES,), 0, TYPES), jax.random.fold_in(splits[2], 1), 0, TYPES - 1).astype(jnp.int32)
    teleport = jnp.clip(jnp.exp(jax.random.uniform(splits[3], (TYPES,), jnp.float32, math.log(0.05), math.log(0.5))), 0.05, 0.5)
    tile_values = noise(splits[4], (ROW_BLOCKS, RANGES, SLOTS, TB, TB), (SLOTS * TB // TILES_DEV) ** -0.5, 0.109375, ((0, 8), (1, 4)))
    tile_row = draw_tile_row(jax.random.fold_in(splits[8], 71), 0)
    tile_col = draw_tile_col(jax.random.fold_in(splits[8], 71), 0)
    tile_count = draw_tile_count(jax.random.fold_in(splits[8], 71), 0)
    return {"h_start": h_start, "cotangent": cotangent, "node_type": node_type, "teleport": teleport, "tile_values": tile_values, "tile_row": tile_row, "tile_col": tile_col, "tile_count": tile_count}


def column_tiles(col_index):
    range_ids = jnp.arange(RANGES, dtype=jnp.int32)[:, None]
    return (col_index // TILES_DEV * RANGES + range_ids) * TILES_DEV + col_index % TILES_DEV


def active_slots(tile_count, block_id):
    slot_ids = jnp.arange(SLOTS, dtype=jnp.int32)[None, :]
    return (slot_ids < tile_count[block_id][:, None]).astype(jnp.float32)


def forward_product(panel, tile_values, tile_row, tile_col, tile_count):
    panel_tiles = panel.reshape(NODES // TB, TB, F)

    def one_block(block_id):
        tile_block = tile_values[block_id].astype(jnp.float32)
        row_index = tile_row[block_id]
        col_index = tile_col[block_id]
        active = active_slots(tile_count, block_id)
        fetched = panel_tiles[column_tiles(col_index)].astype(jnp.float32)
        product = jnp.einsum("csij,csjf->csif", tile_block, fetched)
        row_onehot = (row_index[:, :, None] == jnp.arange(ROW_TILES, dtype=jnp.int32)[None, None, :]).astype(jnp.float32)
        row_onehot = row_onehot * active[:, :, None]
        return jnp.einsum("csq,csif->qif", row_onehot, product)

    result = lax.map(one_block, jnp.arange(ROW_BLOCKS, dtype=jnp.int32))
    return result.reshape(NODES, F)


def adjoint_product(adjoint, tile_values, tile_row, tile_col, tile_count):
    adjoint_tiles = adjoint.reshape(NODES // TB, TB, F)

    def advance(running, block_id):
        tile_block = tile_values[block_id].astype(jnp.float32)
        row_index = tile_row[block_id]
        col_index = tile_col[block_id]
        active = active_slots(tile_count, block_id)
        rows_block = lax.dynamic_slice_in_dim(adjoint_tiles, (block_id * ROW_TILES).astype(jnp.int32), ROW_TILES, 0)
        fetched = rows_block[row_index].astype(jnp.float32)
        product = jnp.einsum("csji,csjf->csif", tile_block, fetched) * active[:, :, None, None]
        targets = column_tiles(col_index).reshape(RANGES * SLOTS)
        running = running.at[targets].add(product.reshape(RANGES * SLOTS, TB, F))
        return running, None

    start = jnp.zeros((NODES // TB, TB, F), jnp.float32)
    running = lax.scan(advance, start, jnp.arange(ROW_BLOCKS, dtype=jnp.int32))[0]
    return running.reshape(NODES, F)


def reference(h_start, cotangent, node_type, teleport, tile_values, tile_row, tile_col, tile_count):
    teleport_rate = teleport[node_type][:, None]
    keep_rate = 1.0 - teleport_rate
    hop_one = keep_rate * forward_product(h_start.astype(jnp.bfloat16), tile_values, tile_row, tile_col, tile_count) + teleport_rate * h_start
    propagated = keep_rate * forward_product(hop_one.astype(jnp.bfloat16), tile_values, tile_row, tile_col, tile_count) + teleport_rate * h_start
    back_one = adjoint_product((keep_rate * cotangent).astype(jnp.bfloat16), tile_values, tile_row, tile_col, tile_count)
    back_two = adjoint_product((keep_rate * back_one).astype(jnp.bfloat16), tile_values, tile_row, tile_col, tile_count)
    input_grad = teleport_rate * cotangent + teleport_rate * back_one + back_two
    return propagated, input_grad
```

```python
import jax
import jax.numpy as jnp
from jax import lax
from jax.experimental import pallas as pl
from jax.experimental.pallas import tpu as pltpu
from jax.sharding import PartitionSpec as P

VMEM_LIMIT = 48 * 1024 * 1024
BF16 = jnp.bfloat16
F32 = jnp.float32


def vmem():
    return pl.BlockSpec(memory_space=pltpu.VMEM)


def smem():
    return pl.BlockSpec(memory_space=pltpu.SMEM)


def call(body, outs, in_specs, args, flops, name, scratch=()):
    nbytes = sum(a.size * a.dtype.itemsize for a in (*args, *outs))
    return pl.pallas_call(
        body,
        out_shape=outs,
        in_specs=in_specs,
        out_specs=[vmem()] * len(outs),
        scratch_shapes=list(scratch),
        compiler_params=pltpu.CompilerParams(vmem_limit_bytes=VMEM_LIMIT),
        cost_estimate=pl.CostEstimate(flops=flops, bytes_accessed=nbytes, transcendentals=0),
        name=name,
    )(*args)


def rate_row(types_ref, teleport_ref):
    types = types_ref[...]
    rate = jnp.zeros(types.shape, F32)
    for t in range(teleport_ref.shape[0]):
        rate = jnp.where(types == t, teleport_ref[t], rate)
    return rate


def rate_column(row, width):
    size = row.shape[1]
    return jnp.broadcast_to(row, (width, size)).T


def start_body(h_ref, cot_ref, types_ref, teleport_ref, p_ref, q_ref):
    rate = rate_row(types_ref, teleport_ref)
    p_ref[...] = h_ref[...].astype(BF16)
    q_ref[...] = ((1.0 - rate) * cot_ref[...].T).astype(BF16)


def dense_body(rows, cols, local_tiles, tiles_ref, row_ref, col_ref, count_ref, dense_ref):
    size = tiles_ref.shape[-1]
    me_row = lax.axis_index("rows")
    me_col = lax.axis_index("cols")
    dense_ref[...] = jnp.zeros_like(dense_ref)

    def place(slot, carry):
        row = row_ref[0, 0, slot] ^ me_col
        col = col_ref[0, 0, slot] ^ me_row
        dense_ref[
            pl.ds(pl.multiple_of(row * size, size), size),
            pl.ds(pl.multiple_of(col * size, size), size),
        ] = tiles_ref[0, 0, slot]
        return carry

    lax.fori_loop(0, count_ref[0, 0], place, 0)


def forward_body(n_rows, n_cols, dense_ref, *refs):
    panels, outs = refs[:n_rows], refs[n_rows:]
    size = panels[0].shape[0]
    total = None
    step = 2 if n_rows % 2 == 0 else 1
    for s in range(0, n_rows, step):
        panel = jnp.concatenate([panels[s + e][...] for e in range(step)], axis=0)
        part = jnp.dot(
            dense_ref[:, s * size : (s + step) * size], panel, preferred_element_type=F32
        )
        total = part if total is None else total + part
    for j in range(n_cols):
        outs[j][...] = total[j * size : (j + 1) * size].astype(outs[j].dtype)


def adjoint_body(n_rows, n_cols, dense_ref, *refs):
    blocks, outs = refs[:n_cols], refs[n_cols:]
    size = blocks[0].shape[1]
    left = jnp.concatenate([b[...] for b in blocks], axis=1)
    step = 2 if n_rows % 2 == 0 else 1
    for s in range(0, n_rows, step):
        part = jnp.dot(
            left, dense_ref[:, s * size : (s + step) * size], preferred_element_type=F32
        )
        for e in range(step):
            outs[s + e][...] = part[:, e * size : (e + 1) * size].astype(outs[s + e].dtype)


def sum_refs(refs):
    terms = [ref[...].astype(F32) for ref in refs]
    while len(terms) > 1:
        terms = [sum(terms[i : i + 2][1:], terms[i]) for i in range(0, len(terms), 2)]
    return terms[0]


def forward_end_body(h_ref, types_ref, teleport_ref, *refs):
    *parts, out_ref = refs
    rate = rate_column(rate_row(types_ref, teleport_ref), h_ref.shape[1])
    value = (1.0 - rate) * sum_refs(parts) + rate * h_ref[...]
    out_ref[...] = value.astype(out_ref.dtype)


def adjoint_mid_body(types_ref, teleport_ref, *refs):
    *parts, d_ref, q_ref = refs
    rate = rate_row(types_ref, teleport_ref)
    total = sum_refs(parts)
    d_ref[...] = total
    q_ref[...] = ((1.0 - rate) * total).astype(BF16)


def adjoint_end_body(cot_ref, d_ref, types_ref, teleport_ref, *refs):
    *parts, out_ref = refs
    rate = rate_row(types_ref, teleport_ref)
    column = rate_column(rate, cot_ref.shape[1])
    out_ref[...] = column * cot_ref[...] + (rate * d_ref[...] + sum_refs(parts)).T


def swap(values, axis, count):
    return [values[0]] + [
        lax.ppermute(values[s], axis, [(i, i ^ s) for i in range(count)]) for s in range(1, count)
    ]


def shards(h_start, cotangent, node_type, teleport, tile_values, tile_row, tile_col, tile_count):
    n_rows = lax.axis_size("rows")
    n_cols = lax.axis_size("cols")
    size = tile_values.shape[-1]
    features = h_start.shape[-1]
    types = node_type.reshape(1, size)
    hop_flops = 2 * n_rows * n_cols * size * size * features

    def shape(kind, rows=size, columns=features):
        return jax.ShapeDtypeStruct((rows, columns), kind)

    p0, q0 = call(
        start_body,
        [shape(BF16), shape(BF16, features, size)],
        [vmem(), vmem(), vmem(), smem()],
        (h_start, cotangent, types, teleport),
        0,
        "start",
    )
    (dense,) = call(
        lambda *refs: dense_body(n_rows, n_cols, 1, *refs),
        [shape(BF16, n_cols * size, n_rows * size)],
        [vmem(), smem(), smem(), smem()],
        (tile_values, tile_row, tile_col, tile_count),
        0,
        "dense",
    )

    def forward_hop(part, kind):
        panels = swap([part] * n_rows, "rows", n_rows)
        sums = call(
            lambda *refs: forward_body(n_rows, n_cols, *refs),
            [shape(kind)] * n_cols,
            [vmem()] * (1 + n_rows),
            (dense, *panels),
            hop_flops,
            "forward",
        )
        return swap(sums, "cols", n_cols)

    def adjoint_hop(part, kind):
        blocks = swap([part] * n_cols, "cols", n_cols)
        sums = call(
            lambda *refs: adjoint_body(n_rows, n_cols, *refs),
            [shape(kind, features, size)] * n_rows,
            [vmem()] * (1 + n_cols),
            (dense, *blocks),
            hop_flops,
            "adjoint",
        )
        return swap(sums, "rows", n_rows)

    def forward_end(parts, kind):
        return call(
            forward_end_body,
            [shape(kind)],
            [vmem(), vmem(), smem()] + [vmem()] * n_cols,
            (h_start, types, teleport, *parts),
            0,
            "forward_end",
        )[0]

    first = forward_hop(p0, F32)
    back = adjoint_hop(q0, F32)
    p1 = forward_end(first, BF16)
    d1, q1 = call(
        adjoint_mid_body,
        [shape(F32, features, size), shape(BF16, features, size)],
        [vmem(), smem()] + [vmem()] * n_rows,
        (types, teleport, *back),
        0,
        "adjoint_mid",
    )
    second = forward_hop(p1, F32)
    back_two = adjoint_hop(q1, F32)
    propagated = forward_end(second, F32)
    (input_grad,) = call(
        adjoint_end_body,
        [shape(F32)],
        [vmem(), vmem(), vmem(), smem()] + [vmem()] * n_rows,
        (cotangent, d1, types, teleport, *back_two),
        0,
        "adjoint_end",
    )
    return propagated, input_grad


def solution(mesh):
    placed = (
        P(("rows", "cols"), None),
        P(("rows", "cols"), None),
        P(("rows", "cols")),
        P(),
        P("rows", "cols", None, None, None),
        P("rows", "cols", None),
        P("rows", "cols", None),
        P("rows", "cols"),
    )
    return jax.shard_map(
        shards,
        mesh=mesh,
        in_specs=placed,
        out_specs=(P(("rows", "cols"), None), P(("rows", "cols"), None)),
        check_vma=False,
    )
```

```python
import jax
import jax.numpy as jnp
from jax import lax
from jax.experimental import pallas as pl
from jax.experimental.pallas import tpu as pltpu
from jax.sharding import PartitionSpec as P

VMEM_LIMIT = 32 * 1024 * 1024
BF16 = jnp.bfloat16
F32 = jnp.float32


def vmem():
    return pl.BlockSpec(memory_space=pltpu.VMEM)


def smem():
    return pl.BlockSpec(memory_space=pltpu.SMEM)


def call(body, outs, in_specs, args, flops, name):
    nbytes = sum(a.size * a.dtype.itemsize for a in (*args, *outs))
    return pl.pallas_call(
        body,
        out_shape=outs,
        in_specs=in_specs,
        out_specs=[vmem()] * len(outs),
        compiler_params=pltpu.CompilerParams(vmem_limit_bytes=VMEM_LIMIT),
        cost_estimate=pl.CostEstimate(flops=flops, bytes_accessed=nbytes, transcendentals=0),
        name=name,
    )(*args)


def rate_row(types_ref, teleport_ref):
    types = types_ref[...]
    rate = jnp.zeros(types.shape, F32)
    for t in range(teleport_ref.shape[0]):
        rate = jnp.where(types == t, teleport_ref[t], rate)
    return rate


def rate_column(row, width):
    size = row.shape[1]
    return jnp.broadcast_to(row, (width, size)).T


def split_store(out_ref, block, first, count, value):
    rest = value
    for part in range(count):
        high = rest.astype(BF16)
        out_ref[block, first + part] = high
        rest = rest - high.astype(F32)


def merged(in_ref, first, count):
    total = None
    for part in reversed(range(first, first + count)):
        for block in range(in_ref.shape[0]):
            term = in_ref[block, part].astype(F32)
            total = term if total is None else total + term
    return total


def start_body(cot_ref, types_ref, teleport_ref, q_ref):
    rate = rate_row(types_ref, teleport_ref)
    value = ((1.0 - rate) * cot_ref[...].T).astype(BF16)
    for block in range(q_ref.shape[0]):
        q_ref[block, 0] = value


def dense_body(tiles_ref, row_ref, col_ref, count_ref, dense_ref):
    size = tiles_ref.shape[-1]
    dense_ref[...] = jnp.zeros_like(dense_ref)

    def place(slot, carry):
        row = row_ref[0, 0, slot]
        col = col_ref[0, 0, slot]
        dense_ref[
            pl.ds(pl.multiple_of(row * size, size), size),
            pl.ds(pl.multiple_of(col * size, size), size),
        ] = tiles_ref[0, 0, slot]
        return carry

    lax.fori_loop(0, count_ref[0, 0], place, 0)


def adjoint_product(dense_ref, in_ref, part, out_ref, first, count):
    size = in_ref.shape[-1]
    n_rows, n_cols = out_ref.shape[0], in_ref.shape[0]
    left = jnp.concatenate([in_ref[j, part] for j in range(n_cols)], axis=1)
    step = 2 if n_rows % 2 == 0 else 1
    for s in range(0, n_rows, step):
        product = jnp.dot(
            left, dense_ref[:, s * size : (s + step) * size], preferred_element_type=F32
        )
        for e in range(step):
            split_store(out_ref, s + e, first, count, product[:, e * size : (e + 1) * size])


def forward_product(dense_ref, in_ref, part, out_ref, first, count):
    size = in_ref.shape[-1]
    n_rows, n_cols = in_ref.shape[0], out_ref.shape[0]
    total = None
    step = 2 if n_rows % 2 == 0 else 1
    for s in range(0, n_rows, step):
        panel = jnp.concatenate([in_ref[s + e, part] for e in range(step)], axis=0)
        term = jnp.dot(
            dense_ref[:, s * size : (s + step) * size], panel, preferred_element_type=F32
        )
        total = term if total is None else total + term
    for j in range(n_cols):
        split_store(out_ref, j, first, count, total[j * size : (j + 1) * size])


def first_body(dense_ref, q_ref, h_ref, out_ref):
    panel = h_ref[...].astype(BF16)
    for block in range(out_ref.shape[0]):
        out_ref[block, 0] = panel
    adjoint_product(dense_ref, q_ref, 0, out_ref, 1, 2)


def second_body(dense_ref, in_ref, types_ref, teleport_ref, out_ref, d_ref):
    rate = rate_row(types_ref, teleport_ref)
    total = merged(in_ref, 1, 2)
    d_ref[...] = total
    value = ((1.0 - rate) * total).astype(BF16)
    for block in range(out_ref.shape[0]):
        out_ref[block, 0] = value
    forward_product(dense_ref, in_ref, 0, out_ref, 1, 2)


def third_body(dense_ref, in_ref, h_ref, types_ref, teleport_ref, out_ref):
    rate = rate_column(rate_row(types_ref, teleport_ref), h_ref.shape[1])
    panel = ((1.0 - rate) * merged(in_ref, 1, 2) + rate * h_ref[...]).astype(BF16)
    for block in range(out_ref.shape[0]):
        out_ref[block, 0] = panel
    adjoint_product(dense_ref, in_ref, 0, out_ref, 1, 1)


def fourth_body(dense_ref, in_ref, cot_ref, d_ref, types_ref, teleport_ref, out_ref, grad_ref):
    forward_product(dense_ref, in_ref, 0, out_ref, 0, 1)
    rate = rate_row(types_ref, teleport_ref)
    column = rate_column(rate, cot_ref.shape[1])
    grad_ref[...] = column * cot_ref[...] + (rate * d_ref[...] + merged(in_ref, 1, 1)).T


def fifth_body(in_ref, h_ref, types_ref, teleport_ref, out_ref):
    rate = rate_column(rate_row(types_ref, teleport_ref), h_ref.shape[1])
    out_ref[...] = (1.0 - rate) * merged(in_ref, 0, 1) + rate * h_ref[...]


def exchange(blocks, axis):
    return lax.all_to_all(blocks, axis, split_axis=0, concat_axis=0, tiled=True)


def shards(h_start, cotangent, node_type, teleport, tile_values, tile_row, tile_col, tile_count):
    n_rows = lax.axis_size("rows")
    n_cols = lax.axis_size("cols")
    size = tile_values.shape[-1]
    features = h_start.shape[-1]
    types = node_type.reshape(1, size)
    hop_flops = 2 * n_rows * n_cols * size * size * features

    def blocks(count, parts):
        return jax.ShapeDtypeStruct((count, parts, size, features), BF16)

    def single():
        return jax.ShapeDtypeStruct((size, features), F32)

    (dense,) = call(
        dense_body,
        [jax.ShapeDtypeStruct((n_cols * size, n_rows * size), BF16)],
        [vmem(), smem(), smem(), smem()],
        (tile_values, tile_row, tile_col, tile_count),
        0,
        "dense",
    )
    (out,) = call(
        start_body,
        [blocks(n_cols, 1)],
        [vmem(), vmem(), smem()],
        (cotangent, types, teleport),
        0,
        "start",
    )
    got = exchange(out, "cols")
    (out,) = call(
        first_body, [blocks(n_rows, 3)], [vmem()] * 3, (dense, got, h_start), hop_flops, "first"
    )
    got = exchange(out, "rows")
    out, d1 = call(
        second_body,
        [blocks(n_cols, 3), single()],
        [vmem()] * 3 + [smem()],
        (dense, got, types, teleport),
        hop_flops,
        "second",
    )
    got = exchange(out, "cols")
    (out,) = call(
        third_body,
        [blocks(n_rows, 2)],
        [vmem()] * 4 + [smem()],
        (dense, got, h_start, types, teleport),
        hop_flops,
        "third",
    )
    got = exchange(out, "rows")
    out, input_grad = call(
        fourth_body,
        [blocks(n_cols, 1), single()],
        [vmem()] * 5 + [smem()],
        (dense, got, cotangent, d1, types, teleport),
        hop_flops,
        "fourth",
    )
    got = exchange(out, "cols")
    (propagated,) = call(
        fifth_body,
        [single()],
        [vmem()] * 3 + [smem()],
        (got, h_start, types, teleport),
        0,
        "fifth",
    )
    return propagated, input_grad


def solution(mesh):
    placed = (
        P(("rows", "cols"), None),
        P(("rows", "cols"), None),
        P(("rows", "cols")),
        P(),
        P("rows", "cols", None, None, None),
        P("rows", "cols", None),
        P("rows", "cols", None),
        P("rows", "cols"),
    )
    return jax.shard_map(
        shards,
        mesh=mesh,
        in_specs=placed,
        out_specs=(P(("rows", "cols"), None), P(("rows", "cols"), None)),
        check_vma=False,
    )
```

```python
import jax
import jax.numpy as jnp
from jax import lax
from jax.experimental import pallas as pl
from jax.experimental.pallas import tpu as pltpu
from jax.sharding import PartitionSpec as P

VMEM_LIMIT = 32 * 1024 * 1024
BF16 = jnp.bfloat16
F32 = jnp.float32


def vmem():
    return pl.BlockSpec(memory_space=pltpu.VMEM)


def smem():
    return pl.BlockSpec(memory_space=pltpu.SMEM)


def hbm():
    return pl.BlockSpec(memory_space=pltpu.HBM)


def call(body, outs, in_specs, args, flops, name, scratch=()):
    nbytes = sum(a.size * a.dtype.itemsize for a in (*args, *outs))
    return pl.pallas_call(
        body,
        out_shape=outs,
        in_specs=in_specs,
        out_specs=[vmem()] * len(outs),
        scratch_shapes=list(scratch),
        compiler_params=pltpu.CompilerParams(vmem_limit_bytes=VMEM_LIMIT),
        cost_estimate=pl.CostEstimate(flops=flops, bytes_accessed=nbytes, transcendentals=0),
        name=name,
    )(*args)


def fetch(pairs, sems):
    copies = [pltpu.make_async_copy(a, b, sems.at[i]) for i, (a, b) in enumerate(pairs)]
    for copy in copies:
        copy.start()
    for copy in copies:
        copy.wait()


def rate_row(types_ref, teleport_ref):
    types = types_ref[...]
    rate = jnp.zeros(types.shape, F32)
    for t in range(teleport_ref.shape[0]):
        rate = jnp.where(types == t, teleport_ref[t], rate)
    return rate


def rate_column(row, width):
    size = row.shape[1]
    return jnp.broadcast_to(row, (width, size)).T


def start_body(cot_hbm, types_hbm, teleport_hbm, q_ref, cot_ref, types_ref, teleport_ref, sems):
    fetch(
        [(cot_hbm, cot_ref), (types_hbm, types_ref), (teleport_hbm, teleport_ref)],
        sems,
    )
    rate = rate_row(types_ref, teleport_ref)
    q_ref[...] = ((1.0 - rate) * cot_ref[...].T).astype(BF16)


def dense_body(
    tiles_hbm, row_hbm, col_hbm, count_hbm, dense_ref, row_ref, col_ref, count_ref, sems, slot_sems
):
    size = tiles_hbm.shape[-1]
    me_row = lax.axis_index("rows")
    me_col = lax.axis_index("cols")
    dense_ref[...] = jnp.zeros_like(dense_ref)
    fetch([(row_hbm, row_ref), (col_hbm, col_ref), (count_hbm, count_ref)], sems)
    count = count_ref[0, 0]

    def copy(slot):
        row = row_ref[0, 0, slot] ^ me_col
        col = col_ref[0, 0, slot] ^ me_row
        return pltpu.make_async_copy(
            tiles_hbm.at[0, 0, slot],
            dense_ref.at[
                pl.ds(pl.multiple_of(row * size, size), size),
                pl.ds(pl.multiple_of(col * size, size), size),
            ],
            slot_sems.at[slot],
        )

    def begin(slot, carry):
        copy(slot).start()
        return carry

    def end(slot, carry):
        copy(slot).wait()
        return carry

    lax.fori_loop(0, count, begin, 0)
    lax.fori_loop(0, count, end, 0)


def adjoint_body(n_rows, n_cols, dense_ref, *refs):
    blocks, outs = refs[:n_cols], refs[n_cols:]
    send_far, send_near, keep_far, keep_near = outs
    half = n_rows // 2
    near = send_near.shape[0]
    size = blocks[0].shape[1]
    left = jnp.concatenate([b[...] for b in blocks], axis=1)
    for zz in reversed(range(half)):
        part = jnp.dot(
            left, dense_ref[:, 2 * zz * size : (2 * zz + 2) * size], preferred_element_type=F32
        )
        keep, send, at = (
            (keep_near, send_near, zz) if zz < near else (keep_far, send_far, zz - near)
        )
        keep[at] = part[:, :size]
        send[at] = part[:, size:].astype(send.dtype)


def add_body(keep_ref, got_ref, *outs):
    for at, out in enumerate(outs):
        out[...] = (keep_ref[at] + got_ref[at].astype(F32)).astype(out.dtype)


def pack_body(*refs):
    *parts, out_ref = refs
    for at, part in enumerate(parts):
        out_ref[at] = part[...]


def forward_body(half, n_cols, dense_ref, other_ref, *refs):
    panels, outs = refs[:half], refs[half:]
    size = panels[0].shape[0]
    total = None
    for zz in range(half):
        panel = jnp.concatenate([panels[zz][...], other_ref[zz]], axis=0)
        part = jnp.dot(
            dense_ref[:, 2 * zz * size : (2 * zz + 2) * size], panel, preferred_element_type=F32
        )
        total = part if total is None else total + part
    for j in range(n_cols):
        outs[j][...] = total[j * size : (j + 1) * size].astype(outs[j].dtype)


def sum_refs(refs):
    terms = [ref[...].astype(F32) for ref in refs]
    while len(terms) > 1:
        terms = [sum(terms[i : i + 2][1:], terms[i]) for i in range(0, len(terms), 2)]
    return terms[0]


def forward_end_body(h_ref, types_ref, teleport_ref, *refs):
    *parts, out_ref = refs
    rate = rate_column(rate_row(types_ref, teleport_ref), h_ref.shape[1])
    value = (1.0 - rate) * sum_refs(parts) + rate * h_ref[...]
    out_ref[...] = value.astype(out_ref.dtype)


def adjoint_mid_body(types_ref, teleport_ref, *refs):
    *parts, d_ref, q_ref = refs
    rate = rate_row(types_ref, teleport_ref)
    total = sum_refs(parts)
    d_ref[...] = total
    q_ref[...] = ((1.0 - rate) * total).astype(BF16)


def adjoint_end_body(cot_ref, d_ref, types_ref, teleport_ref, *refs):
    *parts, out_ref = refs
    rate = rate_row(types_ref, teleport_ref)
    column = rate_column(rate, cot_ref.shape[1])
    out_ref[...] = column * cot_ref[...] + (rate * d_ref[...] + sum_refs(parts)).T


def send(value, axis, count, step):
    return lax.ppermute(value, axis, [(i, i ^ step) for i in range(count)])


def shards(h_start, cotangent, node_type, teleport, tile_values, tile_row, tile_col, tile_count):
    n_rows = lax.axis_size("rows")
    n_cols = lax.axis_size("cols")
    half = n_rows // 2
    near = half // 2
    size = tile_values.shape[-1]
    slots = tile_values.shape[2]
    features = h_start.shape[-1]
    types = node_type.reshape(1, size)
    hop_flops = 2 * n_rows * n_cols * size * size * features

    def shape(kind, *lead):
        return jax.ShapeDtypeStruct((*lead, size, features), kind)

    (q0,) = call(
        start_body,
        [shape(BF16)],
        [hbm()] * 3,
        (cotangent, types, teleport),
        0,
        "start",
        [
            pltpu.VMEM(cotangent.shape, F32),
            pltpu.VMEM(types.shape, jnp.int32),
            pltpu.SMEM(teleport.shape, F32),
            pltpu.SemaphoreType.DMA((3,)),
        ],
    )
    (dense,) = call(
        dense_body,
        [jax.ShapeDtypeStruct((n_cols * size, n_rows * size), BF16)],
        [hbm()] * 4,
        (tile_values, tile_row, tile_col, tile_count),
        0,
        "dense",
        [
            pltpu.SMEM(tile_row.shape, jnp.int32),
            pltpu.SMEM(tile_col.shape, jnp.int32),
            pltpu.SMEM(tile_count.shape, jnp.int32),
            pltpu.SemaphoreType.DMA((3,)),
            pltpu.SemaphoreType.DMA((slots,)),
        ],
    )
    p0 = h_start.astype(BF16)

    def add(keep, got, kinds, name):
        return call(add_body, [shape(kind) for kind in kinds], [vmem()] * 2, (keep, got), 0, name)

    def adjoint_hop(part, kind):
        blocks = [part] + [send(part, "cols", n_cols, s) for s in range(1, n_cols)]
        send_far, send_near, keep_far, keep_near = call(
            lambda *refs: adjoint_body(n_rows, n_cols, *refs),
            [shape(kind, half - near), shape(kind, near), shape(F32, half - near), shape(F32, near)],
            [vmem()] * (1 + n_cols),
            [dense, *blocks],
            hop_flops,
            "adjoint",
        )
        far = add(keep_far, send(send_far, "rows", n_rows, 1), [kind] * (half - near), "add_far")
        far = [send(far[s - near], "rows", n_rows, 2 * s) for s in range(near, half)]
        kinds = [F32] + [kind] * (near - 1)
        close = add(keep_near, send(send_near, "rows", n_rows, 1), kinds, "add_near")
        close = [close[0]] + [send(close[s], "rows", n_rows, 2 * s) for s in range(1, near)]
        return close + far

    def forward_hop(part, kind):
        panels = [part] + [send(part, "rows", n_rows, 2 * s) for s in range(1, half)]
        (packed,) = call(
            pack_body, [shape(BF16, half)], [vmem()] * half, panels, 0, "pack"
        )
        other = send(packed, "rows", n_rows, 1)
        sums = call(
            lambda *refs: forward_body(half, n_cols, *refs),
            [shape(kind)] * n_cols,
            [vmem()] * (2 + half),
            (dense, other, *panels),
            hop_flops,
            "forward",
        )
        return [sums[0]] + [send(sums[s], "cols", n_cols, s) for s in range(1, n_cols)]

    def forward_end(parts, kind):
        return call(
            forward_end_body,
            [shape(kind)],
            [vmem(), vmem(), smem()] + [vmem()] * n_cols,
            (h_start, types, teleport, *parts),
            0,
            "forward_end",
        )[0]

    back = adjoint_hop(q0, F32)
    first = forward_hop(p0, F32)
    d1, q1 = call(
        adjoint_mid_body,
        [shape(F32), shape(BF16)],
        [vmem(), smem()] + [vmem()] * half,
        (types, teleport, *back),
        0,
        "adjoint_mid",
    )
    p1 = forward_end(first, BF16)
    back_two = adjoint_hop(q1, BF16)
    second = forward_hop(p1, BF16)
    propagated = forward_end(second, F32)
    (input_grad,) = call(
        adjoint_end_body,
        [shape(F32)],
        [vmem(), vmem(), vmem(), smem()] + [vmem()] * half,
        (cotangent, d1, types, teleport, *back_two),
        0,
        "adjoint_end",
    )
    return propagated, input_grad


def solution(mesh):
    placed = (
        P(("rows", "cols"), None),
        P(("rows", "cols"), None),
        P(("rows", "cols")),
        P(),
        P("rows", "cols", None, None, None),
        P("rows", "cols", None),
        P("rows", "cols", None),
        P("rows", "cols"),
    )
    return jax.shard_map(
        shards,
        mesh=mesh,
        in_specs=placed,
        out_specs=(P(("rows", "cols"), None), P(("rows", "cols"), None)),
        check_vma=False,
    )
```

```python
import jax
import jax.numpy as jnp
from jax import lax
from jax.experimental import pallas as pl
from jax.experimental.pallas import tpu as pltpu
from jax.sharding import PartitionSpec as P

VMEM_LIMIT = 32 * 1024 * 1024
BF16 = jnp.bfloat16
F32 = jnp.float32


def vmem():
    return pl.BlockSpec(memory_space=pltpu.VMEM)


def smem():
    return pl.BlockSpec(memory_space=pltpu.SMEM)


def hbm():
    return pl.BlockSpec(memory_space=pltpu.HBM)


def in_hbm(*arrays):
    return [pltpu.with_memory_space_constraint(a, pltpu.HBM) for a in arrays]


def call(body, outs, in_specs, args, flops, name, scratch=()):
    nbytes = sum(a.size * a.dtype.itemsize for a in (*args, *outs))
    return pl.pallas_call(
        body,
        out_shape=outs,
        in_specs=in_specs,
        out_specs=[vmem()] * len(outs),
        scratch_shapes=list(scratch),
        compiler_params=pltpu.CompilerParams(vmem_limit_bytes=VMEM_LIMIT),
        cost_estimate=pl.CostEstimate(flops=flops, bytes_accessed=nbytes, transcendentals=0),
        name=name,
    )(*args)


def fetch(pairs, sems):
    copies = [pltpu.make_async_copy(a, b, sems.at[i]) for i, (a, b) in enumerate(pairs)]
    for copy in copies:
        copy.start()
    for copy in copies:
        copy.wait()


def rate_row(types_ref, teleport_ref):
    types = types_ref[...]
    rate = jnp.zeros(types.shape, F32)
    for t in range(teleport_ref.shape[0]):
        rate = jnp.where(types == t, teleport_ref[t], rate)
    return rate


def rate_column(row, width):
    size = row.shape[1]
    return jnp.broadcast_to(row, (width, size)).T


def start_body(
    cot_hbm,
    h_hbm,
    types_hbm,
    teleport_hbm,
    q_ref,
    p_ref,
    row_ref,
    column_ref,
    cot_ref,
    h_ref,
    types_ref,
    teleport_ref,
    sems,
):
    fetch(
        [
            (types_hbm, types_ref),
            (teleport_hbm, teleport_ref),
            (cot_hbm, cot_ref),
            (h_hbm, h_ref),
        ],
        sems,
    )
    rate = rate_row(types_ref, teleport_ref)
    row_ref[...] = rate
    column_ref[...] = rate_column(rate, h_ref.shape[1])
    q_ref[...] = ((1.0 - rate) * cot_ref[...].T).astype(BF16)
    p_ref[...] = h_ref[...].astype(BF16)


def dense_body(
    q_ref,
    tiles_hbm,
    row_hbm,
    col_hbm,
    count_ref,
    dense_ref,
    row_ref,
    col_ref,
    sems,
    slot_sems,
):
    size = tiles_hbm.shape[-1]
    me_row = lax.axis_index("rows")
    me_col = lax.axis_index("cols")
    dense_ref[...] = jnp.zeros_like(dense_ref)
    fetch([(row_hbm, row_ref), (col_hbm, col_ref)], sems)
    count = count_ref[0, 0]

    def copy(slot):
        row = row_ref[0, 0, slot] ^ me_col
        col = col_ref[0, 0, slot] ^ me_row
        return pltpu.make_async_copy(
            tiles_hbm.at[0, 0, slot],
            dense_ref.at[
                pl.ds(pl.multiple_of(row * size, size), size),
                pl.ds(pl.multiple_of(col * size, size), size),
            ],
            slot_sems.at[slot],
        )

    def begin(slot, carry):
        copy(slot).start()
        return carry

    def end(slot, carry):
        copy(slot).wait()
        return carry

    lax.fori_loop(0, count, begin, 0)
    lax.fori_loop(0, count, end, 0)


def adjoint_body(n_rows, n_cols, dense_ref, *refs):
    blocks, refs = refs[:n_cols], refs[n_cols:]
    *pair, send_far, send_near, keep_far, keep_near = refs
    half = n_rows // 2
    near = send_near.shape[0]
    size = blocks[0].shape[1]
    left = jnp.concatenate([b[...] for b in blocks], axis=1)
    for zz in reversed(range(half)):
        part = jnp.dot(
            left, dense_ref[:, 2 * zz * size : (2 * zz + 2) * size], preferred_element_type=F32
        )
        keep, send, at = (
            (keep_near, send_near, zz) if zz < near else (keep_far, send_far, zz - near)
        )
        keep[at] = part[:, :size]
        send[at] = part[:, size:].astype(send.dtype)
    if pair:
        own, other, both = pair
        both[0] = own[...]
        both[1] = other[...]


def add_body(keep_ref, got_ref, *outs):
    for at, out in enumerate(outs):
        out[...] = (keep_ref[at] + got_ref[at].astype(F32)).astype(out.dtype)


def pack_body(*refs):
    *parts, out_ref = refs
    for at, part in enumerate(parts):
        out_ref[at] = part[...]


def forward_body(half, n_cols, paired, dense_ref, *refs):
    count = half if paired else half + 1
    panels, outs = refs[:count], refs[count:]
    size = panels[0].shape[-1]
    total = None
    for zz in range(half):
        if paired:
            panel = jnp.concatenate([panels[zz][0], panels[zz][1]], axis=0)
        else:
            panel = jnp.concatenate([panels[zz][...], panels[half][zz]], axis=0)
        part = jnp.dot(
            dense_ref[:, 2 * zz * size : (2 * zz + 2) * size], panel, preferred_element_type=F32
        )
        total = part if total is None else total + part
    for j in range(n_cols):
        outs[j][...] = total[j * size : (j + 1) * size].astype(outs[j].dtype)


def sum_refs(refs):
    terms = [ref[...].astype(F32) for ref in refs]
    while len(terms) > 1:
        terms = [sum(terms[i : i + 2][1:], terms[i]) for i in range(0, len(terms), 2)]
    return terms[0]


def forward_end_body(h_ref, rate_ref, *refs):
    *parts, out_ref = refs
    rate = rate_ref[...]
    value = (1.0 - rate) * sum_refs(parts) + rate * h_ref[...]
    out_ref[...] = value.astype(out_ref.dtype)


def adjoint_mid_body(rate_ref, *refs):
    *parts, d_ref, q_ref = refs
    total = sum_refs(parts)
    d_ref[...] = total
    q_ref[...] = ((1.0 - rate_ref[...]) * total).astype(BF16)


def adjoint_end_body(cot_ref, d_ref, row_ref, column_ref, *refs):
    *parts, out_ref = refs
    change = (row_ref[...] * d_ref[...] + sum_refs(parts)).T
    out_ref[...] = column_ref[...] * cot_ref[...] + change


def send(value, axis, count, step):
    return lax.ppermute(value, axis, [(i, i ^ step) for i in range(count)])


def shards(h_start, cotangent, node_type, teleport, tile_values, tile_row, tile_col, tile_count):
    n_rows = lax.axis_size("rows")
    n_cols = lax.axis_size("cols")
    half = n_rows // 2
    near = half // 2
    size = tile_values.shape[-1]
    slots = tile_values.shape[2]
    features = h_start.shape[-1]
    types = node_type.reshape(1, size)
    hop_flops = 2 * n_rows * n_cols * size * size * features

    def shape(kind, *lead):
        return jax.ShapeDtypeStruct((*lead, size, features), kind)

    q0, p0, rate, column = call(
        start_body,
        [shape(BF16), shape(BF16), jax.ShapeDtypeStruct((1, size), F32), shape(F32)],
        [hbm()] * 4,
        in_hbm(cotangent, h_start, types, teleport),
        0,
        "start",
        [
            pltpu.VMEM(cotangent.shape, F32),
            pltpu.VMEM(h_start.shape, F32),
            pltpu.VMEM(types.shape, jnp.int32),
            pltpu.SMEM(teleport.shape, F32),
            pltpu.SemaphoreType.DMA((4,)),
        ],
    )
    (dense,) = call(
        dense_body,
        [jax.ShapeDtypeStruct((n_cols * size, n_rows * size), BF16)],
        [vmem()] + [hbm()] * 3 + [smem()],
        [q0, *in_hbm(tile_values, tile_row, tile_col), tile_count],
        0,
        "dense",
        [
            pltpu.SMEM(tile_row.shape, jnp.int32),
            pltpu.SMEM(tile_col.shape, jnp.int32),
            pltpu.SemaphoreType.DMA((2,)),
            pltpu.SemaphoreType.DMA((slots,)),
        ],
    )

    def add(keep, got, kinds, name):
        return call(add_body, [shape(kind) for kind in kinds], [vmem()] * 2, (keep, got), 0, name)

    def adjoint_hop(part, kind, pair):
        blocks = [part] + [send(part, "cols", n_cols, s) for s in range(1, n_cols)]
        *both, send_far, send_near, keep_far, keep_near = call(
            lambda *refs: adjoint_body(n_rows, n_cols, *refs),
            [shape(BF16, 2)] * (len(pair) // 2)
            + [shape(kind, half - near), shape(kind, near)]
            + [shape(F32, half - near), shape(F32, near)],
            [vmem()] * (1 + n_cols + len(pair)),
            [dense, *blocks, *pair],
            hop_flops,
            "adjoint",
        )
        far = add(keep_far, send(send_far, "rows", n_rows, 1), [kind] * (half - near), "add_far")
        far = [send(far[s - near], "rows", n_rows, 2 * s) for s in range(near, half)]
        kinds = [F32] + [kind] * (near - 1)
        close = add(keep_near, send(send_near, "rows", n_rows, 1), kinds, "add_near")
        close = [close[0]] + [send(close[s], "rows", n_rows, 2 * s) for s in range(1, near)]
        return close + far, both

    def forward_hop(part, kind, paired):
        panels = [part] + [send(part, "rows", n_rows, 2 * s) for s in range(1, half)]
        if not paired:
            (packed,) = call(
                pack_body, [shape(BF16, half)], [vmem()] * half, panels, 0, "pack"
            )
            panels = panels + [send(packed, "rows", n_rows, 1)]
        sums = call(
            lambda *refs: forward_body(half, n_cols, paired, *refs),
            [shape(kind)] * n_cols,
            [vmem()] * (1 + len(panels)),
            [dense, *panels],
            hop_flops,
            "forward",
        )
        return [sums[0]] + [send(sums[s], "cols", n_cols, s) for s in range(1, n_cols)]

    def forward_end(parts, kind):
        return call(
            forward_end_body,
            [shape(kind)],
            [vmem()] * (2 + n_cols),
            (h_start, column, *parts),
            0,
            "forward_end",
        )[0]

    back, (both,) = adjoint_hop(q0, F32, [p0, send(p0, "rows", n_rows, 1)])
    first = forward_hop(both, F32, True)
    d1, q1 = call(
        adjoint_mid_body,
        [shape(F32), shape(BF16)],
        [vmem()] * (1 + half),
        (rate, *back),
        0,
        "adjoint_mid",
    )
    p1 = forward_end(first, BF16)
    back_two, _ = adjoint_hop(q1, BF16, [])
    second = forward_hop(p1, BF16, False)
    propagated = forward_end(second, F32)
    (input_grad,) = call(
        adjoint_end_body,
        [shape(F32)],
        [vmem()] * (4 + half),
        (cotangent, d1, rate, column, *back_two),
        0,
        "adjoint_end",
    )
    return propagated, input_grad


def solution(mesh):
    placed = (
        P(("rows", "cols"), None),
        P(("rows", "cols"), None),
        P(("rows", "cols")),
        P(),
        P("rows", "cols", None, None, None),
        P("rows", "cols", None),
        P("rows", "cols", None),
        P("rows", "cols"),
    )
    return jax.shard_map(
        shards,
        mesh=mesh,
        in_specs=placed,
        out_specs=(P(("rows", "cols"), None), P(("rows", "cols"), None)),
        check_vma=False,
    )
```

```python
import jax
import jax.numpy as jnp
from jax import lax
from jax.experimental import pallas as pl
from jax.experimental.pallas import tpu as pltpu
from jax.sharding import PartitionSpec as P

VMEM_LIMIT = 32 * 1024 * 1024
BF16 = jnp.bfloat16
F32 = jnp.float32


def vmem():
    return pl.BlockSpec(memory_space=pltpu.VMEM)


def smem():
    return pl.BlockSpec(memory_space=pltpu.SMEM)


def hbm():
    return pl.BlockSpec(memory_space=pltpu.HBM)


def in_hbm(*arrays):
    return [pltpu.with_memory_space_constraint(a, pltpu.HBM) for a in arrays]


def call(body, outs, in_specs, args, flops, name, scratch=(), after=()):
    nbytes = sum(a.size * a.dtype.itemsize for a in (*args, *outs))
    count = len(args)

    def ordered(*refs):
        body(*refs[:count], *refs[count + len(after) :])

    return pl.pallas_call(
        ordered,
        out_shape=outs,
        in_specs=[*in_specs, *[pl.BlockSpec(memory_space=pl.ANY)] * len(after)],
        out_specs=[vmem()] * len(outs),
        scratch_shapes=list(scratch),
        compiler_params=pltpu.CompilerParams(vmem_limit_bytes=VMEM_LIMIT),
        cost_estimate=pl.CostEstimate(flops=flops, bytes_accessed=nbytes, transcendentals=0),
        name=name,
    )(*args, *after)


def fetch(pairs, sems):
    copies = [pltpu.make_async_copy(a, b, sems.at[i]) for i, (a, b) in enumerate(pairs)]
    for copy in copies:
        copy.start()
    for copy in copies:
        copy.wait()


def rate_row(types_ref, teleport_ref):
    types = types_ref[...]
    rate = jnp.zeros(types.shape, F32)
    for t in range(teleport_ref.shape[0]):
        rate = jnp.where(types == t, teleport_ref[t], rate)
    return rate


def rate_column(row, width):
    size = row.shape[1]
    return jnp.broadcast_to(row, (width, size)).T


def start_body(
    cot_hbm,
    h_hbm,
    types_hbm,
    teleport_hbm,
    q_ref,
    p_ref,
    row_ref,
    column_ref,
    cot_ref,
    h_ref,
    types_ref,
    teleport_ref,
    sems,
):
    fetch(
        [
            (types_hbm, types_ref),
            (teleport_hbm, teleport_ref),
            (cot_hbm, cot_ref),
            (h_hbm, h_ref),
        ],
        sems,
    )
    rate = rate_row(types_ref, teleport_ref)
    row_ref[...] = rate
    column_ref[...] = rate_column(rate, h_ref.shape[1])
    q_ref[...] = ((1.0 - rate) * cot_ref[...].T).astype(BF16)
    p_ref[...] = h_ref[...].astype(BF16)


def dense_body(
    q_ref,
    tiles_hbm,
    row_hbm,
    col_hbm,
    count_ref,
    dense_ref,
    row_ref,
    col_ref,
    sems,
    slot_sems,
):
    size = tiles_hbm.shape[-1]
    me_row = lax.axis_index("rows")
    me_col = lax.axis_index("cols")
    dense_ref[...] = jnp.zeros_like(dense_ref)
    fetch([(row_hbm, row_ref), (col_hbm, col_ref)], sems)
    count = count_ref[0, 0]

    def copy(slot):
        row = row_ref[0, 0, slot] ^ me_col
        col = col_ref[0, 0, slot] ^ me_row
        return pltpu.make_async_copy(
            tiles_hbm.at[0, 0, slot],
            dense_ref.at[
                pl.ds(pl.multiple_of(row * size, size), size),
                pl.ds(pl.multiple_of(col * size, size), size),
            ],
            slot_sems.at[slot],
        )

    def begin(slot, carry):
        copy(slot).start()
        return carry

    def end(slot, carry):
        copy(slot).wait()
        return carry

    lax.fori_loop(0, count, begin, 0)
    lax.fori_loop(0, count, end, 0)


def adjoint_body(n_rows, n_cols, dense_ref, *refs):
    blocks, refs = refs[:n_cols], refs[n_cols:]
    *pair, send_far, send_near, keep_far, keep_near = refs
    half = n_rows // 2
    near = send_near.shape[0]
    size = blocks[0].shape[1]
    left = jnp.concatenate([b[...] for b in blocks], axis=1)
    for zz in reversed(range(half)):
        part = jnp.dot(
            left, dense_ref[:, 2 * zz * size : (2 * zz + 2) * size], preferred_element_type=F32
        )
        keep, send, at = (
            (keep_near, send_near, zz) if zz < near else (keep_far, send_far, zz - near)
        )
        keep[at] = part[:, :size]
        send[at] = part[:, size:].astype(send.dtype)
    if pair:
        own, other, both = pair
        both[0] = own[...]
        both[1] = other[...]


def add_body(keep_ref, got_ref, *outs):
    for at, out in enumerate(outs):
        out[...] = (keep_ref[at] + got_ref[at].astype(F32)).astype(out.dtype)


def pack_body(*refs):
    *parts, out_ref = refs
    for at, part in enumerate(parts):
        out_ref[at] = part[...]


def forward_body(half, n_cols, paired, dense_ref, *refs):
    count = half if paired else half + 1
    panels, outs = refs[:count], refs[count:]
    size = panels[0].shape[-1]
    total = None
    for zz in range(half):
        if paired:
            panel = jnp.concatenate([panels[zz][0], panels[zz][1]], axis=0)
        else:
            panel = jnp.concatenate([panels[zz][...], panels[half][zz]], axis=0)
        part = jnp.dot(
            dense_ref[:, 2 * zz * size : (2 * zz + 2) * size], panel, preferred_element_type=F32
        )
        total = part if total is None else total + part
    for j in range(n_cols):
        outs[j][...] = total[j * size : (j + 1) * size].astype(outs[j].dtype)


def sum_refs(refs):
    terms = [ref[...].astype(F32) for ref in refs]
    while len(terms) > 1:
        terms = [sum(terms[i : i + 2][1:], terms[i]) for i in range(0, len(terms), 2)]
    return terms[0]


def forward_end_body(h_ref, rate_ref, *refs):
    *parts, out_ref = refs
    rate = rate_ref[...]
    value = (1.0 - rate) * sum_refs(parts) + rate * h_ref[...]
    out_ref[...] = value.astype(out_ref.dtype)


def adjoint_mid_body(rate_ref, *refs):
    *parts, d_ref, q_ref = refs
    total = sum_refs(parts)
    d_ref[...] = total
    q_ref[...] = ((1.0 - rate_ref[...]) * total).astype(BF16)


def adjoint_end_body(cot_ref, d_ref, row_ref, column_ref, *refs):
    *parts, out_ref = refs
    change = (row_ref[...] * d_ref[...] + sum_refs(parts)).T
    out_ref[...] = column_ref[...] * cot_ref[...] + change


def send(value, axis, count, step):
    return lax.ppermute(value, axis, [(i, i ^ step) for i in range(count)])


def shards(h_start, cotangent, node_type, teleport, tile_values, tile_row, tile_col, tile_count):
    n_rows = lax.axis_size("rows")
    n_cols = lax.axis_size("cols")
    half = n_rows // 2
    near = half // 2
    size = tile_values.shape[-1]
    slots = tile_values.shape[2]
    features = h_start.shape[-1]
    types = node_type.reshape(1, size)
    hop_flops = 2 * n_rows * n_cols * size * size * features

    def shape(kind, *lead):
        return jax.ShapeDtypeStruct((*lead, size, features), kind)

    q0, p0, rate, column = call(
        start_body,
        [shape(BF16), shape(BF16), jax.ShapeDtypeStruct((1, size), F32), shape(F32)],
        [hbm()] * 4,
        in_hbm(cotangent, h_start, types, teleport),
        0,
        "start",
        [
            pltpu.VMEM(cotangent.shape, F32),
            pltpu.VMEM(h_start.shape, F32),
            pltpu.VMEM(types.shape, jnp.int32),
            pltpu.SMEM(teleport.shape, F32),
            pltpu.SemaphoreType.DMA((4,)),
        ],
    )
    (dense,) = call(
        dense_body,
        [jax.ShapeDtypeStruct((n_cols * size, n_rows * size), BF16)],
        [vmem()] + [hbm()] * 3 + [smem()],
        [q0, *in_hbm(tile_values, tile_row, tile_col), tile_count],
        0,
        "dense",
        [
            pltpu.SMEM(tile_row.shape, jnp.int32),
            pltpu.SMEM(tile_col.shape, jnp.int32),
            pltpu.SemaphoreType.DMA((2,)),
            pltpu.SemaphoreType.DMA((slots,)),
        ],
    )

    def add(keep, got, kinds, name):
        return call(add_body, [shape(kind) for kind in kinds], [vmem()] * 2, (keep, got), 0, name)

    def adjoint_hop(part, kind, pair):
        blocks = [part] + [send(part, "cols", n_cols, s) for s in range(1, n_cols)]
        *both, send_far, send_near, keep_far, keep_near = call(
            lambda *refs: adjoint_body(n_rows, n_cols, *refs),
            [shape(BF16, 2)] * (len(pair) // 2)
            + [shape(kind, half - near), shape(kind, near)]
            + [shape(F32, half - near), shape(F32, near)],
            [vmem()] * (1 + n_cols + len(pair)),
            [dense, *blocks, *pair],
            hop_flops,
            "adjoint",
        )
        far = add(keep_far, send(send_far, "rows", n_rows, 1), [kind] * (half - near), "add_far")
        far = [send(far[s - near], "rows", n_rows, 2 * s) for s in range(near, half)]
        kinds = [F32] + [kind] * (near - 1)
        close = add(keep_near, send(send_near, "rows", n_rows, 1), kinds, "add_near")
        close = [close[0]] + [send(close[s], "rows", n_rows, 2 * s) for s in range(1, near)]
        return close + far, both

    def forward_hop(part, kind, paired, after):
        panels = [part] + [send(part, "rows", n_rows, 2 * s) for s in range(1, half)]
        if not paired:
            (packed,) = call(
                pack_body, [shape(BF16, half)], [vmem()] * half, panels, 0, "pack"
            )
            panels = panels + [send(packed, "rows", n_rows, 1)]
        sums = call(
            lambda *refs: forward_body(half, n_cols, paired, *refs),
            [shape(kind)] * n_cols,
            [vmem()] * (1 + len(panels)),
            [dense, *panels],
            hop_flops,
            "forward",
            after=after,
        )
        return [sums[0]] + [send(sums[s], "cols", n_cols, s) for s in range(1, n_cols)]

    def forward_end(parts, kind, after=()):
        return call(
            forward_end_body,
            [shape(kind)],
            [vmem()] * (2 + n_cols),
            (h_start, column, *parts),
            0,
            "forward_end",
            after=after,
        )[0]

    back, (both,) = adjoint_hop(q0, F32, [p0, send(p0, "rows", n_rows, 1)])
    first = forward_hop(both, F32, True, back[:1])
    d1, q1 = call(
        adjoint_mid_body,
        [shape(F32), shape(BF16)],
        [vmem()] * (1 + half),
        (rate, *back),
        0,
        "adjoint_mid",
    )
    p1 = forward_end(first, BF16, [d1])
    back_two, _ = adjoint_hop(q1, BF16, [])
    second = forward_hop(p1, BF16, False, back_two[:1])
    propagated = forward_end(second, F32)
    (input_grad,) = call(
        adjoint_end_body,
        [shape(F32)],
        [vmem()] * (4 + half),
        (cotangent, d1, rate, column, *back_two),
        0,
        "adjoint_end",
    )
    return propagated, input_grad


def solution(mesh):
    placed = (
        P(("rows", "cols"), None),
        P(("rows", "cols"), None),
        P(("rows", "cols")),
        P(),
        P("rows", "cols", None, None, None),
        P("rows", "cols", None),
        P("rows", "cols", None),
        P("rows", "cols"),
    )
    return jax.shard_map(
        shards,
        mesh=mesh,
        in_specs=placed,
        out_specs=(P(("rows", "cols"), None), P(("rows", "cols"), None)),
        check_vma=False,
    )
```

```python
import jax
import jax.numpy as jnp
from jax import lax
from jax.experimental import pallas as pl
from jax.experimental.pallas import tpu as pltpu
from jax.sharding import PartitionSpec as P

VMEM_LIMIT = 32 * 1024 * 1024
BF16 = jnp.bfloat16
F32 = jnp.float32


def vmem():
    return pl.BlockSpec(memory_space=pltpu.VMEM)


def smem():
    return pl.BlockSpec(memory_space=pltpu.SMEM)


def hbm():
    return pl.BlockSpec(memory_space=pltpu.HBM)


def in_hbm(*arrays):
    return [pltpu.with_memory_space_constraint(a, pltpu.HBM) for a in arrays]


def call(body, outs, in_specs, args, flops, name, scratch=(), after=()):
    nbytes = sum(a.size * a.dtype.itemsize for a in (*args, *outs))
    count = len(args)

    def ordered(*refs):
        body(*refs[:count], *refs[count + len(after) :])

    return pl.pallas_call(
        ordered,
        out_shape=outs,
        in_specs=[*in_specs, *[pl.BlockSpec(memory_space=pl.ANY)] * len(after)],
        out_specs=[vmem()] * len(outs),
        scratch_shapes=list(scratch),
        compiler_params=pltpu.CompilerParams(vmem_limit_bytes=VMEM_LIMIT),
        cost_estimate=pl.CostEstimate(flops=flops, bytes_accessed=nbytes, transcendentals=0),
        name=name,
    )(*args, *after)


def rate_row(types_ref, teleport_ref):
    types = types_ref[...]
    rate = jnp.zeros(types.shape, F32)
    for t in range(teleport_ref.shape[0]):
        rate = jnp.where(types == t, teleport_ref[t], rate)
    return rate


def rate_column(row, width):
    size = row.shape[1]
    return jnp.broadcast_to(row, (width, size)).T


def start_body(
    row_hbm,
    col_hbm,
    types_hbm,
    teleport_hbm,
    cot_hbm,
    h_hbm,
    tiles_hbm,
    count_ref,
    q_ref,
    p_ref,
    rate_ref,
    column_ref,
    dense_ref,
    row_ref,
    col_ref,
    types_ref,
    teleport_ref,
    cot_ref,
    h_ref,
    sems,
    slot_sems,
):
    sources = (row_hbm, col_hbm, types_hbm, teleport_hbm, cot_hbm, h_hbm)
    targets = (row_ref, col_ref, types_ref, teleport_ref, cot_ref, h_ref)
    copies = [
        pltpu.make_async_copy(a, b, sems.at[i]) for i, (a, b) in enumerate(zip(sources, targets))
    ]
    for copy in copies:
        copy.start()
    size = tiles_hbm.shape[-1]
    me_row = lax.axis_index("rows")
    me_col = lax.axis_index("cols")
    dense_ref[...] = jnp.zeros_like(dense_ref)
    copies[0].wait()
    copies[1].wait()
    count = count_ref[0, 0]

    def tile_copy(slot):
        row = row_ref[0, 0, slot] ^ me_col
        col = col_ref[0, 0, slot] ^ me_row
        return pltpu.make_async_copy(
            tiles_hbm.at[0, 0, slot],
            dense_ref.at[
                pl.ds(pl.multiple_of(row * size, size), size),
                pl.ds(pl.multiple_of(col * size, size), size),
            ],
            slot_sems.at[slot],
        )

    def begin(slot, carry):
        tile_copy(slot).start()
        return carry

    def end(slot, carry):
        tile_copy(slot).wait()
        return carry

    lax.fori_loop(0, count, begin, 0)
    for copy in copies[2:]:
        copy.wait()
    rate = rate_row(types_ref, teleport_ref)
    rate_ref[...] = rate
    column_ref[...] = rate_column(rate, h_ref.shape[1])
    q_ref[...] = ((1.0 - rate) * cot_ref[...].T).astype(BF16)
    p_ref[...] = h_ref[...].astype(BF16)
    lax.fori_loop(0, count, end, 0)


def adjoint_body(n_rows, n_cols, dense_ref, *refs):
    blocks, outs = refs[:n_cols], refs[n_cols:]
    send_far, send_near, keep_far, keep_near = outs
    half = n_rows // 2
    near = send_near.shape[0]
    size = blocks[0].shape[1]
    left = jnp.concatenate([b[...] for b in blocks], axis=1)
    for zz in reversed(range(half)):
        part = jnp.dot(
            left, dense_ref[:, 2 * zz * size : (2 * zz + 2) * size], preferred_element_type=F32
        )
        keep, send, at = (
            (keep_near, send_near, zz) if zz < near else (keep_far, send_far, zz - near)
        )
        keep[at] = part[:, :size]
        send[at] = part[:, size:].astype(send.dtype)


def add_body(keep_ref, got_ref, *outs):
    for at, out in enumerate(outs):
        out[...] = (keep_ref[at] + got_ref[at].astype(F32)).astype(out.dtype)


def pack_body(*refs):
    *parts, out_ref = refs
    for at, part in enumerate(parts):
        out_ref[at] = part[...]


def forward_body(half, n_cols, paired, dense_ref, *refs):
    count = half if paired else half + 1
    panels, outs = refs[:count], refs[count:]
    size = panels[0].shape[-1]
    total = None
    for zz in range(half):
        if paired:
            panel = jnp.concatenate([panels[zz][0], panels[zz][1]], axis=0)
        else:
            panel = jnp.concatenate([panels[zz][...], panels[half][zz]], axis=0)
        part = jnp.dot(
            dense_ref[:, 2 * zz * size : (2 * zz + 2) * size], panel, preferred_element_type=F32
        )
        total = part if total is None else total + part
    for j in range(n_cols):
        outs[j][...] = total[j * size : (j + 1) * size].astype(outs[j].dtype)


def sum_refs(refs):
    terms = [ref[...].astype(F32) for ref in refs]
    while len(terms) > 1:
        terms = [sum(terms[i : i + 2][1:], terms[i]) for i in range(0, len(terms), 2)]
    return terms[0]


def forward_end_body(h_ref, rate_ref, *refs):
    *parts, out_ref = refs
    rate = rate_ref[...]
    value = (1.0 - rate) * sum_refs(parts) + rate * h_ref[...]
    out_ref[...] = value.astype(out_ref.dtype)


def adjoint_mid_body(rate_ref, *refs):
    *parts, d_ref, q_ref = refs
    total = sum_refs(parts)
    d_ref[...] = total
    q_ref[...] = ((1.0 - rate_ref[...]) * total).astype(BF16)


def adjoint_end_body(cot_ref, d_ref, row_ref, column_ref, *refs):
    *parts, out_ref = refs
    change = (row_ref[...] * d_ref[...] + sum_refs(parts)).T
    out_ref[...] = column_ref[...] * cot_ref[...] + change


def send(value, axis, count, step):
    return lax.ppermute(value, axis, [(i, i ^ step) for i in range(count)])


def shards(h_start, cotangent, node_type, teleport, tile_values, tile_row, tile_col, tile_count):
    n_rows = lax.axis_size("rows")
    n_cols = lax.axis_size("cols")
    half = n_rows // 2
    near = half // 2
    size = tile_values.shape[-1]
    slots = tile_values.shape[2]
    features = h_start.shape[-1]
    types = node_type.reshape(1, size)
    hop_flops = 2 * n_rows * n_cols * size * size * features

    def shape(kind, *lead):
        return jax.ShapeDtypeStruct((*lead, size, features), kind)

    q0, p0, rate, column, dense = call(
        start_body,
        [
            shape(BF16),
            shape(BF16),
            jax.ShapeDtypeStruct((1, size), F32),
            shape(F32),
            jax.ShapeDtypeStruct((n_cols * size, n_rows * size), BF16),
        ],
        [hbm()] * 7 + [smem()],
        [
            *in_hbm(tile_row, tile_col, types, teleport, cotangent, h_start, tile_values),
            tile_count,
        ],
        0,
        "start",
        [
            pltpu.SMEM(tile_row.shape, jnp.int32),
            pltpu.SMEM(tile_col.shape, jnp.int32),
            pltpu.VMEM(types.shape, jnp.int32),
            pltpu.SMEM(teleport.shape, F32),
            pltpu.VMEM(cotangent.shape, F32),
            pltpu.VMEM(h_start.shape, F32),
            pltpu.SemaphoreType.DMA((6,)),
            pltpu.SemaphoreType.DMA((slots,)),
        ],
    )

    def add(keep, got, kinds, name, after=()):
        outs = [shape(kind) for kind in kinds]
        return call(add_body, outs, [vmem()] * 2, (keep, got), 0, name, after=after)

    def pack(parts, after=()):
        (packed,) = call(
            pack_body, [shape(BF16, len(parts))], [vmem()] * len(parts), parts, 0, "pack", after=after
        )
        return packed

    def swap_cols(parts):
        return [parts[0]] + [send(parts[s], "cols", n_cols, s) for s in range(1, n_cols)]

    def swap_high(part):
        return [part] + [send(part, "rows", n_rows, 2 * s) for s in range(1, half)]

    def adjoint_products(part, kind, after=()):
        return call(
            lambda *refs: adjoint_body(n_rows, n_cols, *refs),
            [shape(kind, half - near), shape(kind, near)]
            + [shape(F32, half - near), shape(F32, near)],
            [vmem()] * (1 + n_cols),
            [dense, *swap_cols([part] * n_cols)],
            hop_flops,
            "adjoint",
            after=after,
        )

    def far_sums(keep, sent, kind):
        got = send(sent, "rows", n_rows, 1)
        sums = add(keep, got, [kind] * (half - near), "add_far")
        return sums[:1], [send(sums[s - near], "rows", n_rows, 2 * s) for s in range(near, half)]

    def near_sums(keep, sent, kind, after):
        got = send(sent, "rows", n_rows, 1)
        sums = add(keep, got, [F32] + [kind] * (near - 1), "add_near", after)
        return [sums[0]] + [send(sums[s], "rows", n_rows, 2 * s) for s in range(1, near)]

    def forward_products(panels, kind, paired, after):
        return call(
            lambda *refs: forward_body(half, n_cols, paired, *refs),
            [shape(kind)] * n_cols,
            [vmem()] * (1 + len(panels)),
            [dense, *panels],
            hop_flops,
            "forward",
            after=after,
        )

    def forward_end(parts, kind):
        return call(
            forward_end_body,
            [shape(kind)],
            [vmem()] * (2 + n_cols),
            (h_start, column, *parts),
            0,
            "forward_end",
        )[0]

    both = pack([p0, send(p0, "rows", n_rows, 1)])
    panels = swap_high(both)
    send_far, send_near, keep_far, keep_near = adjoint_products(q0, F32, [both])
    last, far = far_sums(keep_far, send_far, F32)
    close = near_sums(keep_near, send_near, F32, last)
    first = forward_products(panels, F32, True, close[:1])
    p1 = forward_end(swap_cols(first), BF16)
    panels = swap_high(p1)
    d1, q1 = call(
        adjoint_mid_body,
        [shape(F32), shape(BF16)],
        [vmem()] * (1 + half),
        (rate, *close, *far),
        0,
        "adjoint_mid",
        after=[p1],
    )
    panels = panels + [send(pack(panels, [q1]), "rows", n_rows, 1)]
    send_far, send_near, keep_far, keep_near = adjoint_products(q1, BF16)
    last, far = far_sums(keep_far, send_far, BF16)
    close = near_sums(keep_near, send_near, BF16, last)
    second = forward_products(panels, BF16, False, close[:1])
    propagated = forward_end(swap_cols(second), F32)
    (input_grad,) = call(
        adjoint_end_body,
        [shape(F32)],
        [vmem()] * (4 + half),
        (cotangent, d1, rate, column, *close, *far),
        0,
        "adjoint_end",
    )
    return propagated, input_grad


def solution(mesh):
    placed = (
        P(("rows", "cols"), None),
        P(("rows", "cols"), None),
        P(("rows", "cols")),
        P(),
        P("rows", "cols", None, None, None),
        P("rows", "cols", None),
        P("rows", "cols", None),
        P("rows", "cols"),
    )
    return jax.shard_map(
        shards,
        mesh=mesh,
        in_specs=placed,
        out_specs=(P(("rows", "cols"), None), P(("rows", "cols"), None)),
        check_vma=False,
    )
```

```python
import jax
import jax.numpy as jnp
from jax import lax
from jax.experimental import pallas as pl
from jax.experimental.pallas import tpu as pltpu
from jax.sharding import PartitionSpec as P

VMEM_LIMIT = 32 * 1024 * 1024
BF16 = jnp.bfloat16
F32 = jnp.float32


def vmem():
    return pl.BlockSpec(memory_space=pltpu.VMEM)


def smem():
    return pl.BlockSpec(memory_space=pltpu.SMEM)


def hbm():
    return pl.BlockSpec(memory_space=pltpu.HBM)


def in_hbm(*arrays):
    return [pltpu.with_memory_space_constraint(a, pltpu.HBM) for a in arrays]


def call(body, outs, in_specs, args, flops, name, scratch=(), after=()):
    nbytes = sum(a.size * a.dtype.itemsize for a in (*args, *outs))
    count = len(args)

    def ordered(*refs):
        body(*refs[:count], *refs[count + len(after) :])

    return pl.pallas_call(
        ordered,
        out_shape=outs,
        in_specs=[*in_specs, *[pl.BlockSpec(memory_space=pl.ANY)] * len(after)],
        out_specs=[vmem()] * len(outs),
        scratch_shapes=list(scratch),
        compiler_params=pltpu.CompilerParams(vmem_limit_bytes=VMEM_LIMIT),
        cost_estimate=pl.CostEstimate(flops=flops, bytes_accessed=nbytes, transcendentals=0),
        name=name,
    )(*args, *after)


def fetch(pairs, sems):
    copies = [pltpu.make_async_copy(a, b, sems.at[i]) for i, (a, b) in enumerate(pairs)]
    for copy in copies:
        copy.start()
    for copy in copies:
        copy.wait()


def rate_row(types_ref, teleport_ref):
    types = types_ref[...]
    rate = jnp.zeros(types.shape, F32)
    for t in range(teleport_ref.shape[0]):
        rate = jnp.where(types == t, teleport_ref[t], rate)
    return rate


def rate_column(row, width):
    size = row.shape[1]
    return jnp.broadcast_to(row, (width, size)).T


def start_body(
    cot_hbm,
    h_hbm,
    types_hbm,
    teleport_hbm,
    q_ref,
    p_ref,
    row_ref,
    column_ref,
    cot_ref,
    h_ref,
    types_ref,
    teleport_ref,
    sems,
):
    fetch(
        [
            (types_hbm, types_ref),
            (teleport_hbm, teleport_ref),
            (cot_hbm, cot_ref),
            (h_hbm, h_ref),
        ],
        sems,
    )
    rate = rate_row(types_ref, teleport_ref)
    row_ref[...] = rate
    column_ref[...] = rate_column(rate, h_ref.shape[1])
    q_ref[...] = ((1.0 - rate) * cot_ref[...].T).astype(BF16)
    p_ref[...] = h_ref[...].astype(BF16)


def dense_body(
    q_ref,
    tiles_hbm,
    row_hbm,
    col_hbm,
    count_ref,
    dense_ref,
    row_ref,
    col_ref,
    sems,
    slot_sems,
):
    size = tiles_hbm.shape[-1]
    me_row = lax.axis_index("rows")
    me_col = lax.axis_index("cols")
    dense_ref[...] = jnp.zeros_like(dense_ref)
    fetch([(row_hbm, row_ref), (col_hbm, col_ref)], sems)
    count = count_ref[0, 0]

    def copy(slot):
        row = row_ref[0, 0, slot] ^ me_col
        col = col_ref[0, 0, slot] ^ me_row
        return pltpu.make_async_copy(
            tiles_hbm.at[0, 0, slot],
            dense_ref.at[
                pl.ds(pl.multiple_of(row * size, size), size),
                pl.ds(pl.multiple_of(col * size, size), size),
            ],
            slot_sems.at[slot],
        )

    def begin(slot, carry):
        copy(slot).start()
        return carry

    def end(slot, carry):
        copy(slot).wait()
        return carry

    lax.fori_loop(0, count, begin, 0)
    lax.fori_loop(0, count, end, 0)


def adjoint_body(n_rows, n_cols, dense_ref, *refs):
    blocks, outs = refs[:n_cols], refs[n_cols:]
    send_far, send_near, keep_far, keep_near = outs
    half = n_rows // 2
    near = send_near.shape[0]
    size = blocks[0].shape[1]
    left = jnp.concatenate([b[...] for b in blocks], axis=1)
    for zz in reversed(range(half)):
        part = jnp.dot(
            left, dense_ref[:, 2 * zz * size : (2 * zz + 2) * size], preferred_element_type=F32
        )
        keep, send, at = (
            (keep_near, send_near, zz) if zz < near else (keep_far, send_far, zz - near)
        )
        keep[at] = part[:, :size]
        send[at] = part[:, size:].astype(send.dtype)


def add_body(keep_ref, got_ref, *outs):
    for at, out in enumerate(outs):
        out[...] = (keep_ref[at] + got_ref[at].astype(F32)).astype(out.dtype)


def pack_body(*refs):
    *parts, out_ref = refs
    for at, part in enumerate(parts):
        out_ref[at] = part[...]


def forward_body(half, n_cols, dense_ref, *refs):
    panels, other_ref, outs = refs[:half], refs[half], refs[half + 1 :]
    size = other_ref.shape[-1]
    total = None
    for zz in range(half):
        panel = jnp.concatenate([panels[zz][...], other_ref[zz]], axis=0)
        part = jnp.dot(
            dense_ref[:, 2 * zz * size : (2 * zz + 2) * size], panel, preferred_element_type=F32
        )
        total = part if total is None else total + part
    for j in range(n_cols):
        outs[j][...] = total[j * size : (j + 1) * size].astype(outs[j].dtype)


def sum_refs(refs):
    terms = [ref[...].astype(F32) for ref in refs]
    while len(terms) > 1:
        terms = [sum(terms[i : i + 2][1:], terms[i]) for i in range(0, len(terms), 2)]
    return terms[0]


def forward_end_body(h_ref, rate_ref, *refs):
    *parts, out_ref = refs
    rate = rate_ref[...]
    value = (1.0 - rate) * sum_refs(parts) + rate * h_ref[...]
    out_ref[...] = value.astype(out_ref.dtype)


def adjoint_mid_body(rate_ref, *refs):
    *parts, d_ref, q_ref = refs
    total = sum_refs(parts)
    d_ref[...] = total
    q_ref[...] = ((1.0 - rate_ref[...]) * total).astype(BF16)


def adjoint_end_body(cot_ref, d_ref, row_ref, column_ref, *refs):
    *parts, out_ref = refs
    change = (row_ref[...] * d_ref[...] + sum_refs(parts)).T
    out_ref[...] = column_ref[...] * cot_ref[...] + change


def send(value, axis, count, step):
    return lax.ppermute(value, axis, [(i, i ^ step) for i in range(count)])


def shards(h_start, cotangent, node_type, teleport, tile_values, tile_row, tile_col, tile_count):
    n_rows = lax.axis_size("rows")
    n_cols = lax.axis_size("cols")
    half = n_rows // 2
    near = half // 2
    size = tile_values.shape[-1]
    slots = tile_values.shape[2]
    features = h_start.shape[-1]
    types = node_type.reshape(1, size)
    hop_flops = 2 * n_rows * n_cols * size * size * features

    def shape(kind, *lead):
        return jax.ShapeDtypeStruct((*lead, size, features), kind)

    q0, p0, rate, column = call(
        start_body,
        [shape(BF16), shape(BF16), jax.ShapeDtypeStruct((1, size), F32), shape(F32)],
        [hbm()] * 4,
        in_hbm(cotangent, h_start, types, teleport),
        0,
        "start",
        [
            pltpu.VMEM(cotangent.shape, F32),
            pltpu.VMEM(h_start.shape, F32),
            pltpu.VMEM(types.shape, jnp.int32),
            pltpu.SMEM(teleport.shape, F32),
            pltpu.SemaphoreType.DMA((4,)),
        ],
    )
    (dense,) = call(
        dense_body,
        [jax.ShapeDtypeStruct((n_cols * size, n_rows * size), BF16)],
        [vmem()] + [hbm()] * 3 + [smem()],
        [q0, *in_hbm(tile_values, tile_row, tile_col), tile_count],
        0,
        "dense",
        [
            pltpu.SMEM(tile_row.shape, jnp.int32),
            pltpu.SMEM(tile_col.shape, jnp.int32),
            pltpu.SemaphoreType.DMA((2,)),
            pltpu.SemaphoreType.DMA((slots,)),
        ],
    )

    def add(keep, got, kinds, name):
        return call(add_body, [shape(kind) for kind in kinds], [vmem()] * 2, (keep, got), 0, name)

    def adjoint_hop(part, kind):
        blocks = [part] + [send(part, "cols", n_cols, s) for s in range(1, n_cols)]
        send_far, send_near, keep_far, keep_near = call(
            lambda *refs: adjoint_body(n_rows, n_cols, *refs),
            [shape(kind, half - near), shape(kind, near)]
            + [shape(F32, half - near), shape(F32, near)],
            [vmem()] * (1 + n_cols),
            [dense, *blocks],
            hop_flops,
            "adjoint",
        )
        far = add(keep_far, send(send_far, "rows", n_rows, 1), [kind] * (half - near), "add_far")
        far = [send(far[s - near], "rows", n_rows, 2 * s) for s in range(near, half)]
        kinds = [F32] + [kind] * (near - 1)
        close = add(keep_near, send(send_near, "rows", n_rows, 1), kinds, "add_near")
        close = [close[0]] + [send(close[s], "rows", n_rows, 2 * s) for s in range(1, near)]
        return close + far, blocks

    def forward_hop(part, kind, after):
        panels = [part] + [send(part, "rows", n_rows, 2 * s) for s in range(1, half)]
        (packed,) = call(pack_body, [shape(BF16, half)], [vmem()] * half, panels, 0, "pack")
        panels = panels + [send(packed, "rows", n_rows, 1)]
        sums = call(
            lambda *refs: forward_body(half, n_cols, *refs),
            [shape(kind)] * n_cols,
            [vmem()] * (1 + len(panels)),
            [dense, *panels],
            hop_flops,
            "forward",
            after=after,
        )
        return [sums[0]] + [send(sums[s], "cols", n_cols, s) for s in range(1, n_cols)]

    def forward_end(parts, kind, after=()):
        return call(
            forward_end_body,
            [shape(kind)],
            [vmem()] * (2 + n_cols),
            (h_start, column, *parts),
            0,
            "forward_end",
            after=after,
        )[0]

    back, _ = adjoint_hop(q0, F32)
    first = forward_hop(p0, F32, back[:1])
    d1, q1 = call(
        adjoint_mid_body,
        [shape(F32), shape(BF16)],
        [vmem()] * (1 + half),
        (rate, *back),
        0,
        "adjoint_mid",
    )
    back_two, blocks = adjoint_hop(q1, BF16)
    p1 = forward_end(first, BF16, blocks[1:])
    second = forward_hop(p1, BF16, back_two[:1])
    propagated = forward_end(second, F32)
    (input_grad,) = call(
        adjoint_end_body,
        [shape(F32)],
        [vmem()] * (4 + half),
        (cotangent, d1, rate, column, *back_two),
        0,
        "adjoint_end",
    )
    return propagated, input_grad


def solution(mesh):
    placed = (
        P(("rows", "cols"), None),
        P(("rows", "cols"), None),
        P(("rows", "cols")),
        P(),
        P("rows", "cols", None, None, None),
        P("rows", "cols", None),
        P("rows", "cols", None),
        P("rows", "cols"),
    )
    return jax.shard_map(
        shards,
        mesh=mesh,
        in_specs=placed,
        out_specs=(P(("rows", "cols"), None), P(("rows", "cols"), None)),
        check_vma=False,
    )
```

```python
import jax
import jax.numpy as jnp
from jax import lax
from jax.experimental import pallas as pl
from jax.experimental.pallas import tpu as pltpu
from jax.sharding import PartitionSpec as P

VMEM_LIMIT = 32 * 1024 * 1024
BF16 = jnp.bfloat16
F32 = jnp.float32


def vmem():
    return pl.BlockSpec(memory_space=pltpu.VMEM)


def smem():
    return pl.BlockSpec(memory_space=pltpu.SMEM)


def hbm():
    return pl.BlockSpec(memory_space=pltpu.HBM)


def in_hbm(*arrays):
    return [pltpu.with_memory_space_constraint(a, pltpu.HBM) for a in arrays]


def call(body, outs, in_specs, args, flops, name, scratch=(), after=()):
    nbytes = sum(a.size * a.dtype.itemsize for a in (*args, *outs))
    count = len(args)

    def ordered(*refs):
        body(*refs[:count], *refs[count + len(after) :])

    return pl.pallas_call(
        ordered,
        out_shape=outs,
        in_specs=[*in_specs, *[pl.BlockSpec(memory_space=pl.ANY)] * len(after)],
        out_specs=[vmem()] * len(outs),
        scratch_shapes=list(scratch),
        compiler_params=pltpu.CompilerParams(vmem_limit_bytes=VMEM_LIMIT),
        cost_estimate=pl.CostEstimate(flops=flops, bytes_accessed=nbytes, transcendentals=0),
        name=name,
    )(*args, *after)


def fetch(pairs, sems):
    copies = [pltpu.make_async_copy(a, b, sems.at[i]) for i, (a, b) in enumerate(pairs)]
    for copy in copies:
        copy.start()
    for copy in copies:
        copy.wait()


def rate_row(types_ref, teleport_ref):
    types = types_ref[...]
    rate = jnp.zeros(types.shape, F32)
    for t in range(teleport_ref.shape[0]):
        rate = jnp.where(types == t, teleport_ref[t], rate)
    return rate


def rate_column(row, width):
    size = row.shape[1]
    return jnp.broadcast_to(row, (width, size)).T


def start_body(
    cot_hbm,
    h_hbm,
    types_hbm,
    teleport_hbm,
    q_ref,
    p_ref,
    row_ref,
    column_ref,
    cot_ref,
    h_ref,
    types_ref,
    teleport_ref,
    sems,
):
    fetch(
        [
            (types_hbm, types_ref),
            (teleport_hbm, teleport_ref),
            (cot_hbm, cot_ref),
            (h_hbm, h_ref),
        ],
        sems,
    )
    rate = rate_row(types_ref, teleport_ref)
    row_ref[...] = rate
    column_ref[...] = rate_column(rate, h_ref.shape[1])
    q_ref[...] = ((1.0 - rate) * cot_ref[...].T).astype(BF16)
    p_ref[...] = h_ref[...].astype(BF16)


def dense_body(
    q_ref,
    tiles_hbm,
    row_hbm,
    col_hbm,
    count_ref,
    dense_ref,
    row_ref,
    col_ref,
    sems,
    slot_sems,
):
    size = tiles_hbm.shape[-1]
    me_row = lax.axis_index("rows")
    me_col = lax.axis_index("cols")
    dense_ref[...] = jnp.zeros_like(dense_ref)
    fetch([(row_hbm, row_ref), (col_hbm, col_ref)], sems)
    count = count_ref[0, 0]

    def copy(slot):
        row = row_ref[0, 0, slot] ^ me_col
        col = col_ref[0, 0, slot] ^ me_row
        return pltpu.make_async_copy(
            tiles_hbm.at[0, 0, slot],
            dense_ref.at[
                pl.ds(pl.multiple_of(row * size, size), size),
                pl.ds(pl.multiple_of(col * size, size), size),
            ],
            slot_sems.at[slot],
        )

    def begin(slot, carry):
        copy(slot).start()
        return carry

    def end(slot, carry):
        copy(slot).wait()
        return carry

    lax.fori_loop(0, count, begin, 0)
    lax.fori_loop(0, count, end, 0)


def adjoint_body(n_rows, n_cols, dense_ref, *refs):
    blocks, outs = refs[:n_cols], refs[n_cols:]
    send_far, send_near, keep_far, keep_near = outs
    half = n_rows // 2
    near = send_near.shape[0]
    size = blocks[0].shape[1]
    left = jnp.concatenate([b[...] for b in blocks], axis=1)
    for zz in reversed(range(half)):
        part = jnp.dot(
            left, dense_ref[:, 2 * zz * size : (2 * zz + 2) * size], preferred_element_type=F32
        )
        keep, send, at = (
            (keep_near, send_near, zz) if zz < near else (keep_far, send_far, zz - near)
        )
        keep[at] = part[:, :size]
        send[at] = part[:, size:].astype(send.dtype)


def add_body(keep_ref, got_ref, *outs):
    for at, out in enumerate(outs):
        out[...] = (keep_ref[at] + got_ref[at].astype(F32)).astype(out.dtype)


def pack_body(*refs):
    *parts, out_ref = refs
    for at, part in enumerate(parts):
        out_ref[at] = part[...]


def forward_body(half, n_cols, dense_ref, *refs):
    panels, other_ref, outs = refs[:half], refs[half], refs[half + 1 :]
    size = other_ref.shape[-1]
    total = None
    for zz in range(half):
        panel = jnp.concatenate([panels[zz][...], other_ref[zz]], axis=0)
        part = jnp.dot(
            dense_ref[:, 2 * zz * size : (2 * zz + 2) * size], panel, preferred_element_type=F32
        )
        total = part if total is None else total + part
    for j in range(n_cols):
        outs[j][...] = total[j * size : (j + 1) * size].astype(outs[j].dtype)


def sum_refs(refs):
    terms = [ref[...].astype(F32) for ref in refs]
    while len(terms) > 1:
        terms = [sum(terms[i : i + 2][1:], terms[i]) for i in range(0, len(terms), 2)]
    return terms[0]


def forward_end_body(h_ref, rate_ref, *refs):
    *parts, out_ref = refs
    rate = rate_ref[...]
    value = (1.0 - rate) * sum_refs(parts) + rate * h_ref[...]
    out_ref[...] = value.astype(out_ref.dtype)


def middle_body(half, row_ref, column_ref, h_ref, *refs):
    back, refs = refs[:half], refs[half:]
    *first, d_ref, q_ref, p_ref = refs
    total = sum_refs(back)
    d_ref[...] = total
    q_ref[...] = ((1.0 - row_ref[...]) * total).astype(BF16)
    rate = column_ref[...]
    p_ref[...] = ((1.0 - rate) * sum_refs(first) + rate * h_ref[...]).astype(BF16)


def adjoint_end_body(cot_ref, d_ref, row_ref, column_ref, *refs):
    *parts, out_ref = refs
    change = (row_ref[...] * d_ref[...] + sum_refs(parts)).T
    out_ref[...] = column_ref[...] * cot_ref[...] + change


ADD_COST = 400_000_000


def send(value, axis, count, step):
    return lax.ppermute(value, axis, [(i, i ^ step) for i in range(count)])


def shards(h_start, cotangent, node_type, teleport, tile_values, tile_row, tile_col, tile_count):
    n_rows = lax.axis_size("rows")
    n_cols = lax.axis_size("cols")
    half = n_rows // 2
    near = half // 2
    size = tile_values.shape[-1]
    slots = tile_values.shape[2]
    features = h_start.shape[-1]
    types = node_type.reshape(1, size)
    hop_flops = 2 * n_rows * n_cols * size * size * features

    def shape(kind, *lead):
        return jax.ShapeDtypeStruct((*lead, size, features), kind)

    q0, p0, rate, column = call(
        start_body,
        [shape(BF16), shape(BF16), jax.ShapeDtypeStruct((1, size), F32), shape(F32)],
        [hbm()] * 4,
        in_hbm(cotangent, h_start, types, teleport),
        0,
        "start",
        [
            pltpu.VMEM(cotangent.shape, F32),
            pltpu.VMEM(h_start.shape, F32),
            pltpu.VMEM(types.shape, jnp.int32),
            pltpu.SMEM(teleport.shape, F32),
            pltpu.SemaphoreType.DMA((4,)),
        ],
    )
    (dense,) = call(
        dense_body,
        [jax.ShapeDtypeStruct((n_cols * size, n_rows * size), BF16)],
        [vmem()] + [hbm()] * 3 + [smem()],
        [q0, *in_hbm(tile_values, tile_row, tile_col), tile_count],
        0,
        "dense",
        [
            pltpu.SMEM(tile_row.shape, jnp.int32),
            pltpu.SMEM(tile_col.shape, jnp.int32),
            pltpu.SemaphoreType.DMA((2,)),
            pltpu.SemaphoreType.DMA((slots,)),
        ],
    )

    def add(keep, got, kinds, name, after=()):
        outs = [shape(kind) for kind in kinds]
        hint = ADD_COST if kinds[-1] == BF16 else 0
        return call(add_body, outs, [vmem()] * 2, (keep, got), hint, name, after=after)

    def adjoint_hop(part, kind):
        blocks = [part] + [send(part, "cols", n_cols, s) for s in range(1, n_cols)]
        send_far, send_near, keep_far, keep_near = call(
            lambda *refs: adjoint_body(n_rows, n_cols, *refs),
            [shape(kind, half - near), shape(kind, near)]
            + [shape(F32, half - near), shape(F32, near)],
            [vmem()] * (1 + n_cols),
            [dense, *blocks],
            hop_flops,
            "adjoint",
        )
        far = add(keep_far, send(send_far, "rows", n_rows, 1), [kind] * (half - near), "add_far")
        far = [send(far[s - near], "rows", n_rows, 2 * s) for s in range(near, half)]
        kinds = [F32] + [kind] * (near - 1)
        close = add(keep_near, send(send_near, "rows", n_rows, 1), kinds, "add_near")
        close = [close[0]] + [send(close[s], "rows", n_rows, 2 * s) for s in range(1, near)]
        return far + close, close[:1]

    def forward_hop(part, kind, after):
        panels = [part] + [send(part, "rows", n_rows, 2 * s) for s in range(1, half)]
        (packed,) = call(pack_body, [shape(BF16, half)], [vmem()] * half, panels, 0, "pack")
        panels = panels + [send(packed, "rows", n_rows, 1)]
        sums = call(
            lambda *refs: forward_body(half, n_cols, *refs),
            [shape(kind)] * n_cols,
            [vmem()] * (1 + len(panels)),
            [dense, *panels],
            hop_flops,
            "forward",
            after=after,
        )
        return [sums[0]] + [send(sums[s], "cols", n_cols, s) for s in range(1, n_cols)]

    def forward_end(parts, kind, after=()):
        return call(
            forward_end_body,
            [shape(kind)],
            [vmem()] * (2 + n_cols),
            (h_start, column, *parts),
            0,
            "forward_end",
            after=after,
        )[0]

    back, last = adjoint_hop(q0, F32)
    first = forward_hop(p0, F32, last)
    d1, q1, p1 = call(
        lambda *refs: middle_body(half, *refs),
        [shape(F32), shape(BF16), shape(BF16)],
        [vmem()] * (3 + half + n_cols),
        (rate, column, h_start, *back, *first),
        0,
        "middle",
    )
    back_two, last = adjoint_hop(q1, BF16)
    second = forward_hop(p1, BF16, last)
    propagated = forward_end(second, F32)
    (input_grad,) = call(
        adjoint_end_body,
        [shape(F32)],
        [vmem()] * (4 + half),
        (cotangent, d1, rate, column, *back_two),
        0,
        "adjoint_end",
    )
    return propagated, input_grad


def solution(mesh):
    placed = (
        P(("rows", "cols"), None),
        P(("rows", "cols"), None),
        P(("rows", "cols")),
        P(),
        P("rows", "cols", None, None, None),
        P("rows", "cols", None),
        P("rows", "cols", None),
        P("rows", "cols"),
    )
    return jax.shard_map(
        shards,
        mesh=mesh,
        in_specs=placed,
        out_specs=(P(("rows", "cols"), None), P(("rows", "cols"), None)),
        check_vma=False,
    )
```

```python
import jax
import jax.numpy as jnp
from jax import lax
from jax.experimental import pallas as pl
from jax.experimental.pallas import tpu as pltpu
from jax.sharding import PartitionSpec as P

VMEM_LIMIT = 32 * 1024 * 1024
BF16 = jnp.bfloat16
F32 = jnp.float32


def vmem():
    return pl.BlockSpec(memory_space=pltpu.VMEM)


def smem():
    return pl.BlockSpec(memory_space=pltpu.SMEM)


def hbm():
    return pl.BlockSpec(memory_space=pltpu.HBM)


def in_hbm(*arrays):
    return [pltpu.with_memory_space_constraint(a, pltpu.HBM) for a in arrays]


def call(body, outs, in_specs, args, flops, name, scratch=(), after=()):
    nbytes = sum(a.size * a.dtype.itemsize for a in (*args, *outs))
    count = len(args)

    def ordered(*refs):
        body(*refs[:count], *refs[count + len(after) :])

    return pl.pallas_call(
        ordered,
        out_shape=outs,
        in_specs=[*in_specs, *[pl.BlockSpec(memory_space=pl.ANY)] * len(after)],
        out_specs=[vmem()] * len(outs),
        scratch_shapes=list(scratch),
        compiler_params=pltpu.CompilerParams(vmem_limit_bytes=VMEM_LIMIT),
        cost_estimate=pl.CostEstimate(flops=flops, bytes_accessed=nbytes, transcendentals=0),
        name=name,
    )(*args, *after)


def fetch(pairs, sems):
    copies = [pltpu.make_async_copy(a, b, sems.at[i]) for i, (a, b) in enumerate(pairs)]
    for copy in copies:
        copy.start()
    for copy in copies:
        copy.wait()


def rate_row(types_ref, teleport_ref):
    types = types_ref[...]
    rate = jnp.zeros(types.shape, F32)
    for t in range(teleport_ref.shape[0]):
        rate = jnp.where(types == t, teleport_ref[t], rate)
    return rate


def rate_column(row, width):
    size = row.shape[1]
    return jnp.broadcast_to(row, (width, size)).T


def start_body(
    cot_hbm,
    h_hbm,
    types_hbm,
    teleport_hbm,
    q_ref,
    p_ref,
    row_ref,
    column_ref,
    cot_ref,
    h_ref,
    types_ref,
    teleport_ref,
    sems,
):
    fetch(
        [
            (types_hbm, types_ref),
            (teleport_hbm, teleport_ref),
            (cot_hbm, cot_ref),
            (h_hbm, h_ref),
        ],
        sems,
    )
    rate = rate_row(types_ref, teleport_ref)
    row_ref[...] = rate
    column_ref[...] = rate_column(rate, h_ref.shape[1])
    q_ref[...] = ((1.0 - rate) * cot_ref[...].T).astype(BF16)
    p_ref[...] = h_ref[...].astype(BF16)


def dense_body(
    q_ref,
    tiles_hbm,
    row_hbm,
    col_hbm,
    count_ref,
    dense_ref,
    row_ref,
    col_ref,
    sems,
    slot_sems,
):
    size = tiles_hbm.shape[-1]
    me_row = lax.axis_index("rows")
    me_col = lax.axis_index("cols")
    dense_ref[...] = jnp.zeros_like(dense_ref)
    fetch([(row_hbm, row_ref), (col_hbm, col_ref)], sems)
    count = count_ref[0, 0]

    def copy(slot):
        row = row_ref[0, 0, slot] ^ me_col
        col = col_ref[0, 0, slot] ^ me_row
        return pltpu.make_async_copy(
            tiles_hbm.at[0, 0, slot],
            dense_ref.at[
                pl.ds(pl.multiple_of(row * size, size), size),
                pl.ds(pl.multiple_of(col * size, size), size),
            ],
            slot_sems.at[slot],
        )

    def begin(slot, carry):
        copy(slot).start()
        return carry

    def end(slot, carry):
        copy(slot).wait()
        return carry

    lax.fori_loop(0, count, begin, 0)
    lax.fori_loop(0, count, end, 0)


def adjoint_body(n_rows, n_cols, dense_ref, *refs):
    blocks, through, outs = refs[:2], refs[2:-4], refs[-4:]
    send_far, send_near, keep_far, keep_near = outs
    for source, target in zip(through[: len(through) // 2], through[len(through) // 2 :]):
        target[...] = source[...]
    half = n_rows // 2
    size = dense_ref.shape[1] // n_rows
    left = jnp.concatenate([block_at(blocks, n_cols, j) for j in range(n_cols)], axis=1)
    for zz in [*range(1, half, 2), *range(0, half, 2)]:
        part = jnp.dot(
            left, dense_ref[:, 2 * zz * size : (2 * zz + 2) * size], preferred_element_type=F32
        )
        keep, send = (keep_far, send_far) if zz % 2 else (keep_near, send_near)
        keep[zz // 2] = part[:, :size]
        send[zz // 2] = part[:, size:].astype(send.dtype)


def block_at(blocks, count, index):
    packed, other = blocks
    return other[index // 2] if index % 2 else packed[index // 2]


def add_body(keep_ref, got_ref, out_ref):
    for at in range(out_ref.shape[0]):
        out_ref[at] = (keep_ref[at] + got_ref[at].astype(F32)).astype(out_ref.dtype)


def fold_body(*refs):
    *terms, own_ref, send_ref = refs
    for at in range(terms[0].shape[0]):
        total = terms[0][at].astype(F32)
        for term in terms[1:]:
            total = total + term[at].astype(F32)
        out_ref = send_ref if at % 2 else own_ref
        out_ref[at // 2] = total.astype(out_ref.dtype)


def pack_body(*refs):
    *parts, out_ref = refs
    for at, part in enumerate(parts):
        out_ref[at] = part[...]


def forward_body(half, n_cols, dense_ref, *refs):
    panels, other_ref, keep_ref, send_ref = refs[:half], refs[half], refs[half + 1], refs[half + 2]
    size = other_ref.shape[-1]
    total = None
    for zz in range(half):
        panel = jnp.concatenate([panels[zz][...], other_ref[zz]], axis=0)
        part = jnp.dot(
            dense_ref[:, 2 * zz * size : (2 * zz + 2) * size], panel, preferred_element_type=F32
        )
        total = part if total is None else total + part
    for j in range(n_cols):
        out_ref = send_ref if j % 2 else keep_ref
        out_ref[j // 2] = total[j * size : (j + 1) * size]


def sum_refs(refs):
    terms = [ref[0].astype(F32) for ref in refs]
    while len(terms) > 1:
        terms = [sum(terms[i : i + 2][1:], terms[i]) for i in range(0, len(terms), 2)]
    return terms[0]


def forward_end_body(h_ref, rate_ref, *refs):
    *parts, out_ref = refs
    rate = rate_ref[...]
    value = (1.0 - rate) * sum_refs(parts) + rate * h_ref[...]
    out_ref[...] = value.astype(out_ref.dtype)


def middle_body(row_ref, column_ref, h_ref, *refs):
    d_own, d_got, y_own, y_got, d_ref, q_ref, p_ref = refs
    total = sum_refs((d_own, d_got))
    d_ref[...] = total
    q_ref[...] = ((1.0 - row_ref[...]) * total).astype(BF16)
    rate = column_ref[...]
    p_ref[...] = ((1.0 - rate) * sum_refs((y_own, y_got)) + rate * h_ref[...]).astype(BF16)


def adjoint_end_body(cot_ref, d_ref, row_ref, column_ref, *refs):
    *parts, out_ref = refs
    change = (row_ref[...] * d_ref[...] + sum_refs(parts)).T
    out_ref[...] = column_ref[...] * cot_ref[...] + change


ADD_COST = 800_000_000
FIRST_COST = 300_000_000


def send(value, axis, count, step):
    return lax.ppermute(value, axis, [(i, i ^ step) for i in range(count)])


def shards(h_start, cotangent, node_type, teleport, tile_values, tile_row, tile_col, tile_count):
    n_rows = lax.axis_size("rows")
    n_cols = lax.axis_size("cols")
    half = n_rows // 2
    size = tile_values.shape[-1]
    slots = tile_values.shape[2]
    features = h_start.shape[-1]
    types = node_type.reshape(1, size)
    hop_flops = 2 * n_rows * n_cols * size * size * features

    def shape(kind, *lead):
        return jax.ShapeDtypeStruct((*lead, size, features), kind)

    q0, p0, rate, column = call(
        start_body,
        [shape(BF16), shape(BF16), jax.ShapeDtypeStruct((1, size), F32), shape(F32)],
        [hbm()] * 4,
        in_hbm(cotangent, h_start, types, teleport),
        0,
        "start",
        [
            pltpu.VMEM(cotangent.shape, F32),
            pltpu.VMEM(h_start.shape, F32),
            pltpu.VMEM(types.shape, jnp.int32),
            pltpu.SMEM(teleport.shape, F32),
            pltpu.SemaphoreType.DMA((4,)),
        ],
    )
    (dense,) = call(
        dense_body,
        [jax.ShapeDtypeStruct((n_cols * size, n_rows * size), BF16)],
        [vmem()] + [hbm()] * 3 + [smem()],
        [q0, *in_hbm(tile_values, tile_row, tile_col), tile_count],
        0,
        "dense",
        [
            pltpu.SMEM(tile_row.shape, jnp.int32),
            pltpu.SMEM(tile_col.shape, jnp.int32),
            pltpu.SemaphoreType.DMA((2,)),
            pltpu.SemaphoreType.DMA((slots,)),
        ],
    )

    def pack(parts, after=()):
        outs = [shape(BF16, len(parts))]
        return call(pack_body, outs, [vmem()] * len(parts), parts, 0, "pack", after=after)[0]

    def fold(terms, kind, name, cost):
        count = terms[0].shape[0] // 2
        outs = [shape(F32, count), shape(kind, count)]
        return call(fold_body, outs, [vmem()] * len(terms), terms, cost, name)

    def adjoint_hop(part, kind, cost, after=(), through=()):
        packed = pack([part, send(part, "cols", n_cols, 2)], after)
        other = send(packed, "cols", n_cols, 1)
        *through, send_far, send_near, keep_far, keep_near = call(
            lambda *refs: adjoint_body(n_rows, n_cols, *refs),
            [shape(BF16)] * len(through)
            + [shape(kind, half // 2)] * 2
            + [shape(F32, half // 2)] * 2,
            [vmem()] * (3 + len(through)),
            [dense, packed, other, *through],
            hop_flops,
            "adjoint",
        )
        got = send(send_far, "rows", n_rows, 1)
        (far,) = call(
            add_body, [shape(kind, half // 2)], [vmem()] * 2, (keep_far, got), cost, "add_far"
        )
        order = [far]
        far = send(far, "rows", n_rows, 2)
        near = send(send_near, "rows", n_rows, 1)
        own, sent = fold([keep_near, near, far], kind, "add_near", cost)
        step = 4
        while own.shape[0] > 1:
            own, sent = fold([own, send(sent, "rows", n_rows, step)], kind, "add_rows", 0)
            step *= 2
        return (own, send(sent, "rows", n_rows, step)), through, order

    def forward_hop(part, kind, after=()):
        panels = [part] + [send(part, "rows", n_rows, 2 * s) for s in range(1, half)]
        other = send(pack(panels), "rows", n_rows, 1)
        keep, sent = call(
            lambda *refs: forward_body(half, n_cols, *refs),
            [shape(F32, n_cols // 2)] * 2,
            [vmem()] * (2 + half),
            [dense, *panels, other],
            hop_flops,
            "forward",
            after=after,
        )
        own, sent = fold([keep, send(sent, "cols", n_cols, 1)], kind, "add_cols", 0)
        return own, send(sent, "cols", n_cols, 2)

    back, (p0,), order = adjoint_hop(q0, F32, FIRST_COST, [dense], [p0])
    first = forward_hop(p0, F32, order)
    d1, q1, p1 = call(
        middle_body,
        [shape(F32), shape(BF16), shape(BF16)],
        [vmem()] * 7,
        (rate, column, h_start, *back, *first),
        0,
        "middle",
    )
    back_two, _, order = adjoint_hop(q1, BF16, ADD_COST)
    second = forward_hop(p1, BF16, order)
    (propagated,) = call(
        forward_end_body,
        [shape(F32)],
        [vmem()] * 4,
        (h_start, column, *second),
        0,
        "forward_end",
    )
    (input_grad,) = call(
        adjoint_end_body,
        [shape(F32)],
        [vmem()] * 6,
        (cotangent, d1, rate, column, *back_two),
        0,
        "adjoint_end",
    )
    return propagated, input_grad


def solution(mesh):
    placed = (
        P(("rows", "cols"), None),
        P(("rows", "cols"), None),
        P(("rows", "cols")),
        P(),
        P("rows", "cols", None, None, None),
        P("rows", "cols", None),
        P("rows", "cols", None),
        P("rows", "cols"),
    )
    return jax.shard_map(
        shards,
        mesh=mesh,
        in_specs=placed,
        out_specs=(P(("rows", "cols"), None), P(("rows", "cols"), None)),
        check_vma=False,
    )
```

```python
import jax
import jax.numpy as jnp
from jax import lax
from jax.experimental import pallas as pl
from jax.experimental.pallas import tpu as pltpu
from jax.sharding import PartitionSpec as P

VMEM_LIMIT = 32 * 1024 * 1024
BF16 = jnp.bfloat16
F32 = jnp.float32


def vmem():
    return pl.BlockSpec(memory_space=pltpu.VMEM)


def smem():
    return pl.BlockSpec(memory_space=pltpu.SMEM)


def hbm():
    return pl.BlockSpec(memory_space=pltpu.HBM)


def in_hbm(*arrays):
    return [pltpu.with_memory_space_constraint(a, pltpu.HBM) for a in arrays]


def call(body, outs, in_specs, args, flops, name, scratch=(), after=()):
    nbytes = sum(a.size * a.dtype.itemsize for a in (*args, *outs))
    count = len(args)

    def ordered(*refs):
        body(*refs[:count], *refs[count + len(after) :])

    return pl.pallas_call(
        ordered,
        out_shape=outs,
        in_specs=[*in_specs, *[pl.BlockSpec(memory_space=pl.ANY)] * len(after)],
        out_specs=[vmem()] * len(outs),
        scratch_shapes=list(scratch),
        compiler_params=pltpu.CompilerParams(vmem_limit_bytes=VMEM_LIMIT),
        cost_estimate=pl.CostEstimate(flops=flops, bytes_accessed=nbytes, transcendentals=0),
        name=name,
    )(*args, *after)


def fetch(pairs, sems):
    copies = [pltpu.make_async_copy(a, b, sems.at[i]) for i, (a, b) in enumerate(pairs)]
    for copy in copies:
        copy.start()
    for copy in copies:
        copy.wait()


def rate_row(types_ref, teleport_ref):
    types = types_ref[...]
    rate = jnp.zeros(types.shape, F32)
    for t in range(teleport_ref.shape[0]):
        rate = jnp.where(types == t, teleport_ref[t], rate)
    return rate


def rate_column(row, width):
    size = row.shape[1]
    return jnp.broadcast_to(row, (width, size)).T


def start_body(
    cot_hbm,
    h_hbm,
    types_hbm,
    teleport_hbm,
    q_ref,
    p_ref,
    row_ref,
    column_ref,
    cot_ref,
    h_ref,
    types_ref,
    teleport_ref,
    sems,
):
    fetch(
        [
            (types_hbm, types_ref),
            (teleport_hbm, teleport_ref),
            (cot_hbm, cot_ref),
            (h_hbm, h_ref),
        ],
        sems,
    )
    rate = rate_row(types_ref, teleport_ref)
    row_ref[...] = rate
    column_ref[...] = rate_column(rate, h_ref.shape[1])
    q_ref[...] = ((1.0 - rate) * cot_ref[...].T).astype(BF16)
    p_ref[...] = h_ref[...].astype(BF16)


def dense_body(
    tiles_hbm,
    row_hbm,
    col_hbm,
    count_ref,
    dense_ref,
    row_ref,
    col_ref,
    sems,
    slot_sems,
):
    size = tiles_hbm.shape[-1]
    ids = [
        pltpu.make_async_copy(row_hbm, row_ref, sems.at[0]),
        pltpu.make_async_copy(col_hbm, col_ref, sems.at[1]),
    ]
    for copy in ids:
        copy.start()
    me_row = lax.axis_index("rows")
    me_col = lax.axis_index("cols")
    dense_ref[...] = jnp.zeros_like(dense_ref)
    for copy in ids:
        copy.wait()
    count = count_ref[0, 0]

    def tile_copy(slot):
        row = row_ref[0, 0, slot] ^ me_col
        col = col_ref[0, 0, slot] ^ me_row
        return pltpu.make_async_copy(
            tiles_hbm.at[0, 0, slot],
            dense_ref.at[
                pl.ds(pl.multiple_of(row * size, size), size),
                pl.ds(pl.multiple_of(col * size, size), size),
            ],
            slot_sems.at[slot],
        )

    def begin(slot, carry):
        tile_copy(slot).start()
        return carry

    def end(slot, carry):
        tile_copy(slot).wait()
        return carry

    lax.fori_loop(0, count, begin, 0)
    lax.fori_loop(0, count, end, 0)


def adjoint_body(n_rows, n_cols, dense_ref, *refs):
    blocks, outs = refs[:n_cols], refs[n_cols:]
    keep_far, keep_near, send_far, send_near = outs
    half = n_rows // 2
    near = send_near.shape[0]
    size = blocks[0].shape[1]
    left = jnp.concatenate([b[...] for b in blocks], axis=1)
    for zz in reversed(range(half)):
        part = jnp.dot(
            left, dense_ref[:, 2 * zz * size : (2 * zz + 2) * size], preferred_element_type=F32
        )
        keep, send, at = (
            (keep_near, send_near, zz) if zz < near else (keep_far, send_far, zz - near)
        )
        keep[at] = part[:, :size]
        send[at] = part[:, size:].astype(send.dtype)


def add_body(keep_ref, got_ref, *outs):
    for at, out in enumerate(outs):
        out[...] = (keep_ref[at] + got_ref[at].astype(F32)).astype(out.dtype)


def pack_body(*refs):
    *parts, out_ref = refs
    for at, part in enumerate(parts):
        out_ref[at] = part[...]


def forward_body(half, n_cols, dense_ref, *refs):
    panels, outs = refs[:half], refs[half:]
    size = panels[0].shape[-1]
    total = None
    for zz in range(half):
        panel = jnp.concatenate([panels[zz][0], panels[zz][1]], axis=0)
        part = jnp.dot(
            dense_ref[:, 2 * zz * size : (2 * zz + 2) * size], panel, preferred_element_type=F32
        )
        total = part if total is None else total + part
    for j in range(n_cols):
        outs[j][...] = total[j * size : (j + 1) * size].astype(outs[j].dtype)


def sum_refs(refs):
    terms = [ref[...].astype(F32) for ref in refs]
    while len(terms) > 1:
        terms = [sum(terms[i : i + 2][1:], terms[i]) for i in range(0, len(terms), 2)]
    return terms[0]


def forward_end_body(h_ref, rate_ref, *refs):
    *parts, out_ref = refs
    rate = rate_ref[...]
    value = (1.0 - rate) * sum_refs(parts) + rate * h_ref[...]
    out_ref[...] = value.astype(out_ref.dtype)


def forward_middle_body(h_ref, rate_ref, *refs):
    *parts, p_ref = refs
    rate = rate_ref[...]
    p_ref[...] = ((1.0 - rate) * sum_refs(parts) + rate * h_ref[...]).astype(BF16)


def adjoint_middle_body(rate_ref, *refs):
    *parts, d_ref, q_ref = refs
    total = sum_refs(parts)
    d_ref[...] = total
    q_ref[...] = ((1.0 - rate_ref[...]) * total).astype(BF16)


def adjoint_end_body(cot_ref, d_ref, row_ref, column_ref, *refs):
    *parts, out_ref = refs
    change = (row_ref[...] * d_ref[...] + sum_refs(parts)).T
    out_ref[...] = column_ref[...] * cot_ref[...] + change


AFTER = {
    "dense": ("start",),
    "pair_one": ("adjoint_one",),
    "forward_one": ("far_one",),
    "far_two": ("pair_two",),
    "forward_two": ("far_two",),
    "pair_two": ("adjoint_two",),
}
COST = {"pair_one": 500, "adjoint_middle": 1000, "near_two": 500}


def send(value, axis, count, step):
    return lax.ppermute(value, axis, [(i, i ^ step) for i in range(count)])


def shards(h_start, cotangent, node_type, teleport, tile_values, tile_row, tile_col, tile_count):
    n_rows = lax.axis_size("rows")
    n_cols = lax.axis_size("cols")
    half = n_rows // 2
    near = half // 2
    size = tile_values.shape[-1]
    slots = tile_values.shape[2]
    features = h_start.shape[-1]
    types = node_type.reshape(1, size)
    hop_flops = 2 * n_rows * n_cols * size * size * features

    def shape(kind, *lead):
        return jax.ShapeDtypeStruct((*lead, size, features), kind)

    made = {}
    makers = {}

    def get(name):
        if name not in made:
            made[name] = makers[name]()
        return made[name]

    def run(name, body, outs, args, in_specs=None, scratch=(), flops=0):
        return call(
            body,
            outs,
            in_specs or [vmem()] * len(args),
            args,
            COST.get(name, 0) * 1_000_000 or flops,
            name,
            scratch,
            [get(other)[0] for other in AFTER.get(name, ())],
        )

    def start():
        return run(
            "start",
            start_body,
            [shape(BF16), shape(BF16), jax.ShapeDtypeStruct((1, size), F32), shape(F32)],
            in_hbm(cotangent, h_start, types, teleport),
            [hbm()] * 4,
            [
                pltpu.VMEM(cotangent.shape, F32),
                pltpu.VMEM(h_start.shape, F32),
                pltpu.VMEM(types.shape, jnp.int32),
                pltpu.SMEM(teleport.shape, F32),
                pltpu.SemaphoreType.DMA((4,)),
            ],
        )

    def dense():
        return run(
            "dense",
            dense_body,
            [jax.ShapeDtypeStruct((n_cols * size, n_rows * size), BF16)],
            [*in_hbm(tile_values, tile_row, tile_col), tile_count],
            [hbm()] * 3 + [smem()],
            [
                pltpu.SMEM(tile_row.shape, jnp.int32),
                pltpu.SMEM(tile_col.shape, jnp.int32),
                pltpu.SemaphoreType.DMA((2,)),
                pltpu.SemaphoreType.DMA((slots,)),
            ],
        )

    def spread(part, axis, count, step):
        return [part] + [send(part, axis, count, step * s) for s in range(1, count // step)]

    def swap_cols(parts):
        return [parts[0]] + [send(parts[s], "cols", n_cols, s) for s in range(1, n_cols)]

    def adjoint(name, part, kind):
        return run(
            name,
            lambda *refs: adjoint_body(n_rows, n_cols, *refs),
            [shape(F32, half - near), shape(F32, near), shape(kind, half - near), shape(kind, near)],
            [get("dense")[0], *spread(part, "cols", n_cols, 1)],
            flops=hop_flops,
        )

    def pair(name, part):
        return run(name, pack_body, [shape(BF16, 2)], [part, send(part, "rows", n_rows, 1)])

    def forward(name, both, kind):
        return run(
            name,
            lambda *refs: forward_body(half, n_cols, *refs),
            [shape(kind)] * n_cols,
            [get("dense")[0], *spread(both, "rows", n_rows, 2)],
            flops=hop_flops,
        )

    def sums(name, kept, sent, kinds):
        got = send(sent, "rows", n_rows, 1)
        return run(name, add_body, [shape(kind) for kind in kinds], [kept, got])

    def row_parts(far, close):
        parts = [send(far[s - near], "rows", n_rows, 2 * s) for s in range(near, half)]
        return parts + [close[0]] + [send(close[s], "rows", n_rows, 2 * s) for s in range(1, near)]

    far_kinds = lambda kind: [kind] * (half - near)
    near_kinds = lambda kind: [F32] + [kind] * (near - 1)
    makers.update(
        start=start,
        dense=dense,
        adjoint_one=lambda: adjoint("adjoint_one", get("start")[0], F32),
        pair_one=lambda: pair("pair_one", get("start")[1]),
        far_one=lambda: sums(
            "far_one", get("adjoint_one")[0], get("adjoint_one")[2], far_kinds(F32)
        ),
        near_one=lambda: sums(
            "near_one", get("adjoint_one")[1], get("adjoint_one")[3], near_kinds(F32)
        ),
        forward_one=lambda: forward("forward_one", get("pair_one")[0], F32),
        adjoint_middle=lambda: run(
            "adjoint_middle",
            adjoint_middle_body,
            [shape(F32), shape(BF16)],
            [get("start")[2], *row_parts(get("far_one"), get("near_one"))],
        ),
        forward_middle=lambda: run(
            "forward_middle",
            forward_middle_body,
            [shape(BF16)],
            [h_start, get("start")[3], *swap_cols(get("forward_one"))],
        ),
        adjoint_two=lambda: adjoint("adjoint_two", get("adjoint_middle")[1], BF16),
        pair_two=lambda: pair("pair_two", get("forward_middle")[0]),
        far_two=lambda: sums(
            "far_two", get("adjoint_two")[0], get("adjoint_two")[2], far_kinds(BF16)
        ),
        near_two=lambda: sums(
            "near_two", get("adjoint_two")[1], get("adjoint_two")[3], near_kinds(BF16)
        ),
        forward_two=lambda: forward("forward_two", get("pair_two")[0], BF16),
        forward_end=lambda: run(
            "forward_end",
            forward_end_body,
            [shape(F32)],
            [h_start, get("start")[3], *swap_cols(get("forward_two"))],
        ),
        adjoint_end=lambda: run(
            "adjoint_end",
            adjoint_end_body,
            [shape(F32)],
            [
                cotangent,
                get("adjoint_middle")[0],
                get("start")[2],
                get("start")[3],
                *row_parts(get("far_two"), get("near_two")),
            ],
        ),
    )
    return get("forward_end")[0], get("adjoint_end")[0]


def solution(mesh):
    placed = (
        P(("rows", "cols"), None),
        P(("rows", "cols"), None),
        P(("rows", "cols")),
        P(),
        P("rows", "cols", None, None, None),
        P("rows", "cols", None),
        P("rows", "cols", None),
        P("rows", "cols"),
    )
    return jax.shard_map(
        shards,
        mesh=mesh,
        in_specs=placed,
        out_specs=(P(("rows", "cols"), None), P(("rows", "cols"), None)),
        check_vma=False,
    )
```

```python
import jax
import jax.numpy as jnp
from jax import lax
from jax.experimental import pallas as pl
from jax.experimental.pallas import tpu as pltpu
from jax.sharding import PartitionSpec as P

VMEM_LIMIT = 32 * 1024 * 1024
BF16 = jnp.bfloat16
F32 = jnp.float32


def vmem():
    return pl.BlockSpec(memory_space=pltpu.VMEM)


def smem():
    return pl.BlockSpec(memory_space=pltpu.SMEM)


def hbm():
    return pl.BlockSpec(memory_space=pltpu.HBM)


def in_hbm(*arrays):
    return [pltpu.with_memory_space_constraint(a, pltpu.HBM) for a in arrays]


def call(body, outs, in_specs, args, flops, name, scratch=(), after=()):
    nbytes = sum(a.size * a.dtype.itemsize for a in (*args, *outs))
    count = len(args)

    def ordered(*refs):
        body(*refs[:count], *refs[count + len(after) :])

    return pl.pallas_call(
        ordered,
        out_shape=outs,
        in_specs=[*in_specs, *[pl.BlockSpec(memory_space=pl.ANY)] * len(after)],
        out_specs=[vmem()] * len(outs),
        scratch_shapes=list(scratch),
        compiler_params=pltpu.CompilerParams(vmem_limit_bytes=VMEM_LIMIT),
        cost_estimate=pl.CostEstimate(flops=flops, bytes_accessed=nbytes, transcendentals=0),
        name=name,
    )(*args, *after)


def fetch(pairs, sems):
    copies = [pltpu.make_async_copy(a, b, sems.at[i]) for i, (a, b) in enumerate(pairs)]
    for copy in copies:
        copy.start()
    for copy in copies:
        copy.wait()


def rate_row(types_ref, teleport_ref):
    types = types_ref[...]
    rate = jnp.zeros(types.shape, F32)
    for t in range(teleport_ref.shape[0]):
        rate = jnp.where(types == t, teleport_ref[t], rate)
    return rate


def rate_column(row, width):
    size = row.shape[1]
    return jnp.broadcast_to(row, (width, size)).T


def start_body(
    cot_hbm,
    h_hbm,
    types_hbm,
    teleport_hbm,
    q_ref,
    p_ref,
    row_ref,
    column_ref,
    cot_ref,
    h_ref,
    types_ref,
    teleport_ref,
    sems,
):
    fetch(
        [
            (types_hbm, types_ref),
            (teleport_hbm, teleport_ref),
            (cot_hbm, cot_ref),
            (h_hbm, h_ref),
        ],
        sems,
    )
    rate = rate_row(types_ref, teleport_ref)
    row_ref[...] = rate
    column_ref[...] = rate_column(rate, h_ref.shape[1])
    q_ref[...] = ((1.0 - rate) * cot_ref[...].T).astype(BF16)
    p_ref[...] = h_ref[...].astype(BF16)


def dense_body(
    tiles_hbm,
    row_hbm,
    col_hbm,
    count_ref,
    dense_ref,
    row_ref,
    col_ref,
    sems,
    slot_sems,
):
    size = tiles_hbm.shape[-1]
    ids = [
        pltpu.make_async_copy(row_hbm, row_ref, sems.at[0]),
        pltpu.make_async_copy(col_hbm, col_ref, sems.at[1]),
    ]
    for copy in ids:
        copy.start()
    me_row = lax.axis_index("rows")
    me_col = lax.axis_index("cols")
    dense_ref[...] = jnp.zeros_like(dense_ref)
    for copy in ids:
        copy.wait()
    count = count_ref[0, 0]

    def tile_copy(slot):
        row = row_ref[0, 0, slot] ^ me_col
        col = col_ref[0, 0, slot] ^ me_row
        return pltpu.make_async_copy(
            tiles_hbm.at[0, 0, slot],
            dense_ref.at[
                pl.ds(pl.multiple_of(row * size, size), size),
                pl.ds(pl.multiple_of(col * size, size), size),
            ],
            slot_sems.at[slot],
        )

    def begin(slot, carry):
        tile_copy(slot).start()
        return carry

    def end(slot, carry):
        tile_copy(slot).wait()
        return carry

    lax.fori_loop(0, count, begin, 0)
    lax.fori_loop(0, count, end, 0)


def adjoint_body(n_rows, n_cols, dense_ref, *refs):
    blocks, outs = refs[:n_cols], refs[n_cols:]
    keep_far, keep_near, send_far, send_near = outs
    half = n_rows // 2
    near = send_near.shape[0]
    size = blocks[0].shape[1]
    left = jnp.concatenate([b[...] for b in blocks], axis=1)
    for zz in reversed(range(half)):
        part = jnp.dot(
            left, dense_ref[:, 2 * zz * size : (2 * zz + 2) * size], preferred_element_type=F32
        )
        keep, send, at = (
            (keep_near, send_near, zz) if zz < near else (keep_far, send_far, zz - near)
        )
        keep[at] = part[:, :size]
        send[at] = part[:, size:].astype(send.dtype)


def add_body(keep_ref, got_ref, *outs):
    for at, out in enumerate(outs):
        out[...] = (keep_ref[at] + got_ref[at].astype(F32)).astype(out.dtype)


def pack_body(*refs):
    *parts, out_ref = refs
    for at, part in enumerate(parts):
        out_ref[at] = part[...]


def forward_body(half, n_cols, dense_ref, *refs):
    panels, outs = refs[:half], refs[half:]
    size = panels[0].shape[-1]
    total = None
    for zz in range(half):
        panel = jnp.concatenate([panels[zz][0], panels[zz][1]], axis=0)
        part = jnp.dot(
            dense_ref[:, 2 * zz * size : (2 * zz + 2) * size], panel, preferred_element_type=F32
        )
        total = part if total is None else total + part
    for j in range(n_cols):
        outs[j][...] = total[j * size : (j + 1) * size].astype(outs[j].dtype)


def sum_refs(refs):
    terms = [ref[...].astype(F32) for ref in refs]
    while len(terms) > 1:
        terms = [sum(terms[i : i + 2][1:], terms[i]) for i in range(0, len(terms), 2)]
    return terms[0]


def forward_end_body(h_ref, rate_ref, *refs):
    *parts, out_ref = refs
    rate = rate_ref[...]
    value = (1.0 - rate) * sum_refs(parts) + rate * h_ref[...]
    out_ref[...] = value.astype(out_ref.dtype)


def forward_middle_body(h_ref, rate_ref, *refs):
    *parts, p_ref = refs
    rate = rate_ref[...]
    p_ref[...] = ((1.0 - rate) * sum_refs(parts) + rate * h_ref[...]).astype(BF16)


def adjoint_middle_body(rate_ref, *refs):
    *parts, d_ref, q_ref = refs
    total = sum_refs(parts)
    d_ref[...] = total
    q_ref[...] = ((1.0 - rate_ref[...]) * total).astype(BF16)


def adjoint_end_body(cot_ref, d_ref, row_ref, column_ref, *refs):
    *parts, out_ref = refs
    change = (row_ref[...] * d_ref[...] + sum_refs(parts)).T
    out_ref[...] = column_ref[...] * cot_ref[...] + change


AFTER = {
    "dense": ("start",),
    "pair_one_late": ("adjoint_one",),
    "forward_one": ("far_one", "near_one"),
    "forward_two": ("far_two", "near_two"),
    "pair_two_late": ("adjoint_two",),
    "forward_end": ("adjoint_end",),
    "adjoint_one": ("pair_one_early",),
    "pair_two_early": ("adjoint_middle",),
    "forward_middle": ("adjoint_middle",),
}
COST = {
    "pair_one_late": 1000,
    "adjoint_middle": 1000,
    "near_two": 500,
    "pair_two_early": 500,
    "far_two": 1000,
    "far_one": 500,
    "forward_end": 3000,
    "pair_two_late": 1000,
    "pair_one_early": 3000,
}


def send(value, axis, count, step):
    return lax.ppermute(value, axis, [(i, i ^ step) for i in range(count)])


def shards(h_start, cotangent, node_type, teleport, tile_values, tile_row, tile_col, tile_count):
    n_rows = lax.axis_size("rows")
    n_cols = lax.axis_size("cols")
    half = n_rows // 2
    near = half // 2
    size = tile_values.shape[-1]
    slots = tile_values.shape[2]
    features = h_start.shape[-1]
    types = node_type.reshape(1, size)
    hop_flops = 2 * n_rows * n_cols * size * size * features

    def shape(kind, *lead):
        return jax.ShapeDtypeStruct((*lead, size, features), kind)

    made = {}
    makers = {}

    def get(name):
        if name not in made:
            made[name] = makers[name]()
        return made[name]

    def run(name, body, outs, args, in_specs=None, scratch=(), flops=0):
        return call(
            body,
            outs,
            in_specs or [vmem()] * len(args),
            args,
            COST.get(name, 0) * 1_000_000 or flops,
            name,
            scratch,
            [get(other)[0] for other in AFTER.get(name, ())],
        )

    def start():
        return run(
            "start",
            start_body,
            [shape(BF16), shape(BF16), jax.ShapeDtypeStruct((1, size), F32), shape(F32)],
            in_hbm(cotangent, h_start, types, teleport),
            [hbm()] * 4,
            [
                pltpu.VMEM(cotangent.shape, F32),
                pltpu.VMEM(h_start.shape, F32),
                pltpu.VMEM(types.shape, jnp.int32),
                pltpu.SMEM(teleport.shape, F32),
                pltpu.SemaphoreType.DMA((4,)),
            ],
        )

    def dense():
        return run(
            "dense",
            dense_body,
            [jax.ShapeDtypeStruct((n_cols * size, n_rows * size), BF16)],
            [*in_hbm(tile_values, tile_row, tile_col), tile_count],
            [hbm()] * 3 + [smem()],
            [
                pltpu.SMEM(tile_row.shape, jnp.int32),
                pltpu.SMEM(tile_col.shape, jnp.int32),
                pltpu.SemaphoreType.DMA((2,)),
                pltpu.SemaphoreType.DMA((slots,)),
            ],
        )

    def spread(part, axis, count, step):
        return [part] + [send(part, axis, count, step * s) for s in range(1, count // step)]

    def swap_cols(parts):
        return [parts[0]] + [send(parts[s], "cols", n_cols, s) for s in range(1, n_cols)]

    def adjoint(name, part, kind):
        return run(
            name,
            lambda *refs: adjoint_body(n_rows, n_cols, *refs),
            [shape(F32, half - near), shape(F32, near), shape(kind, half - near), shape(kind, near)],
            [get("dense")[0], *spread(part, "cols", n_cols, 1)],
            flops=hop_flops,
        )

    def pair(name, part, other):
        return run(name, pack_body, [shape(BF16, 2)], [part, other])

    def forward(name, early, late, kind):
        panels = [early] + [
            send(early if s == half - 1 else late, "rows", n_rows, 2 * s) for s in range(1, half)
        ]
        return run(
            name,
            lambda *refs: forward_body(half, n_cols, *refs),
            [shape(kind)] * n_cols,
            [get("dense")[0], *panels],
            flops=hop_flops,
        )

    def sums(name, kept, sent, kinds):
        got = send(sent, "rows", n_rows, 1)
        return run(name, add_body, [shape(kind) for kind in kinds], [kept, got])

    def row_parts(far, close):
        parts = [send(far[s - near], "rows", n_rows, 2 * s) for s in range(near, half)]
        return parts + [close[0]] + [send(close[s], "rows", n_rows, 2 * s) for s in range(1, near)]

    far_kinds = lambda kind: [kind] * (half - near)
    near_kinds = lambda kind: [F32] + [kind] * (near - 1)
    makers.update(
        start=start,
        dense=dense,
        adjoint_one=lambda: adjoint("adjoint_one", get("start")[0], F32),
        other_one=lambda: send(get("start")[1], "rows", n_rows, 1),
        other_two=lambda: send(get("forward_middle")[0], "rows", n_rows, 1),
        pair_one_early=lambda: pair("pair_one_early", get("start")[1], get("other_one")),
        pair_one_late=lambda: pair("pair_one_late", get("start")[1], get("other_one")),
        far_one=lambda: sums(
            "far_one", get("adjoint_one")[0], get("adjoint_one")[2], far_kinds(F32)
        ),
        near_one=lambda: sums(
            "near_one", get("adjoint_one")[1], get("adjoint_one")[3], near_kinds(F32)
        ),
        forward_one=lambda: forward(
            "forward_one", get("pair_one_early")[0], get("pair_one_late")[0], F32
        ),
        adjoint_middle=lambda: run(
            "adjoint_middle",
            adjoint_middle_body,
            [shape(F32), shape(BF16)],
            [get("start")[2], *row_parts(get("far_one"), get("near_one"))],
        ),
        forward_middle=lambda: run(
            "forward_middle",
            forward_middle_body,
            [shape(BF16)],
            [h_start, get("start")[3], *swap_cols(get("forward_one"))],
        ),
        adjoint_two=lambda: adjoint("adjoint_two", get("adjoint_middle")[1], BF16),
        pair_two_early=lambda: pair("pair_two_early", get("forward_middle")[0], get("other_two")),
        pair_two_late=lambda: pair("pair_two_late", get("forward_middle")[0], get("other_two")),
        far_two=lambda: sums(
            "far_two", get("adjoint_two")[0], get("adjoint_two")[2], far_kinds(BF16)
        ),
        near_two=lambda: sums(
            "near_two", get("adjoint_two")[1], get("adjoint_two")[3], near_kinds(BF16)
        ),
        forward_two=lambda: forward(
            "forward_two", get("pair_two_early")[0], get("pair_two_late")[0], BF16
        ),
        forward_end=lambda: run(
            "forward_end",
            forward_end_body,
            [shape(F32)],
            [h_start, get("start")[3], *swap_cols(get("forward_two"))],
        ),
        adjoint_end=lambda: run(
            "adjoint_end",
            adjoint_end_body,
            [shape(F32)],
            [
                cotangent,
                get("adjoint_middle")[0],
                get("start")[2],
                get("start")[3],
                *row_parts(get("far_two"), get("near_two")),
            ],
        ),
    )
    return get("forward_end")[0], get("adjoint_end")[0]


def solution(mesh):
    placed = (
        P(("rows", "cols"), None),
        P(("rows", "cols"), None),
        P(("rows", "cols")),
        P(),
        P("rows", "cols", None, None, None),
        P("rows", "cols", None),
        P("rows", "cols", None),
        P("rows", "cols"),
    )
    return jax.shard_map(
        shards,
        mesh=mesh,
        in_specs=placed,
        out_specs=(P(("rows", "cols"), None), P(("rows", "cols"), None)),
        check_vma=False,
    )
```

```python
import jax
import jax.numpy as jnp
from jax import lax
from jax.experimental import pallas as pl
from jax.experimental.pallas import tpu as pltpu
from jax.sharding import PartitionSpec as P

VMEM_LIMIT = 32 * 1024 * 1024
BF16 = jnp.bfloat16
F32 = jnp.float32


def vmem():
    return pl.BlockSpec(memory_space=pltpu.VMEM)


def smem():
    return pl.BlockSpec(memory_space=pltpu.SMEM)


def hbm():
    return pl.BlockSpec(memory_space=pltpu.HBM)


def in_hbm(*arrays):
    return [pltpu.with_memory_space_constraint(a, pltpu.HBM) for a in arrays]


def call(body, outs, in_specs, args, flops, name, scratch=(), after=()):
    nbytes = sum(a.size * a.dtype.itemsize for a in (*args, *outs))
    count = len(args)

    def ordered(*refs):
        body(*refs[:count], *refs[count + len(after) :])

    return pl.pallas_call(
        ordered,
        out_shape=outs,
        in_specs=[*in_specs, *[pl.BlockSpec(memory_space=pl.ANY)] * len(after)],
        out_specs=[vmem()] * len(outs),
        scratch_shapes=list(scratch),
        compiler_params=pltpu.CompilerParams(vmem_limit_bytes=VMEM_LIMIT),
        cost_estimate=pl.CostEstimate(flops=flops, bytes_accessed=nbytes, transcendentals=0),
        name=name,
    )(*args, *after)


def rate_row(types_ref, teleport_ref):
    types = types_ref[...]
    rate = jnp.zeros(types.shape, F32)
    for t in range(teleport_ref.shape[0]):
        rate = jnp.where(types == t, teleport_ref[t], rate)
    return rate


def rate_column(row, width):
    size = row.shape[1]
    return jnp.broadcast_to(row, (width, size)).T


def start_body(
    types_hbm,
    teleport_hbm,
    cot_hbm,
    h_hbm,
    tiles_hbm,
    q_ref,
    p_ref,
    row_ref,
    keep_ref,
    h_base_ref,
    cot_base_ref,
    tiles_ref,
    types_ref,
    teleport_ref,
    cot_ref,
    h_ref,
    sems,
):
    sources = (types_hbm, teleport_hbm, cot_hbm, h_hbm, tiles_hbm)
    targets = (types_ref, teleport_ref, cot_ref, h_ref, tiles_ref)
    copies = [
        pltpu.make_async_copy(a, b, sems.at[i]) for i, (a, b) in enumerate(zip(sources, targets))
    ]
    for copy in copies:
        copy.start()
    for copy in copies[:4]:
        copy.wait()
    rate = rate_row(types_ref, teleport_ref)
    column = rate_column(rate, h_ref.shape[1])
    row_ref[...] = rate
    keep_ref[...] = 1.0 - column
    q_ref[...] = ((1.0 - rate) * cot_ref[...].T).astype(BF16)
    p_ref[...] = h_ref[...].astype(BF16)
    h_base_ref[...] = column * h_ref[...]
    cot_base_ref[...] = column * cot_ref[...]
    copies[4].wait()


def dense_body(tiles_ref, row_ref, col_ref, count_ref, dense_ref):
    size = tiles_ref.shape[-1]
    me_row = lax.axis_index("rows")
    me_col = lax.axis_index("cols")
    dense_ref[...] = jnp.zeros_like(dense_ref)

    def place(slot, carry):
        row = row_ref[0, 0, slot] ^ me_col
        col = col_ref[0, 0, slot] ^ me_row
        dense_ref[
            pl.ds(pl.multiple_of(row * size, size), size),
            pl.ds(pl.multiple_of(col * size, size), size),
        ] = tiles_ref[0, 0, slot]
        return carry

    lax.fori_loop(0, count_ref[0, 0], place, 0)


def adjoint_body(n_rows, n_cols, dense_ref, *refs):
    blocks, outs = refs[:n_cols], refs[n_cols:]
    keep_far, keep_near, send_far, send_near = outs
    half = n_rows // 2
    near = send_near.shape[0]
    size = blocks[0].shape[1]
    left = jnp.concatenate([b[...] for b in blocks], axis=1)
    for zz in reversed(range(half)):
        part = jnp.dot(
            left, dense_ref[:, 2 * zz * size : (2 * zz + 2) * size], preferred_element_type=F32
        )
        keep, send, at = (
            (keep_near, send_near, zz) if zz < near else (keep_far, send_far, zz - near)
        )
        keep[at] = part[:, :size]
        send[at] = part[:, size:].astype(send.dtype)


def add_body(keep_ref, got_ref, *outs):
    for at, out in enumerate(outs):
        out[...] = (keep_ref[at] + got_ref[at].astype(F32)).astype(out.dtype)


def pack_body(*refs):
    *parts, out_ref = refs
    for at, part in enumerate(parts):
        out_ref[at] = part[...]


def forward_body(half, n_cols, dense_ref, *refs):
    panels, outs = refs[:half], refs[half:]
    size = panels[0].shape[-1]
    total = None
    for zz in range(half):
        panel = jnp.concatenate([panels[zz][0], panels[zz][1]], axis=0)
        part = jnp.dot(
            dense_ref[:, 2 * zz * size : (2 * zz + 2) * size], panel, preferred_element_type=F32
        )
        total = part if total is None else total + part
    for j in range(n_cols):
        outs[j][...] = total[j * size : (j + 1) * size].astype(outs[j].dtype)


def sum_refs(refs):
    terms = [ref[...].astype(F32) for ref in refs]
    while len(terms) > 1:
        terms = [sum(terms[i : i + 2][1:], terms[i]) for i in range(0, len(terms), 2)]
    return terms[0]


def forward_end_body(base_ref, keep_ref, *refs):
    *parts, out_ref = refs
    out_ref[...] = (keep_ref[...] * sum_refs(parts) + base_ref[...]).astype(out_ref.dtype)


def adjoint_middle_body(rate_ref, *refs):
    *parts, d_ref, q_ref = refs
    total = sum_refs(parts)
    d_ref[...] = total
    q_ref[...] = ((1.0 - rate_ref[...]) * total).astype(BF16)


def adjoint_end_body(base_ref, d_ref, rate_ref, *refs):
    *parts, out_ref = refs
    out_ref[...] = base_ref[...] + (rate_ref[...] * d_ref[...] + sum_refs(parts)).T


AFTER = {
    "pair_one_late": ("adjoint_one",),
    "forward_two": ("far_two", "near_two"),
    "forward_end": ("adjoint_end",),
    "pair_two_early": ("adjoint_middle",),
    "forward_middle": ("adjoint_middle",),
    "pair_one_early": ("dense",),
    "adjoint_middle": ("forward_one",),
}
COST = {
    "pair_one_late": 1000,
    "adjoint_middle": 1000,
    "near_two": 200,
    "pair_two_early": 200,
    "far_two": 1000,
    "far_one": 500,
    "forward_end": 1000,
    "pair_two_late": 1000,
    "pair_one_early": 3000,
    "forward_middle": 3000,
    "adjoint_end": 3000,
}


def send(value, axis, count, step):
    return lax.ppermute(value, axis, [(i, i ^ step) for i in range(count)])


def shards(h_start, cotangent, node_type, teleport, tile_values, tile_row, tile_col, tile_count):
    n_rows = lax.axis_size("rows")
    n_cols = lax.axis_size("cols")
    half = n_rows // 2
    near = half // 2
    size = tile_values.shape[-1]
    features = h_start.shape[-1]
    types = node_type.reshape(1, size)
    hop_flops = 2 * n_rows * n_cols * size * size * features

    def shape(kind, *lead):
        return jax.ShapeDtypeStruct((*lead, size, features), kind)

    made = {}
    makers = {}

    def get(name):
        if name not in made:
            made[name] = makers[name]()
        return made[name]

    def run(name, body, outs, args, in_specs=None, scratch=(), flops=0):
        return call(
            body,
            outs,
            in_specs or [vmem()] * len(args),
            args,
            COST.get(name, 0) * 1_000_000 or flops,
            name,
            scratch,
            [get(other)[0] for other in AFTER.get(name, ())],
        )

    def start():
        return run(
            "start",
            start_body,
            [
                shape(BF16),
                shape(BF16),
                jax.ShapeDtypeStruct((1, size), F32),
                shape(F32),
                shape(F32),
                shape(F32),
                jax.ShapeDtypeStruct(tile_values.shape, BF16),
            ],
            in_hbm(types, teleport, cotangent, h_start, tile_values),
            [hbm()] * 5,
            [
                pltpu.VMEM(types.shape, jnp.int32),
                pltpu.SMEM(teleport.shape, F32),
                pltpu.VMEM(cotangent.shape, F32),
                pltpu.VMEM(h_start.shape, F32),
                pltpu.SemaphoreType.DMA((5,)),
            ],
        )

    def dense():
        return run(
            "dense",
            dense_body,
            [jax.ShapeDtypeStruct((n_cols * size, n_rows * size), BF16)],
            [get("start")[6], *in_hbm(tile_row, tile_col), tile_count],
            [vmem()] + [smem()] * 3,
        )

    def spread(part, axis, count, step):
        return [part] + [send(part, axis, count, step * s) for s in range(1, count // step)]

    def swap_cols(parts):
        return [parts[0]] + [send(parts[s], "cols", n_cols, s) for s in range(1, n_cols)]

    def adjoint(name, part, kind):
        return run(
            name,
            lambda *refs: adjoint_body(n_rows, n_cols, *refs),
            [shape(F32, half - near), shape(F32, near), shape(kind, half - near), shape(kind, near)],
            [get("dense")[0], *spread(part, "cols", n_cols, 1)],
            flops=hop_flops,
        )

    def pair(name, part, other):
        return run(name, pack_body, [shape(BF16, 2)], [part, other])

    def forward(name, early, late, kind):
        panels = [early] + [
            send(early if s == half - 1 else late, "rows", n_rows, 2 * s) for s in range(1, half)
        ]
        return run(
            name,
            lambda *refs: forward_body(half, n_cols, *refs),
            [shape(kind)] * n_cols,
            [get("dense")[0], *panels],
            flops=hop_flops,
        )

    def sums(name, kept, sent, kinds):
        got = send(sent, "rows", n_rows, 1)
        return run(name, add_body, [shape(kind) for kind in kinds], [kept, got])

    def row_parts(far, close):
        parts = [send(far[s - near], "rows", n_rows, 2 * s) for s in range(near, half)]
        return parts + [close[0]] + [send(close[s], "rows", n_rows, 2 * s) for s in range(1, near)]

    far_kinds = lambda kind: [kind] * (half - near)
    near_kinds = lambda kind: [F32] + [kind] * (near - 1)
    makers.update(
        start=start,
        dense=dense,
        adjoint_one=lambda: adjoint("adjoint_one", get("start")[0], F32),
        other_one=lambda: send(get("start")[1], "rows", n_rows, 1),
        other_two=lambda: send(get("forward_middle")[0], "rows", n_rows, 1),
        pair_one_early=lambda: pair("pair_one_early", get("start")[1], get("other_one")),
        pair_one_late=lambda: pair("pair_one_late", get("start")[1], get("other_one")),
        far_one=lambda: sums(
            "far_one", get("adjoint_one")[0], get("adjoint_one")[2], far_kinds(F32)
        ),
        near_one=lambda: sums(
            "near_one", get("adjoint_one")[1], get("adjoint_one")[3], near_kinds(F32)
        ),
        forward_one=lambda: forward(
            "forward_one", get("pair_one_early")[0], get("pair_one_late")[0], F32
        ),
        adjoint_middle=lambda: run(
            "adjoint_middle",
            adjoint_middle_body,
            [shape(F32), shape(BF16)],
            [get("start")[2], *row_parts(get("far_one"), get("near_one"))],
        ),
        forward_middle=lambda: run(
            "forward_middle",
            forward_end_body,
            [shape(BF16)],
            [get("start")[4], get("start")[3], *swap_cols(get("forward_one"))],
        ),
        adjoint_two=lambda: adjoint("adjoint_two", get("adjoint_middle")[1], BF16),
        pair_two_early=lambda: pair("pair_two_early", get("forward_middle")[0], get("other_two")),
        pair_two_late=lambda: pair("pair_two_late", get("forward_middle")[0], get("other_two")),
        far_two=lambda: sums(
            "far_two", get("adjoint_two")[0], get("adjoint_two")[2], far_kinds(BF16)
        ),
        near_two=lambda: sums(
            "near_two", get("adjoint_two")[1], get("adjoint_two")[3], near_kinds(BF16)
        ),
        forward_two=lambda: forward(
            "forward_two", get("pair_two_early")[0], get("pair_two_late")[0], BF16
        ),
        forward_end=lambda: run(
            "forward_end",
            forward_end_body,
            [shape(F32)],
            [get("start")[4], get("start")[3], *swap_cols(get("forward_two"))],
        ),
        adjoint_end=lambda: run(
            "adjoint_end",
            adjoint_end_body,
            [shape(F32)],
            [
                get("start")[5],
                get("adjoint_middle")[0],
                get("start")[2],
                *row_parts(get("far_two"), get("near_two")),
            ],
        ),
    )
    return get("forward_end")[0], get("adjoint_end")[0]


def solution(mesh):
    placed = (
        P(("rows", "cols"), None),
        P(("rows", "cols"), None),
        P(("rows", "cols")),
        P(),
        P("rows", "cols", None, None, None),
        P("rows", "cols", None),
        P("rows", "cols", None),
        P("rows", "cols"),
    )
    return jax.shard_map(
        shards,
        mesh=mesh,
        in_specs=placed,
        out_specs=(P(("rows", "cols"), None), P(("rows", "cols"), None)),
        check_vma=False,
    )
```

```python
import jax
import jax.numpy as jnp
from jax import lax
from jax.experimental import pallas as pl
from jax.experimental.pallas import tpu as pltpu
from jax.sharding import PartitionSpec as P

VMEM_LIMIT = 32 * 1024 * 1024
BF16 = jnp.bfloat16
F32 = jnp.float32


def vmem():
    return pl.BlockSpec(memory_space=pltpu.VMEM)


def smem():
    return pl.BlockSpec(memory_space=pltpu.SMEM)


def hbm():
    return pl.BlockSpec(memory_space=pltpu.HBM)


def in_hbm(*arrays):
    return [pltpu.with_memory_space_constraint(a, pltpu.HBM) for a in arrays]


def call(body, outs, in_specs, args, flops, name, scratch=(), after=()):
    nbytes = sum(a.size * a.dtype.itemsize for a in (*args, *outs))
    count = len(args)

    def ordered(*refs):
        body(*refs[:count], *refs[count + len(after) :])

    return pl.pallas_call(
        ordered,
        out_shape=outs,
        in_specs=[*in_specs, *[pl.BlockSpec(memory_space=pl.ANY)] * len(after)],
        out_specs=[vmem()] * len(outs),
        scratch_shapes=list(scratch),
        compiler_params=pltpu.CompilerParams(vmem_limit_bytes=VMEM_LIMIT),
        cost_estimate=pl.CostEstimate(flops=flops, bytes_accessed=nbytes, transcendentals=0),
        name=name,
    )(*args, *after)


def rate_row(types_ref, teleport_ref):
    types = types_ref[...]
    rate = jnp.zeros(types.shape, F32)
    for t in range(teleport_ref.shape[0]):
        rate = jnp.where(types == t, teleport_ref[t], rate)
    return rate


def rate_column(row, width):
    size = row.shape[1]
    return jnp.broadcast_to(row, (width, size)).T


def start_body(
    types_hbm,
    teleport_hbm,
    cot_hbm,
    h_hbm,
    tiles_hbm,
    q_ref,
    p_ref,
    row_ref,
    keep_ref,
    h_base_ref,
    cot_base_ref,
    tiles_ref,
    types_ref,
    teleport_ref,
    cot_ref,
    h_ref,
    sems,
):
    sources = (types_hbm, teleport_hbm, cot_hbm, h_hbm, tiles_hbm)
    targets = (types_ref, teleport_ref, cot_ref, h_ref, tiles_ref)
    copies = [
        pltpu.make_async_copy(a, b, sems.at[i]) for i, (a, b) in enumerate(zip(sources, targets))
    ]
    for copy in copies:
        copy.start()
    for copy in copies[:4]:
        copy.wait()
    rate = rate_row(types_ref, teleport_ref)
    column = rate_column(rate, h_ref.shape[1])
    row_ref[...] = rate
    keep_ref[...] = 1.0 - column
    q_ref[...] = ((1.0 - rate) * cot_ref[...].T).astype(BF16)
    p_ref[...] = h_ref[...].astype(BF16)
    h_base_ref[...] = column * h_ref[...]
    cot_base_ref[...] = column * cot_ref[...]
    copies[4].wait()


def dense_body(tiles_ref, row_ref, col_ref, count_ref, dense_ref):
    size = tiles_ref.shape[-1]
    me_row = lax.axis_index("rows")
    me_col = lax.axis_index("cols")
    dense_ref[...] = jnp.zeros_like(dense_ref)

    def place(slot, carry):
        row = row_ref[0, 0, slot] ^ me_col
        col = col_ref[0, 0, slot] ^ me_row
        dense_ref[
            pl.ds(pl.multiple_of(row * size, size), size),
            pl.ds(pl.multiple_of(col * size, size), size),
        ] = tiles_ref[0, 0, slot]
        return carry

    lax.fori_loop(0, count_ref[0, 0], place, 0)


def adjoint_body(n_rows, n_cols, dense_ref, *refs):
    blocks, outs = refs[:n_cols], refs[n_cols:]
    keep_far, keep_near, send_far, send_near = outs
    half = n_rows // 2
    near = send_near.shape[0]
    size = blocks[0].shape[1]
    left = jnp.concatenate([b[...] for b in blocks], axis=1)
    for zz in reversed(range(half)):
        part = jnp.dot(
            left, dense_ref[:, 2 * zz * size : (2 * zz + 2) * size], preferred_element_type=F32
        )
        keep, send, at = (
            (keep_near, send_near, zz) if zz < near else (keep_far, send_far, zz - near)
        )
        keep[at] = part[:, :size]
        send[at] = part[:, size:].astype(send.dtype)


def add_body(keep_ref, got_ref, *outs):
    for at, out in enumerate(outs):
        out[...] = (keep_ref[at] + got_ref[at].astype(F32)).astype(out.dtype)


def pack_body(*refs):
    *parts, out_ref = refs
    for at, part in enumerate(parts):
        out_ref[at] = part[...]


def forward_body(half, n_cols, dense_ref, *refs):
    panels, outs = refs[:half], refs[half:]
    size = panels[0].shape[-1]
    total = None
    for zz in range(half):
        panel = jnp.concatenate([panels[zz][0], panels[zz][1]], axis=0)
        part = jnp.dot(
            dense_ref[:, 2 * zz * size : (2 * zz + 2) * size], panel, preferred_element_type=F32
        )
        total = part if total is None else total + part
    for j in range(n_cols):
        outs[j][...] = total[j * size : (j + 1) * size].astype(outs[j].dtype)


def sum_refs(refs):
    terms = [ref[...].astype(F32) for ref in refs]
    while len(terms) > 1:
        terms = [sum(terms[i : i + 2][1:], terms[i]) for i in range(0, len(terms), 2)]
    return terms[0]


def forward_end_body(base_ref, keep_ref, *refs):
    *parts, out_ref = refs
    out_ref[...] = (keep_ref[...] * sum_refs(parts) + base_ref[...]).astype(out_ref.dtype)


def adjoint_middle_body(rate_ref, *refs):
    *parts, d_ref, q_ref = refs
    total = sum_refs(parts)
    d_ref[...] = total
    q_ref[...] = ((1.0 - rate_ref[...]) * total).astype(BF16)


def adjoint_end_body(base_ref, d_ref, rate_ref, *refs):
    *parts, out_ref, token_ref = refs
    out_ref[...] = base_ref[...] + (rate_ref[...] * d_ref[...] + sum_refs(parts)).T
    token_ref[...] = jnp.zeros_like(token_ref)


AFTER = {
    "pair_one_late": ("adjoint_one",),
    "forward_two": ("far_two", "near_two"),
    "forward_end": ("adjoint_end",),
    "pair_two_early": ("adjoint_middle",),
    "forward_middle": ("adjoint_middle",),
    "pair_one_early": ("dense",),
    "adjoint_middle": ("forward_one",),
}
COST = {
    "pair_one_late": 1000,
    "adjoint_middle": 1000,
    "near_two": 200,
    "pair_two_early": 200,
    "far_two": 1000,
    "far_one": 500,
    "forward_end": 1000,
    "pair_two_late": 1000,
    "pair_one_early": 3000,
    "forward_middle": 3000,
    "adjoint_end": 3000,
}


def send(value, axis, count, step):
    return lax.ppermute(value, axis, [(i, i ^ step) for i in range(count)])


def shards(h_start, cotangent, node_type, teleport, tile_values, tile_row, tile_col, tile_count):
    n_rows = lax.axis_size("rows")
    n_cols = lax.axis_size("cols")
    half = n_rows // 2
    near = half // 2
    size = tile_values.shape[-1]
    features = h_start.shape[-1]
    types = node_type.reshape(1, size)
    hop_flops = 2 * n_rows * n_cols * size * size * features

    def shape(kind, *lead):
        return jax.ShapeDtypeStruct((*lead, size, features), kind)

    made = {}
    makers = {}

    def get(name):
        if name not in made:
            made[name] = makers[name]()
        return made[name]

    def run(name, body, outs, args, in_specs=None, scratch=(), flops=0):
        return call(
            body,
            outs,
            in_specs or [vmem()] * len(args),
            args,
            COST.get(name, 0) * 1_000_000 or flops,
            name,
            scratch,
            [get(other)[-1] for other in AFTER.get(name, ())],
        )

    def start():
        return run(
            "start",
            start_body,
            [
                shape(BF16),
                shape(BF16),
                jax.ShapeDtypeStruct((1, size), F32),
                shape(F32),
                shape(F32),
                shape(F32),
                jax.ShapeDtypeStruct(tile_values.shape, BF16),
            ],
            in_hbm(types, teleport, cotangent, h_start, tile_values),
            [hbm()] * 5,
            [
                pltpu.VMEM(types.shape, jnp.int32),
                pltpu.SMEM(teleport.shape, F32),
                pltpu.VMEM(cotangent.shape, F32),
                pltpu.VMEM(h_start.shape, F32),
                pltpu.SemaphoreType.DMA((5,)),
            ],
        )

    def dense():
        return run(
            "dense",
            dense_body,
            [jax.ShapeDtypeStruct((n_cols * size, n_rows * size), BF16)],
            [get("start")[6], *in_hbm(tile_row, tile_col), tile_count],
            [vmem()] + [smem()] * 3,
        )

    def spread(part, axis, count, step):
        return [part] + [send(part, axis, count, step * s) for s in range(1, count // step)]

    def swap_cols(parts):
        return [parts[0]] + [send(parts[s], "cols", n_cols, s) for s in range(1, n_cols)]

    def adjoint(name, part, kind):
        return run(
            name,
            lambda *refs: adjoint_body(n_rows, n_cols, *refs),
            [shape(F32, half - near), shape(F32, near), shape(kind, half - near), shape(kind, near)],
            [get("dense")[0], *spread(part, "cols", n_cols, 1)],
            flops=hop_flops,
        )

    def pair(name, part, other):
        return run(name, pack_body, [shape(BF16, 2)], [part, other])

    def forward(name, early, late, kind):
        panels = [early] + [
            send(early if s == half - 1 else late, "rows", n_rows, 2 * s) for s in range(1, half)
        ]
        return run(
            name,
            lambda *refs: forward_body(half, n_cols, *refs),
            [shape(kind)] * n_cols,
            [get("dense")[0], *panels],
            flops=hop_flops,
        )

    def sums(name, kept, sent, kinds):
        got = send(sent, "rows", n_rows, 1)
        return run(name, add_body, [shape(kind) for kind in kinds], [kept, got])

    def row_parts(far, close):
        parts = [send(far[s - near], "rows", n_rows, 2 * s) for s in range(near, half)]
        return parts + [close[0]] + [send(close[s], "rows", n_rows, 2 * s) for s in range(1, near)]

    far_kinds = lambda kind: [kind] * (half - near)
    near_kinds = lambda kind: [F32] + [kind] * (near - 1)
    makers.update(
        start=start,
        dense=dense,
        adjoint_one=lambda: adjoint("adjoint_one", get("start")[0], F32),
        other_one=lambda: send(get("start")[1], "rows", n_rows, 1),
        other_two=lambda: send(get("forward_middle")[0], "rows", n_rows, 1),
        pair_one_early=lambda: pair("pair_one_early", get("start")[1], get("other_one")),
        pair_one_late=lambda: pair("pair_one_late", get("start")[1], get("other_one")),
        far_one=lambda: sums(
            "far_one", get("adjoint_one")[0], get("adjoint_one")[2], far_kinds(F32)
        ),
        near_one=lambda: sums(
            "near_one", get("adjoint_one")[1], get("adjoint_one")[3], near_kinds(F32)
        ),
        forward_one=lambda: forward(
            "forward_one", get("pair_one_early")[0], get("pair_one_late")[0], F32
        ),
        adjoint_middle=lambda: run(
            "adjoint_middle",
            adjoint_middle_body,
            [shape(F32), shape(BF16)],
            [get("start")[2], *row_parts(get("far_one"), get("near_one"))],
        ),
        forward_middle=lambda: run(
            "forward_middle",
            forward_end_body,
            [shape(BF16)],
            [get("start")[4], get("start")[3], *swap_cols(get("forward_one"))],
        ),
        adjoint_two=lambda: adjoint("adjoint_two", get("adjoint_middle")[1], BF16),
        pair_two_early=lambda: pair("pair_two_early", get("forward_middle")[0], get("other_two")),
        pair_two_late=lambda: pair("pair_two_late", get("forward_middle")[0], get("other_two")),
        far_two=lambda: sums(
            "far_two", get("adjoint_two")[0], get("adjoint_two")[2], far_kinds(BF16)
        ),
        near_two=lambda: sums(
            "near_two", get("adjoint_two")[1], get("adjoint_two")[3], near_kinds(BF16)
        ),
        forward_two=lambda: forward(
            "forward_two", get("pair_two_early")[0], get("pair_two_late")[0], BF16
        ),
        forward_end=lambda: run(
            "forward_end",
            forward_end_body,
            [shape(F32)],
            [get("start")[4], get("start")[3], *swap_cols(get("forward_two"))],
        ),
        adjoint_end=lambda: run(
            "adjoint_end",
            adjoint_end_body,
            [shape(F32), jax.ShapeDtypeStruct((8, features), F32)],
            [
                get("start")[5],
                get("adjoint_middle")[0],
                get("start")[2],
                *row_parts(get("far_two"), get("near_two")),
            ],
        ),
    )
    return get("forward_end")[0], get("adjoint_end")[0]


def solution(mesh):
    placed = (
        P(("rows", "cols"), None),
        P(("rows", "cols"), None),
        P(("rows", "cols")),
        P(),
        P("rows", "cols", None, None, None),
        P("rows", "cols", None),
        P("rows", "cols", None),
        P("rows", "cols"),
    )
    return jax.shard_map(
        shards,
        mesh=mesh,
        in_specs=placed,
        out_specs=(P(("rows", "cols"), None), P(("rows", "cols"), None)),
        check_vma=False,
    )
```

```python
import jax
import jax.numpy as jnp
from jax import lax
from jax.experimental import pallas as pl
from jax.experimental.pallas import tpu as pltpu
from jax.sharding import PartitionSpec as P

VMEM_LIMIT = 32 * 1024 * 1024
BF16 = jnp.bfloat16
F32 = jnp.float32


def vmem():
    return pl.BlockSpec(memory_space=pltpu.VMEM)


def smem():
    return pl.BlockSpec(memory_space=pltpu.SMEM)


def hbm():
    return pl.BlockSpec(memory_space=pltpu.HBM)


def in_hbm(*arrays):
    return [pltpu.with_memory_space_constraint(a, pltpu.HBM) for a in arrays]


def call(body, outs, in_specs, args, flops, name, scratch=(), after=()):
    nbytes = sum(a.size * a.dtype.itemsize for a in (*args, *outs))
    count = len(args)

    def ordered(*refs):
        body(*refs[:count], *refs[count + len(after) :])

    return pl.pallas_call(
        ordered,
        out_shape=outs,
        in_specs=[*in_specs, *[pl.BlockSpec(memory_space=pl.ANY)] * len(after)],
        out_specs=[vmem()] * len(outs),
        scratch_shapes=list(scratch),
        compiler_params=pltpu.CompilerParams(vmem_limit_bytes=VMEM_LIMIT),
        cost_estimate=pl.CostEstimate(flops=flops, bytes_accessed=nbytes, transcendentals=0),
        name=name,
    )(*args, *after)


def rate_row(types_ref, teleport_ref):
    types = types_ref[...]
    rate = jnp.zeros(types.shape, F32)
    for t in range(teleport_ref.shape[0]):
        rate = jnp.where(types == t, teleport_ref[t], rate)
    return rate


def rate_column(row, width):
    size = row.shape[1]
    return jnp.broadcast_to(row, (width, size)).T


def start_body(
    types_hbm,
    teleport_hbm,
    cot_hbm,
    h_hbm,
    tiles_hbm,
    q_ref,
    p_ref,
    row_ref,
    keep_ref,
    h_base_ref,
    cot_base_ref,
    tiles_ref,
    types_ref,
    teleport_ref,
    cot_ref,
    h_ref,
    sems,
):
    sources = (types_hbm, teleport_hbm, cot_hbm, h_hbm, tiles_hbm)
    targets = (types_ref, teleport_ref, cot_ref, h_ref, tiles_ref)
    copies = [
        pltpu.make_async_copy(a, b, sems.at[i]) for i, (a, b) in enumerate(zip(sources, targets))
    ]
    for copy in copies:
        copy.start()
    for copy in copies[:4]:
        copy.wait()
    rate = rate_row(types_ref, teleport_ref)
    column = rate_column(rate, h_ref.shape[1])
    row_ref[...] = rate
    keep_ref[...] = 1.0 - column
    q_ref[...] = ((1.0 - rate) * cot_ref[...].T).astype(BF16)
    p_ref[...] = h_ref[...].astype(BF16)
    h_base_ref[...] = column * h_ref[...]
    cot_base_ref[...] = column * cot_ref[...]
    copies[4].wait()


def dense_body(tiles_ref, row_ref, col_ref, count_ref, dense_ref):
    size = tiles_ref.shape[-1]
    me_row = lax.axis_index("rows")
    me_col = lax.axis_index("cols")
    dense_ref[...] = jnp.zeros_like(dense_ref)

    def place(slot, carry):
        row = row_ref[0, 0, slot] ^ me_col
        col = col_ref[0, 0, slot] ^ me_row
        dense_ref[
            pl.ds(pl.multiple_of(row * size, size), size),
            pl.ds(pl.multiple_of(col * size, size), size),
        ] = tiles_ref[0, 0, slot]
        return carry

    lax.fori_loop(0, count_ref[0, 0], place, 0)


def adjoint_body(n_rows, n_cols, dense_ref, *refs):
    blocks, outs = refs[:n_cols], refs[n_cols:]
    keep_far, keep_near, send_far, send_near = outs
    half = n_rows // 2
    near = send_near.shape[0]
    size = blocks[0].shape[1]
    left = jnp.concatenate([b[...] for b in blocks], axis=1)
    for zz in reversed(range(half)):
        part = jnp.dot(
            left, dense_ref[:, 2 * zz * size : (2 * zz + 2) * size], preferred_element_type=F32
        )
        keep, send, at = (
            (keep_near, send_near, zz) if zz < near else (keep_far, send_far, zz - near)
        )
        keep[at] = part[:, :size]
        send[at] = part[:, size:].astype(send.dtype)


def add_body(keep_ref, got_ref, *outs):
    for at, out in enumerate(outs):
        out[...] = (keep_ref[at] + got_ref[at].astype(F32)).astype(out.dtype)


def pack_body(*refs):
    *parts, out_ref = refs
    for at, part in enumerate(parts):
        out_ref[at] = part[...]


def forward_body(half, n_cols, dense_ref, *refs):
    panels, outs = refs[:half], refs[half:]
    size = panels[0].shape[-1]
    total = None
    for zz in range(half):
        panel = jnp.concatenate([panels[zz][0], panels[zz][1]], axis=0)
        part = jnp.dot(
            dense_ref[:, 2 * zz * size : (2 * zz + 2) * size], panel, preferred_element_type=F32
        )
        total = part if total is None else total + part
    for j in range(n_cols):
        outs[j][...] = total[j * size : (j + 1) * size].astype(outs[j].dtype)


def sum_refs(refs):
    terms = [ref[...].astype(F32) for ref in refs]
    while len(terms) > 1:
        terms = [sum(terms[i : i + 2][1:], terms[i]) for i in range(0, len(terms), 2)]
    return terms[0]


def forward_end_body(base_ref, keep_ref, *refs):
    *parts, out_ref = refs
    out_ref[...] = (keep_ref[...] * sum_refs(parts) + base_ref[...]).astype(out_ref.dtype)


def adjoint_middle_body(rate_ref, *refs):
    *parts, d_ref, q_ref = refs
    total = sum_refs(parts)
    d_ref[...] = total
    q_ref[...] = ((1.0 - rate_ref[...]) * total).astype(BF16)


def adjoint_end_body(base_ref, d_ref, rate_ref, *refs):
    *parts, out_ref, token_ref = refs
    out_ref[...] = base_ref[...] + (rate_ref[...] * d_ref[...] + sum_refs(parts)).T
    token_ref[...] = jnp.zeros_like(token_ref)


AFTER = {
    "pair_one_late": ("adjoint_one",),
    "forward_two": ("far_two", "near_two"),
    "forward_end": ("adjoint_end",),
    "pair_two_early": ("adjoint_middle", "adjoint_two"),
    "pair_one_early": ("dense",),
    "adjoint_middle": ("forward_one",),
}
COST = {
    "pair_one_late": 1000,
    "adjoint_middle": 1000,
    "near_two": 200,
    "pair_two_early": 200,
    "far_two": 1000,
    "far_one": 500,
    "forward_end": 1000,
    "pair_two_late": 1000,
    "pair_one_early": 3000,
    "forward_middle": 3000,
    "adjoint_end": 3000,
}


def send(value, axis, count, step):
    return lax.ppermute(value, axis, [(i, i ^ step) for i in range(count)])


def shards(h_start, cotangent, node_type, teleport, tile_values, tile_row, tile_col, tile_count):
    n_rows = lax.axis_size("rows")
    n_cols = lax.axis_size("cols")
    half = n_rows // 2
    near = half // 2
    size = tile_values.shape[-1]
    features = h_start.shape[-1]
    types = node_type.reshape(1, size)
    hop_flops = 2 * n_rows * n_cols * size * size * features

    def shape(kind, *lead):
        return jax.ShapeDtypeStruct((*lead, size, features), kind)

    made = {}
    makers = {}

    def get(name):
        if name not in made:
            made[name] = makers[name]()
        return made[name]

    def run(name, body, outs, args, in_specs=None, scratch=(), flops=0):
        return call(
            body,
            outs,
            in_specs or [vmem()] * len(args),
            args,
            COST.get(name, 0) * 1_000_000 or flops,
            name,
            scratch,
            [get(other)[-1] for other in AFTER.get(name, ())],
        )

    def start():
        return run(
            "start",
            start_body,
            [
                shape(BF16),
                shape(BF16),
                jax.ShapeDtypeStruct((1, size), F32),
                shape(F32),
                shape(F32),
                shape(F32),
                jax.ShapeDtypeStruct(tile_values.shape, BF16),
            ],
            in_hbm(types, teleport, cotangent, h_start, tile_values),
            [hbm()] * 5,
            [
                pltpu.VMEM(types.shape, jnp.int32),
                pltpu.SMEM(teleport.shape, F32),
                pltpu.VMEM(cotangent.shape, F32),
                pltpu.VMEM(h_start.shape, F32),
                pltpu.SemaphoreType.DMA((5,)),
            ],
        )

    def dense():
        return run(
            "dense",
            dense_body,
            [jax.ShapeDtypeStruct((n_cols * size, n_rows * size), BF16)],
            [get("start")[6], *in_hbm(tile_row, tile_col), tile_count],
            [vmem()] + [smem()] * 3,
        )

    def spread(part, axis, count, step):
        return [part] + [send(part, axis, count, step * s) for s in range(1, count // step)]

    def swap_cols(parts):
        return [parts[0]] + [send(parts[s], "cols", n_cols, s) for s in range(1, n_cols)]

    def adjoint(name, part, kind):
        return run(
            name,
            lambda *refs: adjoint_body(n_rows, n_cols, *refs),
            [shape(F32, half - near), shape(F32, near), shape(kind, half - near), shape(kind, near)],
            [get("dense")[0], *spread(part, "cols", n_cols, 1)],
            flops=hop_flops,
        )

    def pair(name, part, other):
        return run(name, pack_body, [shape(BF16, 2)], [part, other])

    def forward(name, early, late, kind):
        panels = [early] + [
            send(early if s == half - 1 else late, "rows", n_rows, 2 * s) for s in range(1, half)
        ]
        return run(
            name,
            lambda *refs: forward_body(half, n_cols, *refs),
            [shape(kind)] * n_cols,
            [get("dense")[0], *panels],
            flops=hop_flops,
        )

    def sums(name, kept, sent, kinds):
        got = send(sent, "rows", n_rows, 1)
        return run(name, add_body, [shape(kind) for kind in kinds], [kept, got])

    def row_parts(far, close):
        parts = [send(far[s - near], "rows", n_rows, 2 * s) for s in range(near, half)]
        return parts + [close[0]] + [send(close[s], "rows", n_rows, 2 * s) for s in range(1, near)]

    far_kinds = lambda kind: [kind] * (half - near)
    near_kinds = lambda kind: [F32] + [kind] * (near - 1)
    makers.update(
        start=start,
        dense=dense,
        adjoint_one=lambda: adjoint("adjoint_one", get("start")[0], F32),
        other_one=lambda: send(get("start")[1], "rows", n_rows, 1),
        other_two=lambda: send(get("forward_middle")[0], "rows", n_rows, 1),
        pair_one_early=lambda: pair("pair_one_early", get("start")[1], get("other_one")),
        pair_one_late=lambda: pair("pair_one_late", get("start")[1], get("other_one")),
        far_one=lambda: sums(
            "far_one", get("adjoint_one")[0], get("adjoint_one")[2], far_kinds(F32)
        ),
        near_one=lambda: sums(
            "near_one", get("adjoint_one")[1], get("adjoint_one")[3], near_kinds(F32)
        ),
        forward_one=lambda: forward(
            "forward_one", get("pair_one_early")[0], get("pair_one_late")[0], F32
        ),
        adjoint_middle=lambda: run(
            "adjoint_middle",
            adjoint_middle_body,
            [shape(F32), shape(BF16)],
            [get("start")[2], *row_parts(get("far_one"), get("near_one"))],
        ),
        forward_middle=lambda: run(
            "forward_middle",
            forward_end_body,
            [shape(BF16)],
            [get("start")[4], get("start")[3], *swap_cols(get("forward_one"))],
        ),
        adjoint_two=lambda: adjoint("adjoint_two", get("adjoint_middle")[1], BF16),
        pair_two_early=lambda: pair("pair_two_early", get("forward_middle")[0], get("other_two")),
        pair_two_late=lambda: pair("pair_two_late", get("forward_middle")[0], get("other_two")),
        far_two=lambda: sums(
            "far_two", get("adjoint_two")[0], get("adjoint_two")[2], far_kinds(BF16)
        ),
        near_two=lambda: sums(
            "near_two", get("adjoint_two")[1], get("adjoint_two")[3], near_kinds(BF16)
        ),
        forward_two=lambda: forward(
            "forward_two", get("pair_two_early")[0], get("pair_two_late")[0], BF16
        ),
        forward_end=lambda: run(
            "forward_end",
            forward_end_body,
            [shape(F32)],
            [get("start")[4], get("start")[3], *swap_cols(get("forward_two"))],
        ),
        adjoint_end=lambda: run(
            "adjoint_end",
            adjoint_end_body,
            [shape(F32), jax.ShapeDtypeStruct((8, features), F32)],
            [
                get("start")[5],
                get("adjoint_middle")[0],
                get("start")[2],
                *row_parts(get("far_two"), get("near_two")),
            ],
        ),
    )
    return get("forward_end")[0], get("adjoint_end")[0]


def solution(mesh):
    placed = (
        P(("rows", "cols"), None),
        P(("rows", "cols"), None),
        P(("rows", "cols")),
        P(),
        P("rows", "cols", None, None, None),
        P("rows", "cols", None),
        P("rows", "cols", None),
        P("rows", "cols"),
    )
    return jax.shard_map(
        shards,
        mesh=mesh,
        in_specs=placed,
        out_specs=(P(("rows", "cols"), None), P(("rows", "cols"), None)),
        check_vma=False,
    )
```

```python
import jax
import jax.numpy as jnp
from jax import lax
from jax.experimental import pallas as pl
from jax.experimental.pallas import tpu as pltpu
from jax.sharding import PartitionSpec as P

VMEM_LIMIT = 32 * 1024 * 1024
BF16 = jnp.bfloat16
F32 = jnp.float32


def vmem():
    return pl.BlockSpec(memory_space=pltpu.VMEM)


def smem():
    return pl.BlockSpec(memory_space=pltpu.SMEM)


def hbm():
    return pl.BlockSpec(memory_space=pltpu.HBM)


def in_hbm(*arrays):
    return [pltpu.with_memory_space_constraint(a, pltpu.HBM) for a in arrays]


def call(body, outs, in_specs, args, flops, name, scratch=(), after=()):
    nbytes = sum(a.size * a.dtype.itemsize for a in (*args, *outs))
    count = len(args)

    def ordered(*refs):
        body(*refs[:count], *refs[count + len(after) :])

    return pl.pallas_call(
        ordered,
        out_shape=outs,
        in_specs=[*in_specs, *[pl.BlockSpec(memory_space=pl.ANY)] * len(after)],
        out_specs=[vmem()] * len(outs),
        scratch_shapes=list(scratch),
        compiler_params=pltpu.CompilerParams(vmem_limit_bytes=VMEM_LIMIT),
        cost_estimate=pl.CostEstimate(flops=flops, bytes_accessed=nbytes, transcendentals=0),
        name=name,
    )(*args, *after)


def rate_row(types_ref, teleport_ref):
    types = types_ref[...]
    rate = jnp.zeros(types.shape, F32)
    for t in range(teleport_ref.shape[0]):
        rate = jnp.where(types == t, teleport_ref[t], rate)
    return rate


def rate_column(row, width):
    size = row.shape[1]
    return jnp.broadcast_to(row, (width, size)).T


def start_body(
    types_hbm,
    teleport_hbm,
    cot_hbm,
    h_hbm,
    tiles_hbm,
    q_ref,
    p_ref,
    row_ref,
    keep_ref,
    h_base_ref,
    cot_base_ref,
    tiles_ref,
    types_ref,
    teleport_ref,
    cot_ref,
    h_ref,
    sems,
):
    sources = (types_hbm, teleport_hbm, cot_hbm, h_hbm, tiles_hbm)
    targets = (types_ref, teleport_ref, cot_ref, h_ref, tiles_ref)
    copies = [
        pltpu.make_async_copy(a, b, sems.at[i]) for i, (a, b) in enumerate(zip(sources, targets))
    ]
    for copy in copies:
        copy.start()
    for copy in copies[:4]:
        copy.wait()
    rate = rate_row(types_ref, teleport_ref)
    column = rate_column(rate, h_ref.shape[1])
    row_ref[...] = rate
    keep_ref[...] = 1.0 - column
    q_ref[...] = ((1.0 - rate) * cot_ref[...].T).astype(BF16)
    p_ref[...] = h_ref[...].astype(BF16)
    h_base_ref[...] = column * h_ref[...]
    cot_base_ref[...] = column * cot_ref[...]
    copies[4].wait()


def dense_body(tiles_ref, row_ref, col_ref, count_ref, dense_ref):
    size = tiles_ref.shape[-1]
    me_row = lax.axis_index("rows")
    me_col = lax.axis_index("cols")
    dense_ref[...] = jnp.zeros_like(dense_ref)

    def place(slot, carry):
        row = row_ref[0, 0, slot] ^ me_col
        col = col_ref[0, 0, slot] ^ me_row
        dense_ref[
            pl.ds(pl.multiple_of(row * size, size), size),
            pl.ds(pl.multiple_of(col * size, size), size),
        ] = tiles_ref[0, 0, slot]
        return carry

    lax.fori_loop(0, count_ref[0, 0], place, 0)


def adjoint_body(n_rows, n_cols, dense_ref, *refs):
    blocks, outs = refs[:n_cols], refs[n_cols:]
    chunks = list(zip(outs[: len(outs) // 2], outs[len(outs) // 2 :]))
    places = [(keep, send, at) for keep, send in reversed(chunks) for at in range(keep.shape[0])]
    half = n_rows // 2
    size = blocks[0].shape[1]
    left = jnp.concatenate([b[...] for b in blocks], axis=1)
    for zz in reversed(range(half)):
        part = jnp.dot(
            left, dense_ref[:, 2 * zz * size : (2 * zz + 2) * size], preferred_element_type=F32
        )
        keep, send, at = places[zz]
        keep[at] = part[:, :size]
        send[at] = part[:, size:].astype(send.dtype)


def add_body(keep_ref, got_ref, *outs):
    for at, out in enumerate(outs):
        out[...] = (keep_ref[at] + got_ref[at].astype(F32)).astype(out.dtype)


def pack_body(*refs):
    *parts, out_ref = refs
    for at, part in enumerate(parts):
        out_ref[at] = part[...]


def forward_body(half, n_cols, dense_ref, *refs):
    panels, outs = refs[:half], refs[half:]
    size = panels[0].shape[-1]
    total = None
    for zz in range(half):
        panel = jnp.concatenate([panels[zz][0], panels[zz][1]], axis=0)
        part = jnp.dot(
            dense_ref[:, 2 * zz * size : (2 * zz + 2) * size], panel, preferred_element_type=F32
        )
        total = part if total is None else total + part
    for j in range(n_cols):
        outs[j][...] = total[j * size : (j + 1) * size].astype(outs[j].dtype)


def sum_refs(refs):
    terms = [ref[...].astype(F32) for ref in refs]
    while len(terms) > 1:
        terms = [sum(terms[i : i + 2][1:], terms[i]) for i in range(0, len(terms), 2)]
    return terms[0]


def forward_end_body(base_ref, keep_ref, *refs):
    *parts, out_ref = refs
    out_ref[...] = (keep_ref[...] * sum_refs(parts) + base_ref[...]).astype(out_ref.dtype)


def adjoint_middle_body(rate_ref, *refs):
    *parts, d_ref, q_ref = refs
    total = sum_refs(parts)
    d_ref[...] = total
    q_ref[...] = ((1.0 - rate_ref[...]) * total).astype(BF16)


def adjoint_end_body(base_ref, d_ref, rate_ref, *refs):
    *parts, out_ref, token_ref = refs
    out_ref[...] = base_ref[...] + (rate_ref[...] * d_ref[...] + sum_refs(parts)).T
    token_ref[...] = jnp.zeros_like(token_ref)


AFTER = {
    "pair_one_late": ("adjoint_one",),
    "forward_two": ("sums_two",),
    "forward_end": ("adjoint_end",),
    "pair_two_early": ("adjoint_middle", "adjoint_two"),
    "pair_one_early": ("dense",),
    "adjoint_middle": ("forward_one",),
}
COST = {
    "pair_one_late": 1000,
    "adjoint_middle": 1000,
    "pair_two_early": 200,
    "sums_two": 1000,
    "far_one": 500,
    "forward_end": 1000,
    "pair_two_late": 1000,
    "pair_one_early": 3000,
    "forward_middle": 3000,
    "adjoint_end": 3000,
}


def send(value, axis, count, step):
    return lax.ppermute(value, axis, [(i, i ^ step) for i in range(count)])


def shards(h_start, cotangent, node_type, teleport, tile_values, tile_row, tile_col, tile_count):
    n_rows = lax.axis_size("rows")
    n_cols = lax.axis_size("cols")
    half = n_rows // 2
    near = half // 2
    size = tile_values.shape[-1]
    features = h_start.shape[-1]
    types = node_type.reshape(1, size)
    hop_flops = 2 * n_rows * n_cols * size * size * features

    def shape(kind, *lead):
        return jax.ShapeDtypeStruct((*lead, size, features), kind)

    made = {}
    makers = {}

    def get(name):
        if name not in made:
            made[name] = makers[name]()
        return made[name]

    def run(name, body, outs, args, in_specs=None, scratch=(), flops=0):
        return call(
            body,
            outs,
            in_specs or [vmem()] * len(args),
            args,
            COST.get(name, 0) * 1_000_000 or flops,
            name,
            scratch,
            [get(other)[-1] for other in AFTER.get(name, ())],
        )

    def start():
        return run(
            "start",
            start_body,
            [
                shape(BF16),
                shape(BF16),
                jax.ShapeDtypeStruct((1, size), F32),
                shape(F32),
                shape(F32),
                shape(F32),
                jax.ShapeDtypeStruct(tile_values.shape, BF16),
            ],
            in_hbm(types, teleport, cotangent, h_start, tile_values),
            [hbm()] * 5,
            [
                pltpu.VMEM(types.shape, jnp.int32),
                pltpu.SMEM(teleport.shape, F32),
                pltpu.VMEM(cotangent.shape, F32),
                pltpu.VMEM(h_start.shape, F32),
                pltpu.SemaphoreType.DMA((5,)),
            ],
        )

    def dense():
        return run(
            "dense",
            dense_body,
            [jax.ShapeDtypeStruct((n_cols * size, n_rows * size), BF16)],
            [get("start")[6], *in_hbm(tile_row, tile_col), tile_count],
            [vmem()] + [smem()] * 3,
        )

    def spread(part, axis, count, step):
        return [part] + [send(part, axis, count, step * s) for s in range(1, count // step)]

    def swap_cols(parts):
        return [parts[0]] + [send(parts[s], "cols", n_cols, s) for s in range(1, n_cols)]

    def adjoint(name, part, kind, counts):
        return run(
            name,
            lambda *refs: adjoint_body(n_rows, n_cols, *refs),
            [shape(F32, count) for count in counts] + [shape(kind, count) for count in counts],
            [get("dense")[0], *spread(part, "cols", n_cols, 1)],
            flops=hop_flops,
        )

    def pair(name, part, other):
        return run(name, pack_body, [shape(BF16, 2)], [part, other])

    def forward(name, early, late, kind):
        panels = [early] + [
            send(early if s == half - 1 else late, "rows", n_rows, 2 * s) for s in range(1, half)
        ]
        return run(
            name,
            lambda *refs: forward_body(half, n_cols, *refs),
            [shape(kind)] * n_cols,
            [get("dense")[0], *panels],
            flops=hop_flops,
        )

    def sums(name, kept, sent, kinds):
        got = send(sent, "rows", n_rows, 1)
        return run(name, add_body, [shape(kind) for kind in kinds], [kept, got])

    def row_parts(parts):
        order = [*range(near, half), *range(1, near)]
        return [send(parts[s], "rows", n_rows, 2 * s) for s in order] + [parts[0]]

    makers.update(
        start=start,
        dense=dense,
        adjoint_one=lambda: adjoint(
            "adjoint_one", get("start")[0], F32, [half - near, near]
        ),
        other_one=lambda: send(get("start")[1], "rows", n_rows, 1),
        other_two=lambda: send(get("forward_middle")[0], "rows", n_rows, 1),
        pair_one_early=lambda: pair("pair_one_early", get("start")[1], get("other_one")),
        pair_one_late=lambda: pair("pair_one_late", get("start")[1], get("other_one")),
        far_one=lambda: sums(
            "far_one", get("adjoint_one")[0], get("adjoint_one")[2], [F32] * (half - near)
        ),
        near_one=lambda: sums(
            "near_one", get("adjoint_one")[1], get("adjoint_one")[3], [F32] * near
        ),
        forward_one=lambda: forward(
            "forward_one", get("pair_one_early")[0], get("pair_one_late")[0], F32
        ),
        adjoint_middle=lambda: run(
            "adjoint_middle",
            adjoint_middle_body,
            [shape(F32), shape(BF16)],
            [get("start")[2], *row_parts([*get("near_one"), *get("far_one")])],
        ),
        forward_middle=lambda: run(
            "forward_middle",
            forward_end_body,
            [shape(BF16)],
            [get("start")[4], get("start")[3], *swap_cols(get("forward_one"))],
        ),
        adjoint_two=lambda: adjoint(
            "adjoint_two", get("adjoint_middle")[1], BF16, [half]
        ),
        pair_two_early=lambda: pair("pair_two_early", get("forward_middle")[0], get("other_two")),
        pair_two_late=lambda: pair("pair_two_late", get("forward_middle")[0], get("other_two")),
        sums_two=lambda: sums(
            "sums_two", get("adjoint_two")[0], get("adjoint_two")[1], [F32] + [BF16] * (half - 1)
        ),
        forward_two=lambda: forward(
            "forward_two", get("pair_two_early")[0], get("pair_two_late")[0], BF16
        ),
        forward_end=lambda: run(
            "forward_end",
            forward_end_body,
            [shape(F32)],
            [get("start")[4], get("start")[3], *swap_cols(get("forward_two"))],
        ),
        adjoint_end=lambda: run(
            "adjoint_end",
            adjoint_end_body,
            [shape(F32), jax.ShapeDtypeStruct((8, features), F32)],
            [
                get("start")[5],
                get("adjoint_middle")[0],
                get("start")[2],
                *row_parts(get("sums_two")),
            ],
        ),
    )
    return get("forward_end")[0], get("adjoint_end")[0]


def solution(mesh):
    placed = (
        P(("rows", "cols"), None),
        P(("rows", "cols"), None),
        P(("rows", "cols")),
        P(),
        P("rows", "cols", None, None, None),
        P("rows", "cols", None),
        P("rows", "cols", None),
        P("rows", "cols"),
    )
    return jax.shard_map(
        shards,
        mesh=mesh,
        in_specs=placed,
        out_specs=(P(("rows", "cols"), None), P(("rows", "cols"), None)),
        check_vma=False,
    )
```

```python
import jax
import jax.numpy as jnp
from jax import lax
from jax.experimental import pallas as pl
from jax.experimental.pallas import tpu as pltpu
from jax.sharding import PartitionSpec as P

VMEM_LIMIT = 32 * 1024 * 1024
BF16 = jnp.bfloat16
F32 = jnp.float32


def vmem():
    return pl.BlockSpec(memory_space=pltpu.VMEM)


def smem():
    return pl.BlockSpec(memory_space=pltpu.SMEM)


def hbm():
    return pl.BlockSpec(memory_space=pltpu.HBM)


def in_hbm(*arrays):
    return [pltpu.with_memory_space_constraint(a, pltpu.HBM) for a in arrays]


def call(body, outs, in_specs, args, flops, name, scratch=(), after=()):
    nbytes = sum(a.size * a.dtype.itemsize for a in (*args, *outs))
    count = len(args)

    def ordered(*refs):
        body(*refs[:count], *refs[count + len(after) :])

    return pl.pallas_call(
        ordered,
        out_shape=outs,
        in_specs=[*in_specs, *[pl.BlockSpec(memory_space=pl.ANY)] * len(after)],
        out_specs=[vmem()] * len(outs),
        scratch_shapes=list(scratch),
        compiler_params=pltpu.CompilerParams(vmem_limit_bytes=VMEM_LIMIT),
        cost_estimate=pl.CostEstimate(flops=flops, bytes_accessed=nbytes, transcendentals=0),
        name=name,
    )(*args, *after)


def rate_row(types_ref, teleport_ref):
    types = types_ref[...]
    rate = jnp.zeros(types.shape, F32)
    for t in range(teleport_ref.shape[0]):
        rate = jnp.where(types == t, teleport_ref[t], rate)
    return rate


def rate_column(row, width):
    size = row.shape[1]
    return jnp.broadcast_to(row, (width, size)).T


def start_body(
    types_hbm,
    teleport_hbm,
    cot_hbm,
    h_hbm,
    tiles_hbm,
    q_ref,
    p_ref,
    row_ref,
    keep_ref,
    h_base_ref,
    cot_base_ref,
    tiles_ref,
    types_ref,
    teleport_ref,
    cot_ref,
    h_ref,
    sems,
):
    sources = (types_hbm, teleport_hbm, cot_hbm, h_hbm, tiles_hbm)
    targets = (types_ref, teleport_ref, cot_ref, h_ref, tiles_ref)
    copies = [
        pltpu.make_async_copy(a, b, sems.at[i]) for i, (a, b) in enumerate(zip(sources, targets))
    ]
    for copy in copies:
        copy.start()
    for copy in copies[:4]:
        copy.wait()
    rate = rate_row(types_ref, teleport_ref)
    column = rate_column(rate, h_ref.shape[1])
    row_ref[...] = rate
    keep_ref[...] = 1.0 - column
    q_ref[...] = ((1.0 - rate) * cot_ref[...].T).astype(BF16)
    p_ref[...] = h_ref[...].astype(BF16)
    h_base_ref[...] = column * h_ref[...]
    cot_base_ref[...] = column * cot_ref[...]
    copies[4].wait()


def dense_body(tiles_ref, row_ref, col_ref, count_ref, dense_ref):
    size = tiles_ref.shape[-1]
    me_row = lax.axis_index("rows")
    me_col = lax.axis_index("cols")
    dense_ref[...] = jnp.zeros_like(dense_ref)

    def place(slot, carry):
        row = row_ref[0, 0, slot] ^ me_col
        col = col_ref[0, 0, slot] ^ me_row
        dense_ref[
            pl.ds(pl.multiple_of(row * size, size), size),
            pl.ds(pl.multiple_of(col * size, size), size),
        ] = tiles_ref[0, 0, slot]
        return carry

    lax.fori_loop(0, count_ref[0, 0], place, 0)


def adjoint_body(n_rows, n_cols, dense_ref, *refs):
    blocks, outs = refs[:n_cols], refs[n_cols:]
    keep_far, keep_near, send_far, send_near = outs
    half = n_rows // 2
    near = send_near.shape[0]
    size = blocks[0].shape[1]
    left = jnp.concatenate([b[...] for b in blocks], axis=1)
    for zz in reversed(range(half)):
        part = jnp.dot(
            left, dense_ref[:, 2 * zz * size : (2 * zz + 2) * size], preferred_element_type=F32
        )
        keep, send, at = (
            (keep_near, send_near, zz) if zz < near else (keep_far, send_far, zz - near)
        )
        keep[at] = part[:, :size]
        send[at] = part[:, size:].astype(send.dtype)


def add_body(keep_ref, got_ref, *outs):
    for at, out in enumerate(outs):
        out[...] = (keep_ref[at] + got_ref[at].astype(F32)).astype(out.dtype)


def pack_body(*refs):
    *parts, out_ref = refs
    for at, part in enumerate(parts):
        out_ref[at] = part[...]


def forward_body(half, n_cols, dense_ref, *refs):
    panels, outs = refs[:half], refs[half:]
    size = panels[0].shape[-1]
    panel = jnp.concatenate([ref[at] for ref in panels for at in range(2)], axis=0)
    total = jnp.dot(dense_ref[...], panel, preferred_element_type=F32)
    for j in range(n_cols):
        outs[j][...] = total[j * size : (j + 1) * size].astype(outs[j].dtype)


def sum_refs(refs):
    terms = [ref[...].astype(F32) for ref in refs]
    while len(terms) > 1:
        terms = [sum(terms[i : i + 2][1:], terms[i]) for i in range(0, len(terms), 2)]
    return terms[0]


def forward_end_body(base_ref, keep_ref, *refs):
    *parts, out_ref = refs
    out_ref[...] = (keep_ref[...] * sum_refs(parts) + base_ref[...]).astype(out_ref.dtype)


def adjoint_middle_body(rate_ref, *refs):
    *parts, d_ref, q_ref = refs
    total = sum_refs(parts)
    d_ref[...] = total
    q_ref[...] = ((1.0 - rate_ref[...]) * total).astype(BF16)


def adjoint_end_body(base_ref, d_ref, rate_ref, *refs):
    *parts, out_ref, token_ref = refs
    out_ref[...] = base_ref[...] + (rate_ref[...] * d_ref[...] + sum_refs(parts)).T
    token_ref[...] = jnp.zeros_like(token_ref)


AFTER = {
    "pair_one_late": ("adjoint_one",),
    "forward_two": ("far_two", "near_two"),
    "forward_end": ("adjoint_end",),
    "pair_two_early": ("adjoint_middle", "adjoint_two"),
    "pair_one_early": ("dense",),
    "adjoint_middle": ("forward_one",),
}
COST = {
    "pair_one_late": 1000,
    "adjoint_middle": 1000,
    "near_two": 200,
    "pair_two_early": 200,
    "far_two": 1000,
    "far_one": 500,
    "forward_end": 1000,
    "pair_two_late": 1000,
    "pair_one_early": 3000,
    "forward_middle": 3000,
    "adjoint_end": 3000,
}


def send(value, axis, count, step):
    return lax.ppermute(value, axis, [(i, i ^ step) for i in range(count)])


def shards(h_start, cotangent, node_type, teleport, tile_values, tile_row, tile_col, tile_count):
    n_rows = lax.axis_size("rows")
    n_cols = lax.axis_size("cols")
    half = n_rows // 2
    near = half // 2
    size = tile_values.shape[-1]
    features = h_start.shape[-1]
    types = node_type.reshape(1, size)
    hop_flops = 2 * n_rows * n_cols * size * size * features

    def shape(kind, *lead):
        return jax.ShapeDtypeStruct((*lead, size, features), kind)

    made = {}
    makers = {}

    def get(name):
        if name not in made:
            made[name] = makers[name]()
        return made[name]

    def run(name, body, outs, args, in_specs=None, scratch=(), flops=0):
        return call(
            body,
            outs,
            in_specs or [vmem()] * len(args),
            args,
            COST.get(name, 0) * 1_000_000 or flops,
            name,
            scratch,
            [get(other)[-1] for other in AFTER.get(name, ())],
        )

    def start():
        return run(
            "start",
            start_body,
            [
                shape(BF16),
                shape(BF16),
                jax.ShapeDtypeStruct((1, size), F32),
                shape(F32),
                shape(F32),
                shape(F32),
                jax.ShapeDtypeStruct(tile_values.shape, BF16),
            ],
            in_hbm(types, teleport, cotangent, h_start, tile_values),
            [hbm()] * 5,
            [
                pltpu.VMEM(types.shape, jnp.int32),
                pltpu.SMEM(teleport.shape, F32),
                pltpu.VMEM(cotangent.shape, F32),
                pltpu.VMEM(h_start.shape, F32),
                pltpu.SemaphoreType.DMA((5,)),
            ],
        )

    def dense():
        return run(
            "dense",
            dense_body,
            [jax.ShapeDtypeStruct((n_cols * size, n_rows * size), BF16)],
            [get("start")[6], *in_hbm(tile_row, tile_col), tile_count],
            [vmem()] + [smem()] * 3,
        )

    def spread(part, axis, count, step):
        return [part] + [send(part, axis, count, step * s) for s in range(1, count // step)]

    def swap_cols(parts):
        return [parts[0]] + [send(parts[s], "cols", n_cols, s) for s in range(1, n_cols)]

    def adjoint(name, part, kind):
        return run(
            name,
            lambda *refs: adjoint_body(n_rows, n_cols, *refs),
            [shape(F32, half - near), shape(F32, near), shape(kind, half - near), shape(kind, near)],
            [get("dense")[0], *spread(part, "cols", n_cols, 1)],
            flops=hop_flops,
        )

    def pair(name, part, other):
        return run(name, pack_body, [shape(BF16, 2)], [part, other])

    def forward(name, early, late, kind):
        panels = [early] + [
            send(early if s == half - 1 else late, "rows", n_rows, 2 * s) for s in range(1, half)
        ]
        return run(
            name,
            lambda *refs: forward_body(half, n_cols, *refs),
            [shape(kind)] * n_cols,
            [get("dense")[0], *panels],
            flops=hop_flops,
        )

    def sums(name, kept, sent, kinds):
        got = send(sent, "rows", n_rows, 1)
        return run(name, add_body, [shape(kind) for kind in kinds], [kept, got])

    def row_parts(far, close):
        parts = [send(far[s - near], "rows", n_rows, 2 * s) for s in range(near, half)]
        return parts + [close[0]] + [send(close[s], "rows", n_rows, 2 * s) for s in range(1, near)]

    far_kinds = lambda kind: [kind] * (half - near)
    near_kinds = lambda kind: [F32] + [kind] * (near - 1)
    makers.update(
        start=start,
        dense=dense,
        adjoint_one=lambda: adjoint("adjoint_one", get("start")[0], F32),
        other_one=lambda: send(get("start")[1], "rows", n_rows, 1),
        other_two=lambda: send(get("forward_middle")[0], "rows", n_rows, 1),
        pair_one_early=lambda: pair("pair_one_early", get("start")[1], get("other_one")),
        pair_one_late=lambda: pair("pair_one_late", get("start")[1], get("other_one")),
        far_one=lambda: sums(
            "far_one", get("adjoint_one")[0], get("adjoint_one")[2], far_kinds(F32)
        ),
        near_one=lambda: sums(
            "near_one", get("adjoint_one")[1], get("adjoint_one")[3], near_kinds(F32)
        ),
        forward_one=lambda: forward(
            "forward_one", get("pair_one_early")[0], get("pair_one_late")[0], F32
        ),
        adjoint_middle=lambda: run(
            "adjoint_middle",
            adjoint_middle_body,
            [shape(F32), shape(BF16)],
            [get("start")[2], *row_parts(get("far_one"), get("near_one"))],
        ),
        forward_middle=lambda: run(
            "forward_middle",
            forward_end_body,
            [shape(BF16)],
            [get("start")[4], get("start")[3], *swap_cols(get("forward_one"))],
        ),
        adjoint_two=lambda: adjoint("adjoint_two", get("adjoint_middle")[1], BF16),
        pair_two_early=lambda: pair("pair_two_early", get("forward_middle")[0], get("other_two")),
        pair_two_late=lambda: pair("pair_two_late", get("forward_middle")[0], get("other_two")),
        far_two=lambda: sums(
            "far_two", get("adjoint_two")[0], get("adjoint_two")[2], far_kinds(BF16)
        ),
        near_two=lambda: sums(
            "near_two", get("adjoint_two")[1], get("adjoint_two")[3], near_kinds(BF16)
        ),
        forward_two=lambda: forward(
            "forward_two", get("pair_two_early")[0], get("pair_two_late")[0], BF16
        ),
        forward_end=lambda: run(
            "forward_end",
            forward_end_body,
            [shape(F32)],
            [get("start")[4], get("start")[3], *swap_cols(get("forward_two"))],
        ),
        adjoint_end=lambda: run(
            "adjoint_end",
            adjoint_end_body,
            [shape(F32), jax.ShapeDtypeStruct((8, features), F32)],
            [
                get("start")[5],
                get("adjoint_middle")[0],
                get("start")[2],
                *row_parts(get("far_two"), get("near_two")),
            ],
        ),
    )
    return get("forward_end")[0], get("adjoint_end")[0]


def solution(mesh):
    placed = (
        P(("rows", "cols"), None),
        P(("rows", "cols"), None),
        P(("rows", "cols")),
        P(),
        P("rows", "cols", None, None, None),
        P("rows", "cols", None),
        P("rows", "cols", None),
        P("rows", "cols"),
    )
    return jax.shard_map(
        shards,
        mesh=mesh,
        in_specs=placed,
        out_specs=(P(("rows", "cols"), None), P(("rows", "cols"), None)),
        check_vma=False,
    )
```

```python
import jax
import jax.numpy as jnp
from jax import lax
from jax.experimental import pallas as pl
from jax.experimental.pallas import tpu as pltpu
from jax.sharding import PartitionSpec as P

VMEM_LIMIT = 32 * 1024 * 1024
BF16 = jnp.bfloat16
F32 = jnp.float32


def vmem():
    return pl.BlockSpec(memory_space=pltpu.VMEM)


def smem():
    return pl.BlockSpec(memory_space=pltpu.SMEM)


def hbm():
    return pl.BlockSpec(memory_space=pltpu.HBM)


def in_hbm(*arrays):
    return [pltpu.with_memory_space_constraint(a, pltpu.HBM) for a in arrays]


def call(body, outs, in_specs, args, flops, name, scratch=(), after=()):
    nbytes = sum(a.size * a.dtype.itemsize for a in (*args, *outs))
    count = len(args)

    def ordered(*refs):
        body(*refs[:count], *refs[count + len(after) :])

    return pl.pallas_call(
        ordered,
        out_shape=outs,
        in_specs=[*in_specs, *[pl.BlockSpec(memory_space=pl.ANY)] * len(after)],
        out_specs=[vmem()] * len(outs),
        scratch_shapes=list(scratch),
        compiler_params=pltpu.CompilerParams(vmem_limit_bytes=VMEM_LIMIT),
        cost_estimate=pl.CostEstimate(flops=flops, bytes_accessed=nbytes, transcendentals=0),
        name=name,
    )(*args, *after)


def rate_row(types_ref, teleport_ref):
    types = types_ref[...]
    rate = jnp.zeros(types.shape, F32)
    for t in range(teleport_ref.shape[0]):
        rate = jnp.where(types == t, teleport_ref[t], rate)
    return rate


def rate_column(row, width):
    size = row.shape[1]
    return jnp.broadcast_to(row, (width, size)).T


def start_body(
    types_hbm,
    teleport_hbm,
    cot_hbm,
    h_hbm,
    tiles_hbm,
    q_ref,
    p_ref,
    row_ref,
    keep_ref,
    h_base_ref,
    cot_base_ref,
    tiles_ref,
    types_ref,
    teleport_ref,
    cot_ref,
    h_ref,
    sems,
):
    sources = (types_hbm, teleport_hbm, cot_hbm, h_hbm, tiles_hbm)
    targets = (types_ref, teleport_ref, cot_ref, h_ref, tiles_ref)
    copies = [
        pltpu.make_async_copy(a, b, sems.at[i]) for i, (a, b) in enumerate(zip(sources, targets))
    ]
    for copy in copies:
        copy.start()
    for copy in copies[:4]:
        copy.wait()
    rate = rate_row(types_ref, teleport_ref)
    column = rate_column(rate, h_ref.shape[1])
    row_ref[...] = rate
    keep_ref[...] = 1.0 - column
    q_ref[...] = ((1.0 - rate) * cot_ref[...].T).astype(BF16)
    p_ref[...] = h_ref[...].astype(BF16)
    h_base_ref[...] = column * h_ref[...]
    cot_base_ref[...] = column * cot_ref[...]
    copies[4].wait()


def dense_body(tiles_ref, row_ref, col_ref, count_ref, dense_ref):
    size = tiles_ref.shape[-1]
    me_row = lax.axis_index("rows")
    me_col = lax.axis_index("cols")
    dense_ref[...] = jnp.zeros_like(dense_ref)

    def place(slot, carry):
        row = row_ref[0, 0, slot] ^ me_col
        col = col_ref[0, 0, slot] ^ me_row
        dense_ref[
            pl.ds(pl.multiple_of(row * size, size), size),
            pl.ds(pl.multiple_of(col * size, size), size),
        ] = tiles_ref[0, 0, slot]
        return carry

    lax.fori_loop(0, count_ref[0, 0], place, 0)


def adjoint_body(n_rows, n_cols, dense_ref, *refs):
    blocks, outs = refs[:n_cols], refs[n_cols:]
    chunks = list(zip(outs[: len(outs) // 2], outs[len(outs) // 2 :]))
    places = [(keep, send, at) for keep, send in reversed(chunks) for at in range(keep.shape[0])]
    half = n_rows // 2
    size = blocks[0].shape[1]
    left = jnp.concatenate([b[...] for b in blocks], axis=1)
    for zz in reversed(range(half)):
        part = jnp.dot(
            left, dense_ref[:, 2 * zz * size : (2 * zz + 2) * size], preferred_element_type=F32
        )
        keep, send, at = places[zz]
        keep[at] = part[:, :size]
        send[at] = part[:, size:].astype(send.dtype)


def add_body(keep_ref, got_ref, *outs):
    for at, out in enumerate(outs):
        out[...] = (keep_ref[at] + got_ref[at].astype(F32)).astype(out.dtype)


def pack_body(*refs):
    *parts, out_ref = refs
    for at, part in enumerate(parts):
        out_ref[at] = part[...]


def forward_body(half, n_cols, dense_ref, *refs):
    panels, outs = refs[:half], refs[half:]
    size = panels[0].shape[-1]
    total = None
    for zz in range(half):
        panel = jnp.concatenate([panels[zz][0], panels[zz][1]], axis=0)
        part = jnp.dot(
            dense_ref[:, 2 * zz * size : (2 * zz + 2) * size], panel, preferred_element_type=F32
        )
        total = part if total is None else total + part
    for j in range(n_cols):
        outs[j][...] = total[j * size : (j + 1) * size].astype(outs[j].dtype)


def sum_refs(refs):
    terms = [ref[...].astype(F32) for ref in refs]
    while len(terms) > 1:
        terms = [sum(terms[i : i + 2][1:], terms[i]) for i in range(0, len(terms), 2)]
    return terms[0]


def forward_end_body(base_ref, keep_ref, *refs):
    *parts, out_ref = refs
    out_ref[...] = (keep_ref[...] * sum_refs(parts) + base_ref[...]).astype(out_ref.dtype)


def adjoint_middle_body(rate_ref, *refs):
    *parts, d_ref, q_ref = refs
    total = sum_refs(parts)
    d_ref[...] = total
    q_ref[...] = ((1.0 - rate_ref[...]) * total).astype(BF16)


def adjoint_end_body(base_ref, d_ref, rate_ref, *refs):
    *parts, out_ref, token_ref = refs
    out_ref[...] = base_ref[...] + (rate_ref[...] * d_ref[...] + sum_refs(parts)).T
    token_ref[...] = jnp.zeros_like(token_ref)


AFTER = {
    "pair_one_late": ("adjoint_one",),
    "forward_two": ("sums_two",),
    "forward_end": ("adjoint_end",),
    "pair_two_early": ("adjoint_middle", "adjoint_two"),
    "pair_one_early": ("dense",),
    "adjoint_middle": ("forward_one",),
}
COST = {
    "pair_one_late": 1000,
    "adjoint_middle": 1000,
    "pair_two_early": 200,
    "sums_two": 1000,
    "far_one": 500,
    "forward_end": 1000,
    "pair_two_late": 1000,
    "pair_one_early": 3000,
    "forward_middle": 3000,
    "adjoint_end": 3000,
}


def send(value, axis, count, step):
    return lax.ppermute(value, axis, [(i, i ^ step) for i in range(count)])


def shards(h_start, cotangent, node_type, teleport, tile_values, tile_row, tile_col, tile_count):
    n_rows = lax.axis_size("rows")
    n_cols = lax.axis_size("cols")
    half = n_rows // 2
    near = half // 2
    size = tile_values.shape[-1]
    features = h_start.shape[-1]
    types = node_type.reshape(1, size)
    hop_flops = 2 * n_rows * n_cols * size * size * features

    def shape(kind, *lead):
        return jax.ShapeDtypeStruct((*lead, size, features), kind)

    made = {}
    makers = {}

    def get(name):
        if name not in made:
            made[name] = makers[name]()
        return made[name]

    def run(name, body, outs, args, in_specs=None, scratch=(), flops=0):
        return call(
            body,
            outs,
            in_specs or [vmem()] * len(args),
            args,
            COST.get(name, 0) * 1_000_000 or flops,
            name,
            scratch,
            [get(other)[-1] for other in AFTER.get(name, ())],
        )

    def start():
        return run(
            "start",
            start_body,
            [
                shape(BF16),
                shape(BF16),
                jax.ShapeDtypeStruct((1, size), F32),
                shape(F32),
                shape(F32),
                shape(F32),
                jax.ShapeDtypeStruct(tile_values.shape, BF16),
            ],
            in_hbm(types, teleport, cotangent, h_start, tile_values),
            [hbm()] * 5,
            [
                pltpu.VMEM(types.shape, jnp.int32),
                pltpu.SMEM(teleport.shape, F32),
                pltpu.VMEM(cotangent.shape, F32),
                pltpu.VMEM(h_start.shape, F32),
                pltpu.SemaphoreType.DMA((5,)),
            ],
        )

    def dense():
        return run(
            "dense",
            dense_body,
            [jax.ShapeDtypeStruct((n_cols * size, n_rows * size), BF16)],
            [get("start")[6], *in_hbm(tile_row, tile_col), tile_count],
            [vmem()] + [smem()] * 3,
        )

    def spread(part, axis, count, step):
        return [part] + [send(part, axis, count, step * s) for s in range(1, count // step)]

    def swap_cols(parts):
        return [parts[0]] + [send(parts[s], "cols", n_cols, s) for s in range(1, n_cols)]

    def adjoint(name, part, kind, counts):
        return run(
            name,
            lambda *refs: adjoint_body(n_rows, n_cols, *refs),
            [shape(F32, count) for count in counts] + [shape(kind, count) for count in counts],
            [get("dense")[0], *spread(part, "cols", n_cols, 1)],
            flops=hop_flops,
        )

    def pair(name, part, other):
        return run(name, pack_body, [shape(BF16, 2)], [part, other])

    def forward(name, early, late, kind):
        panels = [early] + [
            send(early if s == near else late, "rows", n_rows, 2 * s) for s in range(1, half)
        ]
        return run(
            name,
            lambda *refs: forward_body(half, n_cols, *refs),
            [shape(kind)] * n_cols,
            [get("dense")[0], *panels],
            flops=hop_flops,
        )

    def sums(name, kept, sent, kinds):
        got = send(sent, "rows", n_rows, 1)
        return run(name, add_body, [shape(kind) for kind in kinds], [kept, got])

    def row_parts(parts):
        order = [*range(near, half), *range(1, near)]
        return [send(parts[s], "rows", n_rows, 2 * s) for s in order] + [parts[0]]

    makers.update(
        start=start,
        dense=dense,
        adjoint_one=lambda: adjoint(
            "adjoint_one", get("start")[0], F32, [half - near, near]
        ),
        other_one=lambda: send(get("start")[1], "rows", n_rows, 1),
        other_two=lambda: send(get("forward_middle")[0], "rows", n_rows, 1),
        pair_one_early=lambda: pair("pair_one_early", get("start")[1], get("other_one")),
        pair_one_late=lambda: pair("pair_one_late", get("start")[1], get("other_one")),
        far_one=lambda: sums(
            "far_one", get("adjoint_one")[0], get("adjoint_one")[2], [F32] * (half - near)
        ),
        near_one=lambda: sums(
            "near_one", get("adjoint_one")[1], get("adjoint_one")[3], [F32] * near
        ),
        forward_one=lambda: forward(
            "forward_one", get("pair_one_early")[0], get("pair_one_late")[0], F32
        ),
        adjoint_middle=lambda: run(
            "adjoint_middle",
            adjoint_middle_body,
            [shape(F32), shape(BF16)],
            [get("start")[2], *row_parts([*get("near_one"), *get("far_one")])],
        ),
        forward_middle=lambda: run(
            "forward_middle",
            forward_end_body,
            [shape(BF16)],
            [get("start")[4], get("start")[3], *swap_cols(get("forward_one"))],
        ),
        adjoint_two=lambda: adjoint(
            "adjoint_two", get("adjoint_middle")[1], BF16, [half]
        ),
        pair_two_early=lambda: pair("pair_two_early", get("forward_middle")[0], get("other_two")),
        pair_two_late=lambda: pair("pair_two_late", get("forward_middle")[0], get("other_two")),
        sums_two=lambda: sums(
            "sums_two", get("adjoint_two")[0], get("adjoint_two")[1], [F32] + [BF16] * (half - 1)
        ),
        forward_two=lambda: forward(
            "forward_two", get("pair_two_early")[0], get("pair_two_late")[0], BF16
        ),
        forward_end=lambda: run(
            "forward_end",
            forward_end_body,
            [shape(F32)],
            [get("start")[4], get("start")[3], *swap_cols(get("forward_two"))],
        ),
        adjoint_end=lambda: run(
            "adjoint_end",
            adjoint_end_body,
            [shape(F32), jax.ShapeDtypeStruct((8, features), F32)],
            [
                get("start")[5],
                get("adjoint_middle")[0],
                get("start")[2],
                *row_parts(get("sums_two")),
            ],
        ),
    )
    return get("forward_end")[0], get("adjoint_end")[0]


def solution(mesh):
    placed = (
        P(("rows", "cols"), None),
        P(("rows", "cols"), None),
        P(("rows", "cols")),
        P(),
        P("rows", "cols", None, None, None),
        P("rows", "cols", None),
        P("rows", "cols", None),
        P("rows", "cols"),
    )
    return jax.shard_map(
        shards,
        mesh=mesh,
        in_specs=placed,
        out_specs=(P(("rows", "cols"), None), P(("rows", "cols"), None)),
        check_vma=False,
    )
```

```python
import jax
import jax.numpy as jnp
from jax import lax
from jax.experimental import pallas as pl
from jax.experimental.pallas import tpu as pltpu
from jax.sharding import PartitionSpec as P

VMEM_LIMIT = 32 * 1024 * 1024
BF16 = jnp.bfloat16
F32 = jnp.float32


def vmem():
    return pl.BlockSpec(memory_space=pltpu.VMEM)


def smem():
    return pl.BlockSpec(memory_space=pltpu.SMEM)


def hbm():
    return pl.BlockSpec(memory_space=pltpu.HBM)


def in_hbm(*arrays):
    return [pltpu.with_memory_space_constraint(a, pltpu.HBM) for a in arrays]


def call(body, outs, in_specs, args, flops, name, scratch=(), after=()):
    nbytes = sum(a.size * a.dtype.itemsize for a in (*args, *outs))
    count = len(args)

    def ordered(*refs):
        body(*refs[:count], *refs[count + len(after) :])

    return pl.pallas_call(
        ordered,
        out_shape=outs,
        in_specs=[*in_specs, *[pl.BlockSpec(memory_space=pl.ANY)] * len(after)],
        out_specs=[vmem()] * len(outs),
        scratch_shapes=list(scratch),
        compiler_params=pltpu.CompilerParams(vmem_limit_bytes=VMEM_LIMIT),
        cost_estimate=pl.CostEstimate(flops=flops, bytes_accessed=nbytes, transcendentals=0),
        name=name,
    )(*args, *after)


def rate_row(types_ref, teleport_ref):
    types = types_ref[...]
    rate = jnp.zeros(types.shape, F32)
    for t in range(teleport_ref.shape[0]):
        rate = jnp.where(types == t, teleport_ref[t], rate)
    return rate


def rate_column(row, width):
    size = row.shape[1]
    return jnp.broadcast_to(row, (width, size)).T


def start_body(
    types_hbm,
    teleport_hbm,
    cot_hbm,
    h_hbm,
    tiles_hbm,
    q_ref,
    p_ref,
    row_ref,
    keep_ref,
    h_base_ref,
    cot_base_ref,
    tiles_ref,
    types_ref,
    teleport_ref,
    cot_ref,
    h_ref,
    sems,
):
    sources = (types_hbm, teleport_hbm, cot_hbm, h_hbm, tiles_hbm)
    targets = (types_ref, teleport_ref, cot_ref, h_ref, tiles_ref)
    copies = [
        pltpu.make_async_copy(a, b, sems.at[i]) for i, (a, b) in enumerate(zip(sources, targets))
    ]
    for copy in copies:
        copy.start()
    for copy in copies[:4]:
        copy.wait()
    rate = rate_row(types_ref, teleport_ref)
    column = rate_column(rate, h_ref.shape[1])
    row_ref[...] = rate
    keep_ref[...] = 1.0 - column
    q_ref[...] = ((1.0 - rate) * cot_ref[...].T).astype(BF16)
    p_ref[...] = h_ref[...].astype(BF16)
    h_base_ref[...] = column * h_ref[...]
    cot_base_ref[...] = column * cot_ref[...]
    copies[4].wait()


def dense_body(tiles_ref, row_ref, col_ref, count_ref, dense_ref):
    size = tiles_ref.shape[-1]
    me_row = lax.axis_index("rows")
    me_col = lax.axis_index("cols")
    dense_ref[...] = jnp.zeros_like(dense_ref)

    def place(slot, carry):
        row = row_ref[0, 0, slot] ^ me_col
        col = col_ref[0, 0, slot] ^ me_row
        dense_ref[
            pl.ds(pl.multiple_of(row * size, size), size),
            pl.ds(pl.multiple_of(col * size, size), size),
        ] = tiles_ref[0, 0, slot]
        return carry

    lax.fori_loop(0, count_ref[0, 0], place, 0)


def adjoint_body(n_rows, n_cols, dense_ref, *refs):
    blocks, outs = refs[:n_cols], refs[n_cols:]
    chunks = list(zip(outs[: len(outs) // 2], outs[len(outs) // 2 :]))
    places = [(keep, send, at) for keep, send in reversed(chunks) for at in range(keep.shape[0])]
    half = n_rows // 2
    size = blocks[0].shape[1]
    left = jnp.concatenate([b[...] for b in blocks], axis=1)
    for zz in reversed(range(half)):
        part = jnp.dot(
            left, dense_ref[:, 2 * zz * size : (2 * zz + 2) * size], preferred_element_type=F32
        )
        keep, send, at = places[zz]
        keep[at] = part[:, :size]
        send[at] = part[:, size:].astype(send.dtype)


def add_body(keep_ref, got_ref, *outs):
    for at, out in enumerate(outs):
        out[...] = (keep_ref[at] + got_ref[at].astype(F32)).astype(out.dtype)


def pack_body(*refs):
    *parts, out_ref = refs
    for at, part in enumerate(parts):
        out_ref[at] = part[...]


def forward_body(half, n_cols, dense_ref, *refs):
    panels, outs = refs[:half], refs[half:]
    size = panels[0].shape[-1]
    total = None
    for zz in range(half):
        panel = jnp.concatenate([panels[zz][0], panels[zz][1]], axis=0)
        part = jnp.dot(
            dense_ref[:, 2 * zz * size : (2 * zz + 2) * size], panel, preferred_element_type=F32
        )
        total = part if total is None else total + part
    for j in range(n_cols):
        outs[j][...] = total[j * size : (j + 1) * size].astype(outs[j].dtype)


def sum_refs(refs):
    terms = [ref[...].astype(F32) for ref in refs]
    while len(terms) > 1:
        terms = [sum(terms[i : i + 2][1:], terms[i]) for i in range(0, len(terms), 2)]
    return terms[0]


def forward_end_body(base_ref, keep_ref, *refs):
    *parts, out_ref = refs
    out_ref[...] = (keep_ref[...] * sum_refs(parts) + base_ref[...]).astype(out_ref.dtype)


def adjoint_middle_body(rate_ref, *refs):
    *parts, d_ref, q_ref = refs
    total = sum_refs(parts)
    d_ref[...] = total
    q_ref[...] = ((1.0 - rate_ref[...]) * total).astype(BF16)


def adjoint_end_body(base_ref, d_ref, rate_ref, *refs):
    *parts, out_ref, token_ref = refs
    out_ref[...] = base_ref[...] + (rate_ref[...] * d_ref[...] + sum_refs(parts)).T
    token_ref[...] = jnp.zeros_like(token_ref)


AFTER = {
    "pair_one_late": ("adjoint_one",),
    "forward_two": ("sums_two",),
    "forward_end": ("adjoint_end",),
    "pair_two_early": ("adjoint_middle", "adjoint_two"),
    "pair_one_early": ("dense",),
    "adjoint_middle": ("forward_one",),
}
COST = {
    "pair_one_late": 1000,
    "adjoint_middle": 1000,
    "pair_two_early": 200,
    "sums_two": 1000,
    "far_one": 500,
    "forward_end": 1000,
    "pair_two_late": 1000,
    "pair_one_early": 3000,
    "forward_middle": 3000,
    "adjoint_end": 3000,
}


def send(value, axis, count, step):
    return lax.ppermute(value, axis, [(i, i ^ step) for i in range(count)])


def shards(h_start, cotangent, node_type, teleport, tile_values, tile_row, tile_col, tile_count):
    n_rows = lax.axis_size("rows")
    n_cols = lax.axis_size("cols")
    half = n_rows // 2
    near = half // 2
    size = tile_values.shape[-1]
    features = h_start.shape[-1]
    types = node_type.reshape(1, size)
    hop_flops = 2 * n_rows * n_cols * size * size * features

    def shape(kind, *lead):
        return jax.ShapeDtypeStruct((*lead, size, features), kind)

    made = {}
    makers = {}

    def get(name):
        if name not in made:
            made[name] = makers[name]()
        return made[name]

    def run(name, body, outs, args, in_specs=None, scratch=(), flops=0):
        return call(
            body,
            outs,
            in_specs or [vmem()] * len(args),
            args,
            COST.get(name, 0) * 1_000_000 or flops,
            name,
            scratch,
            [get(other)[-1] for other in AFTER.get(name, ())],
        )

    def start():
        return run(
            "start",
            start_body,
            [
                shape(BF16),
                shape(BF16),
                jax.ShapeDtypeStruct((1, size), F32),
                shape(F32),
                shape(F32),
                shape(F32),
                jax.ShapeDtypeStruct(tile_values.shape, BF16),
            ],
            in_hbm(types, teleport, cotangent, h_start, tile_values),
            [hbm()] * 5,
            [
                pltpu.VMEM(types.shape, jnp.int32),
                pltpu.SMEM(teleport.shape, F32),
                pltpu.VMEM(cotangent.shape, F32),
                pltpu.VMEM(h_start.shape, F32),
                pltpu.SemaphoreType.DMA((5,)),
            ],
        )

    def dense():
        return run(
            "dense",
            dense_body,
            [jax.ShapeDtypeStruct((n_cols * size, n_rows * size), BF16)],
            [get("start")[6], *in_hbm(tile_row, tile_col), tile_count],
            [vmem()] + [smem()] * 3,
        )

    def spread(part, axis, count, step):
        return [part] + [send(part, axis, count, step * s) for s in range(1, count // step)]

    def swap_cols(parts):
        return [parts[0]] + [send(parts[s], "cols", n_cols, s) for s in range(1, n_cols)]

    def adjoint(name, part, kind, counts):
        return run(
            name,
            lambda *refs: adjoint_body(n_rows, n_cols, *refs),
            [shape(F32, count) for count in counts] + [shape(kind, count) for count in counts],
            [get("dense")[0], *spread(part, "cols", n_cols, 1)],
            flops=hop_flops,
        )

    def pair(name, part, other):
        return run(name, pack_body, [shape(BF16, 2)], [part, other])

    def forward(name, early, late, kind):
        panels = [early] + [
            send(early if s == 1 else late, "rows", n_rows, 2 * s) for s in range(1, half)
        ]
        return run(
            name,
            lambda *refs: forward_body(half, n_cols, *refs),
            [shape(kind)] * n_cols,
            [get("dense")[0], *panels],
            flops=hop_flops,
        )

    def sums(name, kept, sent, kinds):
        got = send(sent, "rows", n_rows, 1)
        return run(name, add_body, [shape(kind) for kind in kinds], [kept, got])

    def row_parts(parts):
        order = [*range(near, half), *range(1, near)]
        return [send(parts[s], "rows", n_rows, 2 * s) for s in order] + [parts[0]]

    makers.update(
        start=start,
        dense=dense,
        adjoint_one=lambda: adjoint(
            "adjoint_one", get("start")[0], F32, [half - near, near]
        ),
        other_one=lambda: send(get("start")[1], "rows", n_rows, 1),
        other_two=lambda: send(get("forward_middle")[0], "rows", n_rows, 1),
        pair_one_early=lambda: pair("pair_one_early", get("start")[1], get("other_one")),
        pair_one_late=lambda: pair("pair_one_late", get("start")[1], get("other_one")),
        far_one=lambda: sums(
            "far_one", get("adjoint_one")[0], get("adjoint_one")[2], [F32] * (half - near)
        ),
        near_one=lambda: sums(
            "near_one", get("adjoint_one")[1], get("adjoint_one")[3], [F32] * near
        ),
        forward_one=lambda: forward(
            "forward_one", get("pair_one_early")[0], get("pair_one_late")[0], F32
        ),
        adjoint_middle=lambda: run(
            "adjoint_middle",
            adjoint_middle_body,
            [shape(F32), shape(BF16)],
            [get("start")[2], *row_parts([*get("near_one"), *get("far_one")])],
        ),
        forward_middle=lambda: run(
            "forward_middle",
            forward_end_body,
            [shape(BF16)],
            [get("start")[4], get("start")[3], *swap_cols(get("forward_one"))],
        ),
        adjoint_two=lambda: adjoint(
            "adjoint_two", get("adjoint_middle")[1], BF16, [half]
        ),
        pair_two_early=lambda: pair("pair_two_early", get("forward_middle")[0], get("other_two")),
        pair_two_late=lambda: pair("pair_two_late", get("forward_middle")[0], get("other_two")),
        sums_two=lambda: sums(
            "sums_two", get("adjoint_two")[0], get("adjoint_two")[1], [F32] + [BF16] * (half - 1)
        ),
        forward_two=lambda: forward(
            "forward_two", get("pair_two_early")[0], get("pair_two_late")[0], BF16
        ),
        forward_end=lambda: run(
            "forward_end",
            forward_end_body,
            [shape(F32)],
            [get("start")[4], get("start")[3], *swap_cols(get("forward_two"))],
        ),
        adjoint_end=lambda: run(
            "adjoint_end",
            adjoint_end_body,
            [shape(F32), jax.ShapeDtypeStruct((8, features), F32)],
            [
                get("start")[5],
                get("adjoint_middle")[0],
                get("start")[2],
                *row_parts(get("sums_two")),
            ],
        ),
    )
    return get("forward_end")[0], get("adjoint_end")[0]


def solution(mesh):
    placed = (
        P(("rows", "cols"), None),
        P(("rows", "cols"), None),
        P(("rows", "cols")),
        P(),
        P("rows", "cols", None, None, None),
        P("rows", "cols", None),
        P("rows", "cols", None),
        P("rows", "cols"),
    )
    return jax.shard_map(
        shards,
        mesh=mesh,
        in_specs=placed,
        out_specs=(P(("rows", "cols"), None), P(("rows", "cols"), None)),
        check_vma=False,
    )
```
